32 devices in a mesh: shard: 4 (over x, core), replica: 8 (over z, y).
Axes of the slice: x: 2, y: 2, z: 4, core: 2. Of those that a mesh axis runs over, the one named last changes fastest.
Arguments:
- inputs: bfloat16 [8, 1024, 2048], P('replica', 'shard'), may hold values from -6 to 6
- cotangent: bfloat16 [8, 1024, 2048], P('replica', 'shard'), may hold values from -6 to 6
- gain_attn: bfloat16 [2048], P('shard'), may hold values from 0.5 to 1.5
- w_query: bfloat16 [2048, 2048], P('shard'), may hold values from -0.125 to 0.125
- w_key: bfloat16 [2048, 256], P('shard'), may hold values from -0.125 to 0.125
- w_value: bfloat16 [2048, 256], P('shard'), may hold values from -0.125 to 0.125
- w_output: bfloat16 [2048, 2048], P('shard'), may hold values from -0.5 to 0.5
- gain_mlp: bfloat16 [2048], P('shard'), may hold values from 0.5 to 1.5
- w_gate: bfloat16 [2048, 5632], P('shard'), may hold values from -0.125 to 0.125
- w_up: bfloat16 [2048, 5632], P('shard'), may hold values from -0.125 to 0.125
- w_down: bfloat16 [5632, 2048], P('shard'), may hold values from -0.078125 to 0.078125
Outputs:
- output: bfloat16 [8, 1024, 2048], P('replica', 'shard')
- input_grad: bfloat16 [8, 1024, 2048], P('replica', 'shard')
- grad_gain_attn: float32 [2048], P(('shard', 'replica'))
- grad_query: float32 [2048, 2048], P(('shard', 'replica'))
- grad_key: float32 [2048, 256], P(('shard', 'replica'))
- grad_value: float32 [2048, 256], P(('shard', 'replica'))
- grad_output: float32 [2048, 2048], P(('shard', 'replica'))
- grad_gain_mlp: float32 [2048], P(('shard', 'replica'))
- grad_gate: float32 [2048, 5632], P(('shard', 'replica'))
- grad_up: float32 [2048, 5632], P(('shard', 'replica'))
- grad_down: float32 [5632, 2048], P(('shard', 'replica'))
The draws below stay inside these ranges and needn't reach their ends.
All inputs are finite; a program needn't handle non-finite values.
Results may differ from the reference program's by a relative error of at most 0.022.
Values may be sent and summed in bfloat16 or wider, within the bound.
A program may use at most 448 MiB of HBM per device.

```python
import jax
import jax.numpy as jnp
from jax import lax

D = 2048
H = 32
KV = 4
HD = 64
FF = 5632
LENGTH = 1024
SEQS = 8


def shard_levels(key, shape, split, smallest, high):
    level = 1.0
    for dim, shards_of in split:
        heights = jax.random.uniform(jax.random.fold_in(jax.random.fold_in(key, 6), dim), (shards_of,), jnp.float32, smallest / len(split), high / len(split))
        level = level * jnp.repeat(jnp.exp(heights), shape[dim] // shards_of).reshape((-1,) + (1,) * (len(shape) - 1 - dim))
    return level


def normal_values(stream_key, extent, spread, limit, pieces=(), held_as=jnp.bfloat16):
    factor_of = shard_levels(stream_key, extent, pieces, -0.22, 0.18) if pieces else 1.0
    values = jax.random.normal(stream_key, extent, jnp.float32) * spread * factor_of
    return jnp.minimum(jnp.maximum(values, -limit), limit).astype(held_as)


def setup_inputs(seed: int = 0) -> dict:
    streams_of = jax.random.split(jax.random.key(seed), 12)
    inputs = normal_values(streams_of[0], (SEQS, LENGTH, D), 1.0, 6.0, ((0, 8), (1, 4)))
    cotangent = normal_values(streams_of[1], (SEQS, LENGTH, D), 1.0, 6.0, ((0, 8), (1, 4)))
    gain_attn = jnp.clip(1.0 + 0.1 * jax.random.normal(streams_of[2], (D,), jnp.float32), 0.5, 1.5).astype(jnp.bfloat16)
    w_query = normal_values(streams_of[3], (D, H * HD), D ** -0.5, 0.125, ((0, 4),))
    w_key = normal_values(streams_of[4], (D, KV * HD), D ** -0.5, 0.125, ((0, 4),))
    w_value = normal_values(streams_of[5], (D, KV * HD), D ** -0.5, 0.125, ((0, 4),))
    w_output = normal_values(streams_of[6], (H * HD, D), (D // 16) ** -0.5, 0.5, ((0, 4),))
    gain_mlp = jnp.clip(1.0 + 0.1 * jax.random.normal(streams_of[7], (D,), jnp.float32), 0.5, 1.5).astype(jnp.bfloat16)
    w_gate = normal_values(streams_of[8], (D, FF), D ** -0.5, 0.125, ((0, 4),))
    w_up = normal_values(streams_of[9], (D, FF), D ** -0.5, 0.125, ((0, 4),))
    w_down = normal_values(streams_of[10], (FF, D), FF ** -0.5, 0.078125, ((0, 4),))
    return dict(inputs=inputs, cotangent=cotangent, gain_attn=gain_attn, w_query=w_query, w_key=w_key, w_value=w_value, w_output=w_output, gain_mlp=gain_mlp, w_gate=w_gate, w_up=w_up, w_down=w_down)


EPS = 1e-05
THETA = 10000.0
HIGH = lax.Precision.HIGHEST

@jax.custom_vjp
def low(v):
    return lax.optimization_barrier(v.astype(jnp.bfloat16)).astype(jnp.float32)

@jax.custom_vjp
def low_back(v):
    return v

def low_keep(v):
    return (low(v), None)

def low_pass(kept, grad):
    return (grad,)

def back_keep(v):
    return (v, None)

def back_low(kept, grad):
    return (low(grad),)
low.defvjp(low_keep, low_pass)
low_back.defvjp(back_keep, back_low)

def rotation(positions):
    half_width = HD // 2
    freq_table = THETA ** (-2.0 * jnp.arange(half_width, dtype=jnp.float32) / HD)
    angles = positions.astype(jnp.float32)[:, None] * freq_table[None, :]
    return (jnp.cos(angles), jnp.sin(angles))

def rotate(values, cos_table, sin_table):
    half_width = values.shape[-1] // 2
    first_half = values[..., :half_width]
    second_half = values[..., half_width:]
    cos_part = cos_table[:, None, :]
    sin_part = sin_table[:, None, :]
    return jnp.concatenate([first_half * cos_part - second_half * sin_part, second_half * cos_part + first_half * sin_part], axis=-1)

def matmul_high(left, right):
    return jnp.dot(left, right, precision=HIGH)

def rms_scale(values):
    return lax.rsqrt(lax.optimization_barrier(jnp.mean(values * values, axis=-1, keepdims=True)) + EPS)

def forward(resid, gain_attn, w_query, w_key, w_value, w_output, gain_mlp, w_gate, w_up, w_down):
    seq_len = resid.shape[0]
    group_size = H // KV
    cos_table, sin_table = rotation(jnp.arange(seq_len, dtype=jnp.int32))
    norm1 = low(resid * rms_scale(resid) * gain_attn)
    query_pre = low_back(matmul_high(norm1, w_query)).reshape(seq_len, H, HD)
    key_pre = low_back(matmul_high(norm1, w_key)).reshape(seq_len, KV, HD)
    values = low(low_back(matmul_high(norm1, w_value))).reshape(seq_len, KV, HD)
    queries = low(rotate(query_pre, cos_table, sin_table)).reshape(seq_len, KV, group_size, HD)
    keys = low(rotate(key_pre, cos_table, sin_table))
    scores = low_back(jnp.einsum('qkgd,tkd->kgqt', queries, keys, precision=HIGH) * HD ** (-0.5))
    causal = jnp.arange(seq_len)[:, None] >= jnp.arange(seq_len)[None, :]
    scores = jnp.where(causal, scores, -1e+30)
    row_peak = lax.optimization_barrier(jnp.max(scores, axis=-1, keepdims=True))
    exp_scores = jnp.exp(scores - row_peak)
    soft_weights = low(exp_scores / lax.optimization_barrier(jnp.sum(exp_scores, axis=-1, keepdims=True)))
    mixed = jnp.einsum('kgqt,tkd->qkgd', soft_weights, values, precision=HIGH).reshape(seq_len, H * HD)
    mixed = low_back(low(mixed))
    middle = resid + low_back(matmul_high(mixed, w_output))
    norm2 = low(middle * rms_scale(middle) * gain_mlp)
    gate = low_back(matmul_high(norm2, w_gate))
    up_proj = low_back(matmul_high(norm2, w_up))
    hidden = low(jax.nn.silu(gate) * up_proj)
    return middle + low_back(matmul_high(hidden, w_down))

def reference(inputs, cotangent, gain_attn, w_query, w_key, w_value, w_output, gain_mlp, w_gate, w_up, w_down):
    params = tuple((weight.astype(jnp.float32) for weight in (gain_attn, w_query, w_key, w_value, w_output, gain_mlp, w_gate, w_up, w_down)))

    def one_sequence(totals, members):
        seq_in, seq_cot = members
        result, pull_back = jax.vjp(forward, seq_in.astype(jnp.float32), *params)
        grads = pull_back(seq_cot.astype(jnp.float32))
        totals = tuple((running + fresh for running, fresh in zip(totals, grads[1:])))
        return (totals, (result.astype(jnp.bfloat16), grads[0].astype(jnp.bfloat16)))
    zero_grads = tuple((jnp.zeros_like(weight) for weight in params))
    totals, (outputs, input_grads) = lax.scan(one_sequence, zero_grads, (inputs, cotangent))
    return (outputs, input_grads, totals[0], totals[1], totals[2], totals[3], totals[4], totals[5], totals[6], totals[7], totals[8])
```

```python
import functools

import jax
import jax.numpy as jnp
import numpy as np
from jax import lax
from jax.experimental import pallas as pl
from jax.experimental.pallas import tpu as pltpu
from jax.sharding import PartitionSpec as P

H = 32
KV = 4
HD = 64
EPS = 1e-05
THETA = 10000.0
S = 4
BF = jnp.bfloat16
F32 = jnp.float32
LANES = 128
QB = 256


def matmul(left, right):
    return jnp.dot(left, right, preferred_element_type=F32)


def matmul_left_t(left, right):
    return lax.dot_general(
        left, right, (((0,), (0,)), ((), ())), preferred_element_type=F32
    )


def matmul_right_t(left, right):
    return lax.dot_general(
        left, right, (((1,), (1,)), ((), ())), preferred_element_type=F32
    )


def rms_scale(values):
    return lax.rsqrt(jnp.mean(values * values, axis=-1, keepdims=True) + EPS)


def norm_back(grad_norm, values, scale, gain):
    weighted = grad_norm * gain
    grad_values = scale * weighted - values * scale**3 * jnp.mean(
        weighted * values, axis=-1, keepdims=True
    )
    grad_gain = jnp.sum(grad_norm * values * scale, axis=0)
    return (grad_values, grad_gain)


def swap(values, axis, bit):
    return lax.ppermute(
        values, axis, [(i, i ^ bit) for i in range(lax.axis_size(axis))]
    )


def core_swap(values):
    return swap(values, "shard", 1)


def x_swap(values):
    return swap(values, "shard", 2)


def place(pieces, shard):
    full = jnp.zeros((S,) + pieces[0].shape, pieces[0].dtype)
    for mask, piece in enumerate(pieces):
        full = lax.dynamic_update_index_in_dim(full, piece, shard ^ mask, 0)
    return full


def gather(own, shard):
    across = x_swap(own)
    return place([own, core_swap(own), across, core_swap(across)], shard)


def exchange(parts, shard):
    x, core = shard // 2, shard % 2
    across = x_swap(lax.dynamic_slice_in_dim(parts, 2 * (1 - x), 2, 0))
    beside = core_swap(lax.dynamic_index_in_dim(parts, shard ^ 1, 0, False))
    far = core_swap(lax.dynamic_index_in_dim(across, 1 - core, 0, False))
    mine = lax.dynamic_index_in_dim(parts, shard, 0, False)
    near = lax.dynamic_index_in_dim(across, core, 0, False)
    return place([mine, beside, near, far], shard)


def scatter_blocks(block, shard):
    far = core_swap(block(shard ^ 3).astype(BF))
    across = x_swap((block(shard ^ 2) + far).astype(BF))
    beside = core_swap(block(shard ^ 1).astype(BF))
    return block(shard) + beside + across


def replica_scatter(term, replica):
    groups, count, rows, width = term.shape
    length = count // 2
    place_l, pair = replica // 2, replica % 2
    halves = term.reshape(groups, length, 2, rows, width)
    other = lax.dynamic_index_in_dim(halves, 1 - pair, 2, False)
    own = lax.dynamic_index_in_dim(halves, pair, 2, False)
    own = (own + swap(other, "replica", 1)).astype(BF)
    ups = [(i, i + 2) for i in range(count - 2)]
    downs = [(i + 2, i) for i in range(count - 2)]

    def chunk(index):
        return lax.dynamic_index_in_dim(
            own, jnp.clip(index, 0, length - 1), 1, False
        )

    up = down = None
    for step in range(1, length):
        up_part = chunk(length - step + place_l)
        down_part = chunk(step - length + place_l)
        if up is not None:
            up_part, down_part = up_part + up, down_part + down
        up = lax.ppermute(up_part, "replica", ups)
        down = lax.ppermute(down_part, "replica", downs)
    total = chunk(place_l).astype(F32)
    if up is not None:
        total = total + up + down
    return total


def rope_tables(seq_len):
    half = HD // 2
    freq = THETA ** (-2.0 * np.arange(half, dtype=np.float64) / HD)
    angles = np.arange(seq_len, dtype=np.float64)[:, None] * freq[None, :]
    cos, sin = np.cos(angles), np.sin(angles)
    one, zero = np.ones((seq_len, HD)), np.zeros((seq_len, HD))
    cos_head = np.concatenate([cos, cos], 1)
    sin_head = np.concatenate([-sin, sin], 1)
    tables = [
        np.concatenate([cos_head, cos_head], 1),
        np.concatenate([sin_head, sin_head], 1),
        np.concatenate([cos_head, one], 1),
        np.concatenate([sin_head, zero], 1),
    ]
    return np.stack(tables).astype(np.float32)


def turned(values):
    lane = lax.broadcasted_iota(jnp.int32, values.shape, 1)
    return jnp.where(
        lane % HD < HD // 2,
        pltpu.roll(values, LANES - HD // 2, 1),
        pltpu.roll(values, HD // 2, 1),
    )


def both(first, second):
    lane = lax.broadcasted_iota(jnp.int32, first.shape, 1)
    return jnp.where(lane < HD, first, second)


def two_heads(pair):
    zero = jnp.zeros_like(pair)
    return jnp.concatenate([both(pair, zero), both(zero, pair)], axis=0)


def causal_mask(scores, first_row):
    rows, cols = scores.shape
    row = lax.broadcasted_iota(jnp.int32, scores.shape, 0) % QB + first_row
    col = lax.broadcasted_iota(jnp.int32, scores.shape, 1)
    return jnp.where(col <= row, scores, -1e30)


def attend_kernel(pre_ref, table_ref, heads_ref, mixed_ref, log_ref, kk_ref, vv_ref):
    seq_len, width = pre_ref.shape
    q_width = width - LANES
    pairs = q_width // LANES
    blocks = seq_len // QB
    kv = pre_ref[:, q_width:]
    kv = kv * table_ref[2] + turned(kv) * table_ref[3]
    kv_b = kv.astype(BF)
    heads_ref[:, q_width:] = kv_b
    kv_r = kv_b.astype(F32)
    other = pltpu.roll(kv_r, HD, 1)
    kk_ref[...] = both(kv_r, other).astype(BF)
    vv_ref[...] = both(other, kv_r).astype(BF)
    log_ref[...] = jnp.zeros_like(log_ref)
    for i in range(blocks):
        rows = pl.ds(i * QB, QB)
        seen = (i + 1) * QB

        def pair_step(j, carry):
            cols = pl.ds(pl.multiple_of(j * LANES, LANES), LANES)
            q = pre_ref[rows, cols]
            q = q * table_ref[0, rows] + turned(q) * table_ref[1, rows]
            q = (q.astype(BF).astype(F32) * HD**-0.5).astype(BF)
            heads_ref[rows, cols] = q
            scores = matmul_right_t(two_heads(q), kk_ref[:seen])
            scores = causal_mask(scores, i * QB)
            peak = jnp.max(scores, axis=-1, keepdims=True)
            exps = jnp.exp(scores - peak)
            total = jnp.sum(exps, axis=-1, keepdims=True)
            out = matmul(exps.astype(BF), vv_ref[:seen]) / total
            mixed_ref[rows, cols] = both(out[:QB], out[QB:]).astype(BF)
            logs = peak + jnp.log(total)
            lane = lax.broadcasted_iota(jnp.int32, (QB, LANES), 1)
            old = log_ref[rows]
            old = jnp.where(lane == 2 * j, logs[:QB], old)
            log_ref[rows] = jnp.where(lane == 2 * j + 1, logs[QB:], old)
            return carry

        lax.fori_loop(0, pairs, pair_step, 0)


def attend(pre, tables):
    seq_len, width = pre.shape
    return pl.pallas_call(
        attend_kernel,
        out_shape=(
            jax.ShapeDtypeStruct((seq_len, width), BF),
            jax.ShapeDtypeStruct((seq_len, width - LANES), BF),
            jax.ShapeDtypeStruct((seq_len, LANES), F32),
        ),
        scratch_shapes=[
            pltpu.VMEM((seq_len, LANES), BF),
            pltpu.VMEM((seq_len, LANES), BF),
        ],
        compiler_params=pltpu.CompilerParams(vmem_limit_bytes=40 * 2**20),
        cost_estimate=pl.CostEstimate(
            flops=2 * 2 * 8 * seq_len * seq_len * HD,
            bytes_accessed=8 * seq_len * width,
            transcendentals=4 * seq_len * seq_len,
        ),
    )(pre, tables)


def attend_back_kernel(
    heads_ref, table_ref, log_ref, grad_ref, out_ref, kk_ref, vv_ref, dk_ref, dv_ref
):
    seq_len, width = heads_ref.shape
    q_width = width - LANES
    pairs = q_width // LANES
    blocks = seq_len // QB
    kv = heads_ref[:, q_width:].astype(F32)
    other = pltpu.roll(kv, HD, 1)
    kk_ref[...] = both(kv, other).astype(BF)
    vv_ref[...] = both(other, kv).astype(BF)
    dk_ref[...] = jnp.zeros_like(dk_ref)
    dv_ref[...] = jnp.zeros_like(dv_ref)
    for i in range(blocks):
        rows = pl.ds(i * QB, QB)
        seen = (i + 1) * QB

        def pair_step(j, carry):
            cols = pl.ds(pl.multiple_of(j * LANES, LANES), LANES)
            q = two_heads(heads_ref[rows, cols])
            grad = two_heads(grad_ref[rows, cols])
            lane = lax.broadcasted_iota(jnp.int32, (QB, LANES), 1)
            logs = log_ref[rows]
            log_col = jnp.concatenate(
                [
                    jnp.sum(jnp.where(lane == 2 * j + n, logs, 0.0), -1, keepdims=True)
                    for n in (0, 1)
                ],
                axis=0,
            )
            scores = matmul_right_t(q, kk_ref[:seen])
            soft = jnp.exp(causal_mask(scores, i * QB) - log_col)
            grad_soft = matmul_right_t(grad, vv_ref[:seen])
            inner = jnp.sum(soft * grad_soft, axis=-1, keepdims=True)
            grad_scores = (soft * (grad_soft - inner)).astype(BF)
            dq = matmul(grad_scores, kk_ref[:seen])
            dq = both(dq[:QB], dq[QB:]) * HD**-0.5
            dq = dq * table_ref[0, rows] - turned(dq) * table_ref[1, rows]
            out_ref[rows, cols] = dq.astype(BF)
            dk_ref[:seen] += matmul_left_t(grad_scores, q)
            dv_ref[:seen] += matmul_left_t(soft.astype(BF), grad)
            return carry

        lax.fori_loop(0, pairs, pair_step, 0)
    dk, dv = dk_ref[...], dv_ref[...]
    dk, dv = dk + pltpu.roll(dk, HD, 1), dv + pltpu.roll(dv, HD, 1)
    dkv = both(dk, dv)
    dkv = dkv * table_ref[2] - turned(dkv) * table_ref[3]
    out_ref[:, q_width:] = dkv.astype(BF)


def attend_back(heads, tables, logs, grad_mixed):
    seq_len, width = heads.shape
    return pl.pallas_call(
        attend_back_kernel,
        out_shape=jax.ShapeDtypeStruct((seq_len, width), BF),
        scratch_shapes=[
            pltpu.VMEM((seq_len, LANES), BF),
            pltpu.VMEM((seq_len, LANES), BF),
            pltpu.VMEM((seq_len, LANES), F32),
            pltpu.VMEM((seq_len, LANES), F32),
        ],
        compiler_params=pltpu.CompilerParams(vmem_limit_bytes=48 * 2**20),
        cost_estimate=pl.CostEstimate(
            flops=5 * 2 * 8 * seq_len * seq_len * HD,
            bytes_accessed=8 * seq_len * width,
            transcendentals=4 * seq_len * seq_len,
        ),
    )(heads, tables, logs, grad_mixed)


def on_device(
    inputs, cotangent, gain_attn, w_query, w_key, w_value, w_output, gain_mlp, w_gate, w_up, w_down
):
    shard, replica = lax.axis_index("shard"), lax.axis_index("replica")
    replicas = lax.axis_size("replica")
    tokens, model = inputs.shape[1:]
    seq_len = tokens * S
    rows = w_query.shape[0]
    q_cols, kv_cols = w_query.shape[1] // S, w_key.shape[1] // S
    ff_cols = w_gate.shape[1] // S
    tables = jnp.asarray(rope_tables(seq_len))

    def by_columns(*weights):
        parts = [w.reshape(rows, S, -1).transpose(1, 0, 2) for w in weights]
        full = exchange(jnp.concatenate(parts, axis=2), shard)
        return full.reshape(S * rows, -1)

    def rows_of(array, index):
        return lax.dynamic_slice_in_dim(array, index * tokens, tokens, 0)

    own = inputs[0]
    gains = gather(jnp.stack([gain_attn, gain_mlp]), shard)
    gain_one, gain_two = (
        gains[:, i].reshape(model).astype(F32) for i in range(2)
    )
    entire = gather(own, shard).reshape(seq_len, model)
    w_heads = by_columns(w_query, w_key, w_value)
    grad_out = gather(cotangent[0], shard).reshape(seq_len, model)
    w_ff = by_columns(w_gate, w_up)

    entire_f = entire.astype(F32)
    norm1 = (entire_f * rms_scale(entire_f) * gain_one).astype(BF)
    heads, mixed, logs = attend(matmul(norm1, w_heads), tables)
    resid = own.astype(F32)
    middle = resid + scatter_blocks(
        lambda j: matmul(rows_of(mixed, j), w_output), shard
    )
    scale_two = rms_scale(middle)
    norm2 = gather((middle * scale_two * gain_two).astype(BF), shard)
    norm2 = norm2.reshape(seq_len, model)
    gate_up = matmul(norm2, w_ff)
    gate, up_proj = gate_up[:, :ff_cols], gate_up[:, ff_cols:]
    sigmoid_gate = jax.nn.sigmoid(gate)
    silu_gate = gate * sigmoid_gate
    hidden = (silu_gate * up_proj).astype(BF)
    grad_hidden = matmul_right_t(grad_out, w_down)
    grad_gate = grad_hidden * up_proj * sigmoid_gate * (1.0 + gate * (1.0 - sigmoid_gate))
    grad_ff = jnp.concatenate(
        [grad_gate.astype(BF), (grad_hidden * silu_gate).astype(BF)], axis=1
    )
    term_down = matmul_left_t(hidden, grad_out).astype(BF)
    piece_down = replica_scatter(
        term_down.reshape(1, replicas, -1, model), replica
    ).reshape(-1, model)
    grad_norm2 = scatter_blocks(
        lambda j: matmul_right_t(rows_of(grad_ff, j), w_ff), shard
    )
    term_ff = matmul_left_t(norm2, grad_ff).astype(BF)
    piece_ff = replica_scatter(term_ff.reshape(S, replicas, -1, 2 * ff_cols), replica)
    output = middle + scatter_blocks(
        lambda j: matmul(rows_of(hidden, j), w_down), shard
    )
    output = output.astype(BF)[None]

    grad_middle_norm, term_gain_two = norm_back(grad_norm2, middle, scale_two, gain_two)
    grad_middle = cotangent[0].astype(F32) + grad_middle_norm
    grad_middle_all = gather(grad_middle.astype(BF), shard).reshape(seq_len, model)
    grad_mixed = matmul_right_t(grad_middle_all, w_output).astype(BF)
    term_output = matmul_left_t(mixed, grad_middle_all).astype(BF)
    piece_output = replica_scatter(
        term_output.reshape(1, replicas, -1, model), replica
    ).reshape(-1, model)
    grad_heads = attend_back(heads, tables, logs, grad_mixed)
    term_heads = matmul_left_t(norm1, grad_heads).astype(BF)
    piece_heads = replica_scatter(
        term_heads.reshape(S, replicas, -1, grad_heads.shape[1]), replica
    )
    grad_norm1 = scatter_blocks(
        lambda j: matmul_right_t(rows_of(grad_heads, j), w_heads), shard
    )
    grad_resid_norm, term_gain_one = norm_back(
        grad_norm1, resid, rms_scale(resid), gain_one
    )
    input_grad = (grad_middle + grad_resid_norm).astype(BF)[None]

    piece_ff = exchange(piece_ff.astype(BF), shard).astype(F32)
    piece_heads = exchange(piece_heads.astype(BF), shard).astype(F32)

    def columns(pieces, start, width):
        part = pieces[:, :, start : start + width]
        return part.transpose(1, 0, 2).reshape(part.shape[1], -1)

    gain_terms = lax.psum(
        jnp.stack([term_gain_one, term_gain_two]), ("shard", "replica")
    )
    share = model // (S * replicas)
    gain_pieces = lax.dynamic_slice_in_dim(
        gain_terms, (shard * replicas + replica) * share, share, 1
    )
    return (
        output,
        input_grad,
        gain_pieces[0],
        columns(piece_heads, 0, q_cols),
        columns(piece_heads, q_cols, kv_cols),
        columns(piece_heads, q_cols + kv_cols, kv_cols),
        piece_output,
        gain_pieces[1],
        columns(piece_ff, 0, ff_cols),
        columns(piece_ff, ff_cols, ff_cols),
        piece_down,
    )


def solution(mesh):
    placed = (
        P("replica", "shard", None),
        P("replica", "shard", None),
        P("shard"),
        P("shard", None),
        P("shard", None),
        P("shard", None),
        P("shard", None),
        P("shard"),
        P("shard", None),
        P("shard", None),
        P("shard", None),
    )
    both_axes = ("shard", "replica")
    return jax.shard_map(
        on_device,
        mesh=mesh,
        in_specs=placed,
        out_specs=(
            P("replica", "shard", None),
            P("replica", "shard", None),
            P(both_axes),
            P(both_axes, None),
            P(both_axes, None),
            P(both_axes, None),
            P(both_axes, None),
            P(both_axes),
            P(both_axes, None),
            P(both_axes, None),
            P(both_axes, None),
        ),
        check_vma=False,
    )
```

```python
import functools

import jax
import jax.numpy as jnp
import numpy as np
from jax import lax
from jax.experimental import pallas as pl
from jax.experimental.pallas import tpu as pltpu
from jax.sharding import PartitionSpec as P

H = 32
KV = 4
HD = 64
EPS = 1e-05
THETA = 10000.0
S = 4
BF = jnp.bfloat16
F32 = jnp.float32
LANES = 128
QB = 256


def matmul(left, right):
    return jnp.dot(left, right, preferred_element_type=F32)


def matmul_left_t(left, right):
    return lax.dot_general(
        left, right, (((0,), (0,)), ((), ())), preferred_element_type=F32
    )


def matmul_right_t(left, right):
    return lax.dot_general(
        left, right, (((1,), (1,)), ((), ())), preferred_element_type=F32
    )


def rms_scale(values):
    return lax.rsqrt(jnp.mean(values * values, axis=-1, keepdims=True) + EPS)


def norm_back(grad_norm, values, scale, gain):
    weighted = grad_norm * gain
    return scale * weighted - values * scale**3 * jnp.mean(
        weighted * values, axis=-1, keepdims=True
    )


def swap(values, axis, bit):
    return lax.ppermute(
        values, axis, [(i, i ^ bit) for i in range(lax.axis_size(axis))]
    )


def core_swap(values):
    return swap(values, "shard", 1)


def x_swap(values):
    return swap(values, "shard", 2)


def place(pieces, shard):
    full = jnp.zeros((S,) + pieces[0].shape, pieces[0].dtype)
    for mask, piece in enumerate(pieces):
        full = lax.dynamic_update_index_in_dim(full, piece, shard ^ mask, 0)
    return full


def gather(own, shard):
    across = x_swap(own)
    return place([own, core_swap(own), across, core_swap(across)], shard)


def exchange(parts, shard):
    x, core = shard // 2, shard % 2
    across = x_swap(lax.dynamic_slice_in_dim(parts, 2 * (1 - x), 2, 0))
    beside = core_swap(lax.dynamic_index_in_dim(parts, shard ^ 1, 0, False))
    far = core_swap(lax.dynamic_index_in_dim(across, 1 - core, 0, False))
    mine = lax.dynamic_index_in_dim(parts, shard, 0, False)
    near = lax.dynamic_index_in_dim(across, core, 0, False)
    return [mine, beside, near, far]


def scatter_blocks(block, shard):
    far = core_swap(block(shard ^ 3).astype(BF))
    across = x_swap((block(shard ^ 2) + far).astype(BF))
    beside = core_swap(block(shard ^ 1).astype(BF))
    return block(shard) + beside + across


def replica_scatter(term, replica, order):
    groups, count, rows, width = term.shape
    bits = count.bit_length() - 1
    left = list(range(bits - 1, -1, -1))
    parts = [term.reshape((groups,) + (2,) * bits + (rows, width))]
    for bit in [b for b in order if b < bits] + list(range(len(order), bits)):
        axis = 1 + left.index(bit)
        left.remove(bit)
        mine = (replica >> bit) % 2
        other = sum(
            lax.dynamic_index_in_dim(p, 1 - mine, axis, False).astype(F32)
            for p in parts
        )
        parts = [lax.dynamic_index_in_dim(p, mine, axis, False) for p in parts]
        parts.append(swap(other.astype(BF), "replica", 1 << bit))
    return sum(p.astype(F32) for p in parts)


def finish_kernel(widths, shard_ref, *refs):
    pieces, rest = refs[:S], refs[S:]
    weights, gain_ref = rest[: len(widths)], rest[len(widths)]
    outs, gain_out = rest[len(widths) + 1 : -1], rest[-1]
    shard = shard_ref[0]
    total = jnp.zeros(gain_out.shape, F32)
    for mask, piece in enumerate(pieces):
        owner = shard ^ mask
        start = 0
        for width, weight, out in zip(widths, weights, outs):
            if width % LANES == 0:
                cols = pl.ds(pl.multiple_of(owner * width, LANES), width)
                part = piece[:, start : start + width].astype(F32)
                out[:, cols] = part
                total += jnp.sum(
                    part * weight[:, cols].astype(F32), axis=1, keepdims=True
                )
            else:
                base = start // LANES * LANES
                part = piece[:, base : base + LANES].astype(F32)
                lane = lax.broadcasted_iota(jnp.int32, part.shape, 1) // HD
                turned_part = pltpu.roll(part, HD, 1)
                side = owner % 2
                part = jnp.where(side == (start - base) // HD, part, turned_part)
                part = jnp.where(lane == side, part, 0.0)
                cols = pl.ds(pl.multiple_of(owner // 2 * LANES, LANES), LANES)
                out[:, cols] = jnp.where(lane == side, part, out[:, cols])
                total += jnp.sum(
                    part * weight[:, cols].astype(F32), axis=1, keepdims=True
                )
            start += width
    gain_out[...] = total / gain_ref[...]


def finish(pieces, weights, gain, shard, replica):
    rows = pieces[0].shape[0]
    widths = tuple(w.shape[1] // S for w in weights)
    own = [lax.dynamic_slice_in_dim(w, replica * rows, rows, 0) for w in weights]
    own_gain = lax.dynamic_slice_in_dim(gain, replica * rows, rows, 0)
    vmem = pl.BlockSpec(memory_space=pltpu.VMEM)
    result = pl.pallas_call(
        functools.partial(finish_kernel, widths),
        out_shape=[jax.ShapeDtypeStruct(w.shape, F32) for w in own]
        + [jax.ShapeDtypeStruct((rows, 1), F32)],
        in_specs=[pl.BlockSpec(memory_space=pltpu.SMEM)]
        + [vmem] * (S + len(weights) + 1),
        out_specs=[vmem] * (len(weights) + 1),
        compiler_params=pltpu.CompilerParams(vmem_limit_bytes=32 * 2**20),
    )(
        shard.reshape(1).astype(jnp.int32),
        *pieces,
        *own,
        own_gain.astype(F32).reshape(rows, 1),
    )
    return result[:-1], result[-1].reshape(rows)


def rope_tables(seq_len):
    half = HD // 2
    freq = THETA ** (-2.0 * np.arange(half, dtype=np.float64) / HD)
    angles = np.arange(seq_len, dtype=np.float64)[:, None] * freq[None, :]
    cos, sin = np.cos(angles), np.sin(angles)
    one, zero = np.ones((seq_len, HD)), np.zeros((seq_len, HD))
    cos_head = np.concatenate([cos, cos], 1)
    sin_head = np.concatenate([-sin, sin], 1)
    tables = [
        np.concatenate([cos_head, cos_head], 1),
        np.concatenate([sin_head, sin_head], 1),
        np.concatenate([cos_head, one], 1),
        np.concatenate([sin_head, zero], 1),
    ]
    return np.stack(tables).astype(np.float32)


def turned(values):
    lane = lax.broadcasted_iota(jnp.int32, values.shape, 1)
    return jnp.where(
        lane % HD < HD // 2,
        pltpu.roll(values, LANES - HD // 2, 1),
        pltpu.roll(values, HD // 2, 1),
    )


def both(first, second):
    lane = lax.broadcasted_iota(jnp.int32, first.shape, 1)
    return jnp.where(lane < HD, first, second)


def two_heads(pair):
    zero = jnp.zeros_like(pair)
    return jnp.concatenate([both(pair, zero), both(zero, pair)], axis=0)


def causal_mask(scores, first_row):
    rows, cols = scores.shape
    row = lax.broadcasted_iota(jnp.int32, scores.shape, 0) % QB + first_row
    col = lax.broadcasted_iota(jnp.int32, scores.shape, 1)
    return jnp.where(col <= row, scores, -1e30)


def attend_kernel(pre_ref, table_ref, heads_ref, mixed_ref, log_ref, kk_ref, vv_ref):
    seq_len, width = pre_ref.shape
    q_width = width - LANES
    pairs = q_width // LANES
    blocks = seq_len // QB
    kv = pre_ref[:, q_width:]
    kv = kv * table_ref[2] + turned(kv) * table_ref[3]
    kv_b = kv.astype(BF)
    heads_ref[:, q_width:] = kv_b
    kv_r = kv_b.astype(F32)
    other = pltpu.roll(kv_r, HD, 1)
    kk_ref[...] = both(kv_r, other).astype(BF)
    vv_ref[...] = both(other, kv_r).astype(BF)
    log_ref[...] = jnp.zeros_like(log_ref)
    for i in range(blocks):
        rows = pl.ds(i * QB, QB)
        seen = (i + 1) * QB

        def pair_step(j, carry):
            cols = pl.ds(pl.multiple_of(j * LANES, LANES), LANES)
            q = pre_ref[rows, cols]
            q = q * table_ref[0, rows] + turned(q) * table_ref[1, rows]
            q = (q.astype(BF).astype(F32) * HD**-0.5).astype(BF)
            heads_ref[rows, cols] = q
            scores = matmul_right_t(two_heads(q), kk_ref[:seen])
            scores = causal_mask(scores, i * QB)
            peak = jnp.max(scores, axis=-1, keepdims=True)
            exps = jnp.exp(scores - peak)
            total = jnp.sum(exps, axis=-1, keepdims=True)
            out = matmul(exps.astype(BF), vv_ref[:seen]) / total
            mixed_ref[rows, cols] = both(out[:QB], out[QB:]).astype(BF)
            logs = peak + jnp.log(total)
            lane = lax.broadcasted_iota(jnp.int32, (QB, LANES), 1)
            old = log_ref[rows]
            old = jnp.where(lane == 2 * j, logs[:QB], old)
            log_ref[rows] = jnp.where(lane == 2 * j + 1, logs[QB:], old)
            return carry

        lax.fori_loop(0, pairs, pair_step, 0)


def attend(pre, tables):
    seq_len, width = pre.shape
    return pl.pallas_call(
        attend_kernel,
        out_shape=(
            jax.ShapeDtypeStruct((seq_len, width), BF),
            jax.ShapeDtypeStruct((seq_len, width - LANES), BF),
            jax.ShapeDtypeStruct((seq_len, LANES), F32),
        ),
        scratch_shapes=[
            pltpu.VMEM((seq_len, LANES), BF),
            pltpu.VMEM((seq_len, LANES), BF),
        ],
        compiler_params=pltpu.CompilerParams(vmem_limit_bytes=40 * 2**20),
        cost_estimate=pl.CostEstimate(
            flops=2 * 2 * 8 * seq_len * seq_len * HD,
            bytes_accessed=8 * seq_len * width,
            transcendentals=4 * seq_len * seq_len,
        ),
    )(pre, tables)


def attend_back_kernel(
    heads_ref, table_ref, log_ref, grad_ref, out_ref, kk_ref, vv_ref, dk_ref, dv_ref
):
    seq_len, width = heads_ref.shape
    q_width = width - LANES
    pairs = q_width // LANES
    blocks = seq_len // QB
    kv = heads_ref[:, q_width:].astype(F32)
    other = pltpu.roll(kv, HD, 1)
    kk_ref[...] = both(kv, other).astype(BF)
    vv_ref[...] = both(other, kv).astype(BF)
    dk_ref[...] = jnp.zeros_like(dk_ref)
    dv_ref[...] = jnp.zeros_like(dv_ref)
    for i in range(blocks):
        rows = pl.ds(i * QB, QB)
        seen = (i + 1) * QB

        def pair_step(j, carry):
            cols = pl.ds(pl.multiple_of(j * LANES, LANES), LANES)
            q = two_heads(heads_ref[rows, cols])
            grad = two_heads(grad_ref[rows, cols])
            lane = lax.broadcasted_iota(jnp.int32, (QB, LANES), 1)
            logs = log_ref[rows]
            log_col = jnp.concatenate(
                [
                    jnp.sum(jnp.where(lane == 2 * j + n, logs, 0.0), -1, keepdims=True)
                    for n in (0, 1)
                ],
                axis=0,
            )
            scores = matmul_right_t(q, kk_ref[:seen])
            soft = jnp.exp(causal_mask(scores, i * QB) - log_col)
            grad_soft = matmul_right_t(grad, vv_ref[:seen])
            inner = jnp.sum(soft * grad_soft, axis=-1, keepdims=True)
            grad_scores = (soft * (grad_soft - inner)).astype(BF)
            dq = matmul(grad_scores, kk_ref[:seen])
            dq = both(dq[:QB], dq[QB:]) * HD**-0.5
            dq = dq * table_ref[0, rows] - turned(dq) * table_ref[1, rows]
            out_ref[rows, cols] = dq.astype(BF)
            dk_ref[:seen] += matmul_left_t(grad_scores, q)
            dv_ref[:seen] += matmul_left_t(soft.astype(BF), grad)
            return carry

        lax.fori_loop(0, pairs, pair_step, 0)
    dk, dv = dk_ref[...], dv_ref[...]
    dk, dv = dk + pltpu.roll(dk, HD, 1), dv + pltpu.roll(dv, HD, 1)
    dkv = both(dk, dv)
    dkv = dkv * table_ref[2] - turned(dkv) * table_ref[3]
    out_ref[:, q_width:] = dkv.astype(BF)


def attend_back(heads, tables, logs, grad_mixed):
    seq_len, width = heads.shape
    return pl.pallas_call(
        attend_back_kernel,
        out_shape=jax.ShapeDtypeStruct((seq_len, width), BF),
        scratch_shapes=[
            pltpu.VMEM((seq_len, LANES), BF),
            pltpu.VMEM((seq_len, LANES), BF),
            pltpu.VMEM((seq_len, LANES), F32),
            pltpu.VMEM((seq_len, LANES), F32),
        ],
        compiler_params=pltpu.CompilerParams(vmem_limit_bytes=48 * 2**20),
        cost_estimate=pl.CostEstimate(
            flops=5 * 2 * 8 * seq_len * seq_len * HD,
            bytes_accessed=8 * seq_len * width,
            transcendentals=4 * seq_len * seq_len,
        ),
    )(heads, tables, logs, grad_mixed)


def on_device(
    inputs, cotangent, gain_attn, w_query, w_key, w_value, w_output, gain_mlp, w_gate, w_up, w_down
):
    shard, replica = lax.axis_index("shard"), lax.axis_index("replica")
    replicas = lax.axis_size("replica")
    tokens, model = inputs.shape[1:]
    seq_len = tokens * S
    rows = w_query.shape[0]
    q_cols, kv_cols = w_query.shape[1] // S, w_key.shape[1] // S
    ff_cols = w_gate.shape[1] // S
    tables = jnp.asarray(rope_tables(seq_len))

    def by_columns(*weights):
        parts = [w.reshape(rows, S, -1).transpose(1, 0, 2) for w in weights]
        full = place(exchange(jnp.concatenate(parts, axis=2), shard), shard)
        return full.reshape(S * rows, -1)

    def rows_of(array, index):
        return lax.dynamic_slice_in_dim(array, index * tokens, tokens, 0)

    own = inputs[0]
    gains = gather(jnp.stack([gain_attn, gain_mlp]), shard)
    gain_one, gain_two = (
        gains[:, i].reshape(model).astype(F32) for i in range(2)
    )
    entire = gather(own, shard).reshape(seq_len, model)
    w_heads = by_columns(w_query, w_key, w_value)
    grad_out = gather(cotangent[0], shard).reshape(seq_len, model)
    w_ff = by_columns(w_gate, w_up)

    entire_f = entire.astype(F32)
    norm1 = (entire_f * rms_scale(entire_f) * gain_one).astype(BF)
    heads, mixed, logs = attend(matmul(norm1, w_heads), tables)
    resid = own.astype(F32)
    middle = resid + scatter_blocks(
        lambda j: matmul(rows_of(mixed, j), w_output), shard
    )
    scale_two = rms_scale(middle)
    norm2 = gather((middle * scale_two * gain_two).astype(BF), shard)
    norm2 = norm2.reshape(seq_len, model)
    gate_up = matmul(norm2, w_ff)
    gate, up_proj = gate_up[:, :ff_cols], gate_up[:, ff_cols:]
    sigmoid_gate = jax.nn.sigmoid(gate)
    silu_gate = gate * sigmoid_gate
    hidden = (silu_gate * up_proj).astype(BF)
    grad_hidden = matmul_right_t(grad_out, w_down)
    grad_gate = grad_hidden * up_proj * sigmoid_gate * (1.0 + gate * (1.0 - sigmoid_gate))
    grad_ff = jnp.concatenate(
        [grad_gate.astype(BF), (grad_hidden * silu_gate).astype(BF)], axis=1
    )
    term_down = matmul_left_t(hidden, grad_out).astype(BF)
    piece_down = replica_scatter(
        term_down.reshape(1, replicas, -1, model), replica, (1, 0, 2)
    ).reshape(-1, model)
    grad_norm2 = scatter_blocks(
        lambda j: matmul_right_t(rows_of(grad_ff, j), w_ff), shard
    )
    term_ff = matmul_left_t(norm2, grad_ff).astype(BF)
    piece_ff = replica_scatter(
        term_ff.reshape(S, replicas, -1, 2 * ff_cols), replica, (0, 1, 2)
    )
    output = middle + scatter_blocks(
        lambda j: matmul(rows_of(hidden, j), w_down), shard
    )
    output = output.astype(BF)[None]

    grad_middle_norm = norm_back(grad_norm2, middle, scale_two, gain_two)
    grad_middle = cotangent[0].astype(F32) + grad_middle_norm
    grad_middle_all = gather(grad_middle.astype(BF), shard).reshape(seq_len, model)
    grad_mixed = matmul_right_t(grad_middle_all, w_output).astype(BF)
    term_output = matmul_left_t(mixed, grad_middle_all).astype(BF)
    piece_output = replica_scatter(
        term_output.reshape(1, replicas, -1, model), replica, (0, 1, 2)
    ).reshape(-1, model)
    grad_heads = attend_back(heads, tables, logs, grad_mixed)
    term_heads = matmul_left_t(norm1, grad_heads).astype(BF)
    piece_heads = replica_scatter(
        term_heads.reshape(S, replicas, -1, grad_heads.shape[1]), replica, (0, 1, 2)
    )
    grad_norm1 = scatter_blocks(
        lambda j: matmul_right_t(rows_of(grad_heads, j), w_heads), shard
    )
    grad_resid_norm = norm_back(
        grad_norm1, resid, rms_scale(resid), gain_one
    )
    input_grad = (grad_middle + grad_resid_norm).astype(BF)[None]

    (grad_gate_own, grad_up_own), grad_gain_two = finish(
        exchange(piece_ff.astype(BF), shard), (w_gate, w_up), gain_mlp, shard, replica
    )
    (grad_query, grad_key, grad_value), grad_gain_one = finish(
        exchange(piece_heads.astype(BF), shard),
        (w_query, w_key, w_value),
        gain_attn,
        shard,
        replica,
    )
    return (
        output,
        input_grad,
        grad_gain_one,
        grad_query,
        grad_key,
        grad_value,
        piece_output,
        grad_gain_two,
        grad_gate_own,
        grad_up_own,
        piece_down,
    )


def solution(mesh):
    placed = (
        P("replica", "shard", None),
        P("replica", "shard", None),
        P("shard"),
        P("shard", None),
        P("shard", None),
        P("shard", None),
        P("shard", None),
        P("shard"),
        P("shard", None),
        P("shard", None),
        P("shard", None),
    )
    both_axes = ("shard", "replica")
    return jax.shard_map(
        on_device,
        mesh=mesh,
        in_specs=placed,
        out_specs=(
            P("replica", "shard", None),
            P("replica", "shard", None),
            P(both_axes),
            P(both_axes, None),
            P(both_axes, None),
            P(both_axes, None),
            P(both_axes, None),
            P(both_axes),
            P(both_axes, None),
            P(both_axes, None),
            P(both_axes, None),
        ),
        check_vma=False,
    )
```

```python
import functools

import jax
import jax.numpy as jnp
import numpy as np
from jax import lax
from jax.experimental import pallas as pl
from jax.experimental.pallas import tpu as pltpu
from jax.sharding import PartitionSpec as P

H = 32
KV = 4
HD = 64
EPS = 1e-05
THETA = 10000.0
S = 4
BF = jnp.bfloat16
F32 = jnp.float32
LANES = 128
QB = 256


def matmul(left, right):
    return jnp.dot(left, right, preferred_element_type=F32)


def matmul_left_t(left, right):
    return lax.dot_general(
        left, right, (((0,), (0,)), ((), ())), preferred_element_type=F32
    )


def matmul_right_t(left, right):
    return lax.dot_general(
        left, right, (((1,), (1,)), ((), ())), preferred_element_type=F32
    )


def rms_scale(values):
    return lax.rsqrt(jnp.mean(values * values, axis=-1, keepdims=True) + EPS)


def norm_back(grad_norm, values, scale, gain):
    weighted = grad_norm * gain
    return scale * weighted - values * scale**3 * jnp.mean(
        weighted * values, axis=-1, keepdims=True
    )


def swap(values, axis, bit):
    return lax.ppermute(
        values, axis, [(i, i ^ bit) for i in range(lax.axis_size(axis))]
    )


def core_swap(values):
    return swap(values, "shard", 1)


def x_swap(values):
    return swap(values, "shard", 2)


def place(pieces, shard):
    full = jnp.zeros((S,) + pieces[0].shape, pieces[0].dtype)
    for mask, piece in enumerate(pieces):
        full = lax.dynamic_update_index_in_dim(full, piece, shard ^ mask, 0)
    return full


def gather(own, shard):
    across = x_swap(own)
    return place([own, core_swap(own), across, core_swap(across)], shard)


def exchange(parts, shard):
    x, core = shard // 2, shard % 2
    across = x_swap(lax.dynamic_slice_in_dim(parts, 2 * (1 - x), 2, 0))
    beside = core_swap(lax.dynamic_index_in_dim(parts, shard ^ 1, 0, False))
    far = core_swap(lax.dynamic_index_in_dim(across, 1 - core, 0, False))
    mine = lax.dynamic_index_in_dim(parts, shard, 0, False)
    near = lax.dynamic_index_in_dim(across, core, 0, False)
    return [mine, beside, near, far]


def scatter_blocks(block, shard):
    far = core_swap(block(shard ^ 3).astype(BF))
    across = x_swap((block(shard ^ 2) + far).astype(BF))
    beside = core_swap(block(shard ^ 1).astype(BF))
    return block(shard) + beside + across


def replica_scatter(term, replica, order):
    groups, count, rows, width = term.shape
    bits = count.bit_length() - 1
    left = list(range(bits - 1, -1, -1))
    parts = [term.reshape((groups,) + (2,) * bits + (rows, width))]
    for bit in [b for b in order if b < bits] + list(range(len(order), bits)):
        axis = 1 + left.index(bit)
        left.remove(bit)
        mine = (replica >> bit) % 2
        other = sum(
            lax.dynamic_index_in_dim(p, 1 - mine, axis, False).astype(F32)
            for p in parts
        )
        parts = [lax.dynamic_index_in_dim(p, mine, axis, False) for p in parts]
        parts.append(swap(other.astype(BF), "replica", 1 << bit))
    return sum(p.astype(F32) for p in parts)


def finish_kernel(widths, shard_ref, *refs):
    pieces, rest = refs[:S], refs[S:]
    weights, gain_ref = rest[: len(widths)], rest[len(widths)]
    outs, gain_out = rest[len(widths) + 1 : -1], rest[-1]
    shard = shard_ref[0]
    total = jnp.zeros(gain_out.shape, F32)
    for mask, piece in enumerate(pieces):
        owner = shard ^ mask
        start = 0
        for width, weight, out in zip(widths, weights, outs):
            if width % LANES == 0:
                cols = pl.ds(pl.multiple_of(owner * width, LANES), width)
                part = piece[:, start : start + width].astype(F32)
                out[:, cols] = part
                total += jnp.sum(
                    part * weight[:, cols].astype(F32), axis=1, keepdims=True
                )
            else:
                base = start // LANES * LANES
                part = piece[:, base : base + LANES].astype(F32)
                lane = lax.broadcasted_iota(jnp.int32, part.shape, 1) // HD
                turned_part = pltpu.roll(part, HD, 1)
                side = owner % 2
                part = jnp.where(side == (start - base) // HD, part, turned_part)
                part = jnp.where(lane == side, part, 0.0)
                cols = pl.ds(pl.multiple_of(owner // 2 * LANES, LANES), LANES)
                out[:, cols] = jnp.where(lane == side, part, out[:, cols])
                total += jnp.sum(
                    part * weight[:, cols].astype(F32), axis=1, keepdims=True
                )
            start += width
    gain_out[...] = total / gain_ref[...]


def finish(pieces, weights, gain, shard, replica):
    rows = pieces[0].shape[0]
    widths = tuple(w.shape[1] // S for w in weights)
    own = [lax.dynamic_slice_in_dim(w, replica * rows, rows, 0) for w in weights]
    own_gain = lax.dynamic_slice_in_dim(gain, replica * rows, rows, 0)
    vmem = pl.BlockSpec(memory_space=pltpu.VMEM)
    result = pl.pallas_call(
        functools.partial(finish_kernel, widths),
        out_shape=[jax.ShapeDtypeStruct(w.shape, F32) for w in own]
        + [jax.ShapeDtypeStruct((rows, 1), F32)],
        in_specs=[pl.BlockSpec(memory_space=pltpu.SMEM)]
        + [vmem] * (S + len(weights) + 1),
        out_specs=[vmem] * (len(weights) + 1),
        compiler_params=pltpu.CompilerParams(vmem_limit_bytes=32 * 2**20),
    )(
        shard.reshape(1).astype(jnp.int32),
        *pieces,
        *own,
        own_gain.astype(F32).reshape(rows, 1),
    )
    return result[:-1], result[-1].reshape(rows)


def rope_tables(seq_len):
    half = HD // 2
    freq = THETA ** (-2.0 * np.arange(half, dtype=np.float64) / HD)
    angles = np.arange(seq_len, dtype=np.float64)[:, None] * freq[None, :]
    cos, sin = np.cos(angles), np.sin(angles)
    one, zero = np.ones((seq_len, HD)), np.zeros((seq_len, HD))
    cos_head = np.concatenate([cos, cos], 1)
    sin_head = np.concatenate([-sin, sin], 1)
    tables = [
        np.concatenate([cos_head, cos_head], 1),
        np.concatenate([sin_head, sin_head], 1),
        np.concatenate([cos_head, one], 1),
        np.concatenate([sin_head, zero], 1),
    ]
    return np.stack(tables).astype(np.float32)


def turned(values):
    lane = lax.broadcasted_iota(jnp.int32, values.shape, 1)
    return jnp.where(
        lane % HD < HD // 2,
        pltpu.roll(values, LANES - HD // 2, 1),
        pltpu.roll(values, HD // 2, 1),
    )


def both(first, second):
    lane = lax.broadcasted_iota(jnp.int32, first.shape, 1)
    return jnp.where(lane < HD, first, second)


def two_heads(pair):
    zero = jnp.zeros_like(pair)
    return jnp.concatenate([both(pair, zero), both(zero, pair)], axis=0)


def causal_mask(scores, first_row):
    rows, cols = scores.shape
    row = lax.broadcasted_iota(jnp.int32, scores.shape, 0) % QB + first_row
    col = lax.broadcasted_iota(jnp.int32, scores.shape, 1)
    return jnp.where(col <= row, scores, -1e30)


def attend_kernel(pre_ref, table_ref, heads_ref, mixed_ref, log_ref, kk_ref, vv_ref):
    seq_len, width = pre_ref.shape
    q_width = width - LANES
    pairs = q_width // LANES
    blocks = seq_len // QB
    kv = pre_ref[:, q_width:]
    kv = kv * table_ref[2] + turned(kv) * table_ref[3]
    kv_b = kv.astype(BF)
    heads_ref[:, q_width:] = kv_b
    kv_r = kv_b.astype(F32)
    other = pltpu.roll(kv_r, HD, 1)
    kk_ref[...] = both(kv_r, other).astype(BF)
    vv_ref[...] = both(other, kv_r).astype(BF)
    log_ref[...] = jnp.zeros_like(log_ref)
    for i in range(blocks):
        rows = pl.ds(i * QB, QB)
        seen = (i + 1) * QB

        def pair_step(j, carry):
            cols = pl.ds(pl.multiple_of(j * LANES, LANES), LANES)
            q = pre_ref[rows, cols]
            q = q * table_ref[0, rows] + turned(q) * table_ref[1, rows]
            q = (q.astype(BF).astype(F32) * HD**-0.5).astype(BF)
            heads_ref[rows, cols] = q
            scores = matmul_right_t(two_heads(q), kk_ref[:seen])
            scores = causal_mask(scores, i * QB)
            peak = jnp.max(scores, axis=-1, keepdims=True)
            exps = jnp.exp(scores - peak)
            total = jnp.sum(exps, axis=-1, keepdims=True)
            out = matmul(exps.astype(BF), vv_ref[:seen]) / total
            mixed_ref[rows, cols] = both(out[:QB], out[QB:]).astype(BF)
            logs = peak + jnp.log(total)
            lane = lax.broadcasted_iota(jnp.int32, (QB, LANES), 1)
            old = log_ref[rows]
            old = jnp.where(lane == 2 * j, logs[:QB], old)
            log_ref[rows] = jnp.where(lane == 2 * j + 1, logs[QB:], old)
            return carry

        lax.fori_loop(0, pairs, pair_step, 0)


def attend(pre, tables):
    seq_len, width = pre.shape
    return pl.pallas_call(
        attend_kernel,
        out_shape=(
            jax.ShapeDtypeStruct((seq_len, width), BF),
            jax.ShapeDtypeStruct((seq_len, width - LANES), BF),
            jax.ShapeDtypeStruct((seq_len, LANES), F32),
        ),
        scratch_shapes=[
            pltpu.VMEM((seq_len, LANES), BF),
            pltpu.VMEM((seq_len, LANES), BF),
        ],
        compiler_params=pltpu.CompilerParams(vmem_limit_bytes=40 * 2**20),
        cost_estimate=pl.CostEstimate(
            flops=2 * 2 * 8 * seq_len * seq_len * HD,
            bytes_accessed=8 * seq_len * width,
            transcendentals=4 * seq_len * seq_len,
        ),
    )(pre, tables)


def attend_back_kernel(
    heads_ref, table_ref, log_ref, grad_ref, out_ref, kk_ref, vv_ref, dk_ref, dv_ref
):
    seq_len, width = heads_ref.shape
    q_width = width - LANES
    pairs = q_width // LANES
    blocks = seq_len // QB
    kv = heads_ref[:, q_width:].astype(F32)
    other = pltpu.roll(kv, HD, 1)
    kk_ref[...] = both(kv, other).astype(BF)
    vv_ref[...] = both(other, kv).astype(BF)
    dk_ref[...] = jnp.zeros_like(dk_ref)
    dv_ref[...] = jnp.zeros_like(dv_ref)
    for i in range(blocks):
        rows = pl.ds(i * QB, QB)
        seen = (i + 1) * QB

        def pair_step(j, carry):
            cols = pl.ds(pl.multiple_of(j * LANES, LANES), LANES)
            q = two_heads(heads_ref[rows, cols])
            grad = two_heads(grad_ref[rows, cols])
            lane = lax.broadcasted_iota(jnp.int32, (QB, LANES), 1)
            logs = log_ref[rows]
            log_col = jnp.concatenate(
                [
                    jnp.sum(jnp.where(lane == 2 * j + n, logs, 0.0), -1, keepdims=True)
                    for n in (0, 1)
                ],
                axis=0,
            )
            scores = matmul_right_t(q, kk_ref[:seen])
            soft = jnp.exp(causal_mask(scores, i * QB) - log_col)
            grad_soft = matmul_right_t(grad, vv_ref[:seen])
            inner = jnp.sum(soft * grad_soft, axis=-1, keepdims=True)
            grad_scores = (soft * (grad_soft - inner)).astype(BF)
            dq = matmul(grad_scores, kk_ref[:seen])
            dq = both(dq[:QB], dq[QB:]) * HD**-0.5
            dq = dq * table_ref[0, rows] - turned(dq) * table_ref[1, rows]
            out_ref[rows, cols] = dq.astype(BF)
            dk_ref[:seen] += matmul_left_t(grad_scores, q)
            dv_ref[:seen] += matmul_left_t(soft.astype(BF), grad)
            return carry

        lax.fori_loop(0, pairs, pair_step, 0)
    dk, dv = dk_ref[...], dv_ref[...]
    dk, dv = dk + pltpu.roll(dk, HD, 1), dv + pltpu.roll(dv, HD, 1)
    dkv = both(dk, dv)
    dkv = dkv * table_ref[2] - turned(dkv) * table_ref[3]
    out_ref[:, q_width:] = dkv.astype(BF)


def attend_back(heads, tables, logs, grad_mixed):
    seq_len, width = heads.shape
    return pl.pallas_call(
        attend_back_kernel,
        out_shape=jax.ShapeDtypeStruct((seq_len, width), BF),
        scratch_shapes=[
            pltpu.VMEM((seq_len, LANES), BF),
            pltpu.VMEM((seq_len, LANES), BF),
            pltpu.VMEM((seq_len, LANES), F32),
            pltpu.VMEM((seq_len, LANES), F32),
        ],
        compiler_params=pltpu.CompilerParams(vmem_limit_bytes=48 * 2**20),
        cost_estimate=pl.CostEstimate(
            flops=5 * 2 * 8 * seq_len * seq_len * HD,
            bytes_accessed=8 * seq_len * width,
            transcendentals=4 * seq_len * seq_len,
        ),
    )(heads, tables, logs, grad_mixed)


MESH_ID = pl.DeviceIdType.MESH
ANY = pl.BlockSpec(memory_space=pl.ANY)
VMEM = pl.BlockSpec(memory_space=pltpu.VMEM)


class Links:
    def __init__(self, shard, replica, send, recv, local):
        self.shard, self.replica = shard, replica
        self.send, self.recv, self.local = send, recv, local
        self.used, self.used_local = 0, 0
        self.open = []

    def to(self, source, target, shard=0, replica=0):
        n, self.used = self.used, self.used + 1
        copy = pltpu.make_async_remote_copy(
            src_ref=source,
            dst_ref=target,
            send_sem=self.send.at[n],
            recv_sem=self.recv.at[n],
            device_id={
                "shard": self.shard ^ shard,
                "replica": self.replica ^ replica,
            },
            device_id_type=MESH_ID,
        )
        copy.start()
        self.open.append(copy)
        return copy

    def here(self, source, target):
        n, self.used_local = self.used_local, self.used_local + 1
        copy = pltpu.make_async_copy(source, target, self.local.at[n])
        copy.start()
        return copy

    def close(self):
        for copy in self.open:
            copy.wait_send()


def greet(shard, replica, shard_masks, replica_masks):
    barrier = pltpu.get_barrier_semaphore()
    for mask in shard_masks:
        pl.semaphore_signal(
            barrier,
            inc=1,
            device_id={"shard": shard ^ mask, "replica": replica},
            device_id_type=MESH_ID,
        )
    for mask in replica_masks:
        pl.semaphore_signal(
            barrier,
            inc=1,
            device_id={"shard": shard, "replica": replica ^ mask},
            device_id_type=MESH_ID,
        )
    pl.semaphore_wait(barrier, len(shard_masks) + len(replica_masks))


def norm_rows(source, target, gains, which, start, count):
    model = source.shape[1]
    part = model // S

    def step(i, carry):
        rows = pl.ds(pl.multiple_of(start + i * 16, 16), 16)
        values = source[rows, :].astype(F32)
        scale = rms_scale(values)
        for j in range(S):
            gain = gains[j, which : which + 1, :].astype(F32)
            cols = slice(j * part, (j + 1) * part)
            target[rows, cols] = (values[:, cols] * scale * gain).astype(BF)
        return carry

    lax.fori_loop(0, count // 16, step, 0, unroll=2)


def front_kernel(
    x_ref, cot_ref, gain_ref, wq_ref, wk_ref, wv_ref, wo_ref, gate_ref, up_ref, table_ref,
    norm1_ref, heads_ref, log_ref, mixed_ref, w_heads_ref, mid_ref, norm2_ref, w_ff_ref, cot_all_ref,
    x_all, gains, kv_parts, near_q, near_kv, near_gate, near_up, w_heads, norm1, pre, kk_ref, vv_ref,
    far_out, far_in, across_out, across_in, beside_out, beside_in, term, norm2, send, recv, local,
):
    shard, replica = lax.axis_index("shard"), lax.axis_index("replica")
    x, core, quarter = shard // 2, shard % 2, replica % 4
    tokens, model = x_ref.shape
    seq_len = S * tokens
    rows = wq_ref.shape[0]
    q_cols, ff_cols = wq_ref.shape[1] // S, gate_ref.shape[1] // S
    width = q_cols + LANES
    q_rows, half = rows // 4, tokens // 2
    links = Links(shard, replica, send, recv, local)

    def lanes(index, size):
        return pl.ds(pl.multiple_of(index * size, LANES), size)

    def block(index, size=tokens, extra=0):
        return pl.ds(pl.multiple_of(index * size + extra, 16), size)

    for j in range(S):
        keys = wk_ref[:, j // 2 * LANES : (j // 2 + 1) * LANES].astype(F32)
        vals = wv_ref[:, j // 2 * LANES : (j // 2 + 1) * LANES].astype(F32)
        if j % 2 == 0:
            pair = both(keys, pltpu.roll(vals, HD, 1))
        else:
            pair = both(pltpu.roll(keys, HD, 1), vals)
        kv_parts[j] = pair.astype(BF)

    greet(shard, replica, (1, 2, 3), (1, 2))

    mine = pl.ds(pl.multiple_of(quarter * q_rows, q_rows), q_rows)
    other_chip = 1 - x
    across_q = links.to(wq_ref.at[mine, lanes(other_chip, 2 * q_cols)], near_q, 2)
    across_kv = links.to(kv_parts.at[pl.ds(2 * other_chip, 2), mine], near_kv, 2)
    gain_copies = [links.to(gain_ref, gains.at[shard], m) for m in (1, 2, 3)]
    own_rows = [
        pl.ds(pl.multiple_of(shard * tokens + i * half, half), half) for i in range(2)
    ]
    x_across = [
        links.to(x_ref.at[pl.ds(i * half, half)], x_all.at[own_rows[i]], 2)
        for i in range(2)
    ]
    x_beside = links.to(x_ref, x_all.at[block(shard)], 1)
    own_w = pl.ds(pl.multiple_of(shard * rows, rows), rows)
    pair_shard = shard ^ 1
    w_beside = [
        links.to(
            wq_ref.at[:, lanes(pair_shard, q_cols)], w_heads.at[own_w, :q_cols], 1
        ),
        links.to(kv_parts.at[pair_shard], w_heads.at[own_w, q_cols:], 1),
    ]
    here = [
        links.here(x_ref, x_all.at[block(shard)]),
        links.here(gain_ref, gains.at[shard]),
        links.here(wq_ref.at[:, lanes(shard, q_cols)], w_heads.at[own_w, :q_cols]),
        links.here(kv_parts.at[shard], w_heads.at[own_w, q_cols:]),
    ]
    here_late = [
        links.here(gate_ref.at[:, lanes(shard, ff_cols)], w_ff_ref.at[own_w, :ff_cols]),
        links.here(up_ref.at[:, lanes(shard, ff_cols)], w_ff_ref.at[own_w, ff_cols:]),
        links.here(cot_ref, cot_all_ref.at[block(shard)]),
    ]

    def rows_from(mask, of):
        return pl.ds(
            pl.multiple_of((shard ^ mask) * rows + (quarter ^ of) * q_rows, q_rows),
            q_rows,
        )

    across_q.wait_recv()
    across_kv.wait_recv()
    near_rows, far_rows = rows_from(2, 0), rows_from(3, 0)
    pair_lanes = lanes(1 - core, q_cols)
    core_q = links.to(near_q.at[:, pair_lanes], w_heads.at[near_rows, :q_cols], 1)
    core_kv = links.to(near_kv.at[1 - core], w_heads.at[near_rows, q_cols:], 1)
    near_copies = [
        links.here(near_q.at[:, lanes(core, q_cols)], w_heads.at[near_rows, :q_cols]),
        links.here(near_kv.at[core], w_heads.at[near_rows, q_cols:]),
    ]
    for copy in near_copies:
        copy.wait()
    y_near, z_near = (
        links.to(w_heads.at[near_rows], w_heads.at[near_rows], 0, m) for m in (1, 2)
    )
    core_q.wait_recv()
    core_kv.wait_recv()
    y_far, z_far = (
        links.to(w_heads.at[far_rows], w_heads.at[far_rows], 0, m) for m in (1, 2)
    )
    ff_across = [
        links.to(ref.at[mine, lanes(other_chip, 2 * ff_cols)], near, 2)
        for ref, near in ((gate_ref, near_gate), (up_ref, near_up))
    ]

    for copy in here:
        copy.wait()
    for copy in gain_copies:
        copy.wait_recv()
    norm_rows(x_all, norm1, gains, 0, shard * tokens, tokens)
    x_beside.wait_recv()
    norm_rows(x_all, norm1, gains, 0, (shard ^ 1) * tokens, tokens)

    y_near.wait_recv()
    y_far.wait_recv()
    z_forward = [
        links.to(w_heads.at[r], w_heads.at[r], 0, 2)
        for r in (rows_from(2, 1), rows_from(3, 1))
    ]
    x_core = []
    for i in range(2):
        x_across[i].wait_recv()
        got = pl.ds(pl.multiple_of((shard ^ 2) * tokens + i * half, half), half)
        x_core.append(links.to(x_all.at[got], x_all.at[got], 1))
        norm_rows(x_all, norm1, gains, 0, (shard ^ 2) * tokens + i * half, half)
    for i in range(2):
        x_core[i].wait_recv()
        norm_rows(x_all, norm1, gains, 0, (shard ^ 3) * tokens + i * half, half)
    norm1_out = links.here(norm1, norm1_ref)
    w_beside_ff = [
        links.to(ref.at[:, lanes(pair_shard, ff_cols)], w_ff_ref.at[own_w, cols], 1)
        for ref, cols in (
            (gate_ref, slice(0, ff_cols)),
            (up_ref, slice(ff_cols, 2 * ff_cols)),
        )
    ]
    cot_beside = links.to(cot_ref, cot_all_ref.at[block(shard)], 1)

    for copy in w_beside + [z_near, z_far] + z_forward:
        copy.wait_recv()
    w_heads_out = links.here(w_heads, w_heads_ref)

    def project(b, carry):
        r = pl.ds(pl.multiple_of(b * tokens, tokens), tokens)
        pre[r, :] = matmul(norm1[r, :], w_heads[...])
        return carry

    lax.fori_loop(0, S, project, 0)

    for copy in ff_across:
        copy.wait_recv()
    pair_ff = lanes(1 - core, ff_cols)
    ff_parts = ((near_gate, slice(0, ff_cols)), (near_up, slice(ff_cols, 2 * ff_cols)))
    ff_core = [
        links.to(near.at[:, pair_ff], w_ff_ref.at[near_rows, cols], 1)
        for near, cols in ff_parts
    ]
    ff_here = [
        links.here(near.at[:, lanes(core, ff_cols)], w_ff_ref.at[near_rows, cols])
        for near, cols in ff_parts
    ]
    cot_across = links.to(cot_ref, cot_all_ref.at[block(shard)], 2)

    kv = pre[:, q_cols:]
    kv = (kv * table_ref[2] + turned(kv) * table_ref[3]).astype(BF)
    heads_ref[:, q_cols:] = kv
    kv = kv.astype(F32)
    swapped = pltpu.roll(kv, HD, 1)
    kk_ref[...] = both(kv, swapped).astype(BF)
    vv_ref[...] = both(swapped, kv).astype(BF)
    log_ref[...] = jnp.zeros_like(log_ref)

    for copy in ff_here:
        copy.wait()
    ff_y = [links.to(w_ff_ref.at[near_rows], w_ff_ref.at[near_rows], 0, 1)]
    ff_z = [links.to(w_ff_ref.at[near_rows], w_ff_ref.at[near_rows], 0, 2)]
    for copy in ff_core:
        copy.wait_recv()
    ff_y.append(links.to(w_ff_ref.at[far_rows], w_ff_ref.at[far_rows], 0, 1))
    ff_z.append(links.to(w_ff_ref.at[far_rows], w_ff_ref.at[far_rows], 0, 2))

    def attend_rows(i):
        q_rows_i = slice(i * tokens, (i + 1) * tokens)
        seen = (i + 1) * tokens

        def pair_step(j, carry):
            cols = pl.ds(pl.multiple_of(j * LANES, LANES), LANES)
            q = pre[q_rows_i, cols]
            q = q * table_ref[0, q_rows_i] + turned(q) * table_ref[1, q_rows_i]
            q = (q.astype(BF).astype(F32) * HD**-0.5).astype(BF)
            heads_ref[q_rows_i, cols] = q
            scores = matmul_right_t(two_heads(q), kk_ref[:seen])
            scores = causal_mask(scores, i * tokens)
            peak = jnp.max(scores, axis=-1, keepdims=True)
            exps = jnp.exp(scores - peak)
            total = jnp.sum(exps, axis=-1, keepdims=True)
            out = matmul(exps.astype(BF), vv_ref[:seen]) / total
            mixed_ref[q_rows_i, cols] = both(out[:tokens], out[tokens:]).astype(BF)
            logs = peak + jnp.log(total)
            lane = lax.broadcasted_iota(jnp.int32, (tokens, LANES), 1)
            old = log_ref[q_rows_i]
            old = jnp.where(lane == 2 * j, logs[:tokens], old)
            log_ref[q_rows_i] = jnp.where(lane == 2 * j + 1, logs[tokens:], old)
            return carry

        lax.fori_loop(0, q_cols // LANES, pair_step, 0)

    def out_term(index):
        r = block(index)

        def step(j, carry):
            cols = pl.ds(pl.multiple_of(j * 512, 512), 512)
            term[:, cols] = matmul(mixed_ref[r, :], wo_ref[:, cols])
            return carry

        lax.fori_loop(0, model // 512, step, 0)

    def attend_block(index):
        for i in range(S):
            pl.when(index == i)(functools.partial(attend_rows, i))

    attend_block(shard ^ 3)
    out_term(shard ^ 3)
    far_out[...] = term[...].astype(BF)
    far = links.to(far_out, far_in, 1)
    attend_block(shard ^ 2)
    out_term(shard ^ 2)
    far.wait_recv()
    across = []
    for i in range(2):
        r = slice(i * half, (i + 1) * half)
        across_out[r] = (term[r] + far_in[r].astype(F32)).astype(BF)
        across.append(links.to(across_out.at[r], across_in.at[r], 2))
    attend_block(shard ^ 1)
    out_term(shard ^ 1)
    beside_out[...] = term[...].astype(BF)
    beside = links.to(beside_out, beside_in, 1)
    for copy in ff_y:
        copy.wait_recv()
    ff_forward = [
        links.to(w_ff_ref.at[r], w_ff_ref.at[r], 0, 2)
        for r in (rows_from(2, 1), rows_from(3, 1))
    ]
    attend_block(shard)
    out_term(shard)
    beside.wait_recv()
    term[...] += x_ref[...].astype(F32) + beside_in[...].astype(F32)
    n2_across, n2_beside, n2_here = [], [], []
    for i in range(2):
        r = slice(i * half, (i + 1) * half)
        across[i].wait_recv()
        mid_ref[r] = term[r] + across_in[r].astype(F32)
        norm_rows(mid_ref, norm2, gains, 1, i * half, half)
        n2_across.append(links.to(norm2.at[r], norm2_ref.at[own_rows[i]], 2))
        n2_beside.append(links.to(norm2.at[r], norm2_ref.at[own_rows[i]], 1))
        n2_here.append(links.here(norm2.at[r], norm2_ref.at[own_rows[i]]))
    n2_core = []
    for i in range(2):
        n2_across[i].wait_recv()
        got = pl.ds(pl.multiple_of((shard ^ 2) * tokens + i * half, half), half)
        n2_core.append(links.to(norm2_ref.at[got], norm2_ref.at[got], 1))
    cot_across.wait_recv()
    got = block(shard ^ 2)
    cot_core = links.to(cot_all_ref.at[got], cot_all_ref.at[got], 1)
    for copy in (
        w_beside_ff + [cot_beside] + ff_z + ff_forward + n2_beside + n2_core + [cot_core]
    ):
        copy.wait_recv()
    for copy in here_late + n2_here + [norm1_out, w_heads_out]:
        copy.wait()
    links.close()


def front(x, cot, gains, wq, wk, wv, wo, gate, up, tables):
    tokens, model = x.shape
    seq_len, rows = S * tokens, wq.shape[0]
    q_cols, ff_cols = wq.shape[1] // S, gate.shape[1] // S
    width, q_rows = q_cols + LANES, rows // 4
    shape = jax.ShapeDtypeStruct
    chip_ff = (q_rows, 2 * ff_cols)
    row_block = pltpu.VMEM((tokens, model), BF)
    return pl.pallas_call(
        front_kernel,
        out_shape=(
            shape((seq_len, model), BF),
            shape((seq_len, width), BF),
            shape((seq_len, LANES), F32),
            shape((seq_len, q_cols), BF),
            shape((S * rows, width), BF),
            shape((tokens, model), F32),
            shape((seq_len, model), BF),
            shape((S * rows, 2 * ff_cols), BF),
            shape((seq_len, model), BF),
        ),
        in_specs=[VMEM, ANY, VMEM, ANY, VMEM, VMEM, VMEM, ANY, ANY, VMEM],
        out_specs=[ANY, VMEM, VMEM, VMEM, ANY, VMEM, ANY, ANY, ANY],
        scratch_shapes=[
            pltpu.VMEM((seq_len, model), BF),
            pltpu.VMEM((S, 16, rows), BF),
            pltpu.VMEM((S, rows, LANES), BF),
            pltpu.VMEM((q_rows, 2 * q_cols), BF),
            pltpu.VMEM((2, q_rows, LANES), BF),
            pltpu.VMEM(chip_ff, BF),
            pltpu.VMEM(chip_ff, BF),
            pltpu.VMEM((S * rows, width), BF),
            pltpu.VMEM((seq_len, model), BF),
            pltpu.VMEM((seq_len, width), F32),
            pltpu.VMEM((seq_len, LANES), BF),
            pltpu.VMEM((seq_len, LANES), BF),
            row_block,
            row_block,
            row_block,
            row_block,
            row_block,
            row_block,
            pltpu.VMEM((tokens, model), F32),
            row_block,
            pltpu.SemaphoreType.DMA((48,)),
            pltpu.SemaphoreType.DMA((48,)),
            pltpu.SemaphoreType.DMA((24,)),
        ],
        compiler_params=pltpu.CompilerParams(
            collective_id=0, has_side_effects=True, vmem_limit_bytes=60 * 2**20
        ),
    )(x, cot, gains, wq, wk, wv, wo, gate, up, tables)


def on_device(
    inputs, cotangent, gain_attn, w_query, w_key, w_value, w_output, gain_mlp, w_gate, w_up, w_down
):
    shard, replica = lax.axis_index("shard"), lax.axis_index("replica")
    replicas = lax.axis_size("replica")
    tokens, model = inputs.shape[1:]
    seq_len = tokens * S
    rows = w_query.shape[0]
    q_cols, kv_cols = w_query.shape[1] // S, w_key.shape[1] // S
    ff_cols = w_gate.shape[1] // S
    tables = jnp.asarray(rope_tables(seq_len))

    def rows_of(array, index):
        return lax.dynamic_slice_in_dim(array, index * tokens, tokens, 0)

    own = inputs[0]
    resid = own.astype(F32)
    gains = jnp.concatenate(
        [jnp.stack([gain_attn, gain_mlp]), jnp.zeros((14, rows), BF)]
    )
    norm1, heads, logs, mixed, w_heads, middle, norm2, w_ff, grad_out = front(
        own, cotangent[0], gains, w_query, w_key, w_value, w_output, w_gate, w_up, tables
    )
    scale_two = rms_scale(middle)
    gains = gather(gains, shard)
    gain_one, gain_two = (
        gains[:, i].reshape(model).astype(F32) for i in range(2)
    )
    gate_up = matmul(norm2, w_ff)
    gate, up_proj = gate_up[:, :ff_cols], gate_up[:, ff_cols:]
    sigmoid_gate = jax.nn.sigmoid(gate)
    silu_gate = gate * sigmoid_gate
    hidden = (silu_gate * up_proj).astype(BF)
    grad_hidden = matmul_right_t(grad_out, w_down)
    grad_gate = grad_hidden * up_proj * sigmoid_gate * (1.0 + gate * (1.0 - sigmoid_gate))
    grad_ff = jnp.concatenate(
        [grad_gate.astype(BF), (grad_hidden * silu_gate).astype(BF)], axis=1
    )
    term_down = matmul_left_t(hidden, grad_out).astype(BF)
    piece_down = replica_scatter(
        term_down.reshape(1, replicas, -1, model), replica, (1, 0, 2)
    ).reshape(-1, model)
    grad_norm2 = scatter_blocks(
        lambda j: matmul_right_t(rows_of(grad_ff, j), w_ff), shard
    )
    term_ff = matmul_left_t(norm2, grad_ff).astype(BF)
    piece_ff = replica_scatter(
        term_ff.reshape(S, replicas, -1, 2 * ff_cols), replica, (0, 1, 2)
    )
    output = middle + scatter_blocks(
        lambda j: matmul(rows_of(hidden, j), w_down), shard
    )
    output = output.astype(BF)[None]

    grad_middle_norm = norm_back(grad_norm2, middle, scale_two, gain_two)
    grad_middle = cotangent[0].astype(F32) + grad_middle_norm
    grad_middle_all = gather(grad_middle.astype(BF), shard).reshape(seq_len, model)
    grad_mixed = matmul_right_t(grad_middle_all, w_output).astype(BF)
    term_output = matmul_left_t(mixed, grad_middle_all).astype(BF)
    piece_output = replica_scatter(
        term_output.reshape(1, replicas, -1, model), replica, (0, 1, 2)
    ).reshape(-1, model)
    grad_heads = attend_back(heads, tables, logs, grad_mixed)
    term_heads = matmul_left_t(norm1, grad_heads).astype(BF)
    piece_heads = replica_scatter(
        term_heads.reshape(S, replicas, -1, grad_heads.shape[1]), replica, (0, 1, 2)
    )
    grad_norm1 = scatter_blocks(
        lambda j: matmul_right_t(rows_of(grad_heads, j), w_heads), shard
    )
    grad_resid_norm = norm_back(
        grad_norm1, resid, rms_scale(resid), gain_one
    )
    input_grad = (grad_middle + grad_resid_norm).astype(BF)[None]

    (grad_gate_own, grad_up_own), grad_gain_two = finish(
        exchange(piece_ff.astype(BF), shard), (w_gate, w_up), gain_mlp, shard, replica
    )
    (grad_query, grad_key, grad_value), grad_gain_one = finish(
        exchange(piece_heads.astype(BF), shard),
        (w_query, w_key, w_value),
        gain_attn,
        shard,
        replica,
    )
    return (
        output,
        input_grad,
        grad_gain_one,
        grad_query,
        grad_key,
        grad_value,
        piece_output,
        grad_gain_two,
        grad_gate_own,
        grad_up_own,
        piece_down,
    )


def solution(mesh):
    placed = (
        P("replica", "shard", None),
        P("replica", "shard", None),
        P("shard"),
        P("shard", None),
        P("shard", None),
        P("shard", None),
        P("shard", None),
        P("shard"),
        P("shard", None),
        P("shard", None),
        P("shard", None),
    )
    both_axes = ("shard", "replica")
    return jax.shard_map(
        on_device,
        mesh=mesh,
        in_specs=placed,
        out_specs=(
            P("replica", "shard", None),
            P("replica", "shard", None),
            P(both_axes),
            P(both_axes, None),
            P(both_axes, None),
            P(both_axes, None),
            P(both_axes, None),
            P(both_axes),
            P(both_axes, None),
            P(both_axes, None),
            P(both_axes, None),
        ),
        check_vma=False,
    )
```

```python
import functools
import itertools

import jax
import jax.numpy as jnp
import numpy as np
from jax import lax
from jax.experimental import pallas as pl
from jax.experimental.pallas import tpu as pltpu
from jax.sharding import PartitionSpec as P

H = 32
KV = 4
HD = 64
EPS = 1e-05
THETA = 10000.0
S = 4
BF = jnp.bfloat16
F32 = jnp.float32
LANES = 128
QB = 256


def matmul(left, right):
    return jnp.dot(left, right, preferred_element_type=F32)


def matmul_left_t(left, right):
    return lax.dot_general(
        left, right, (((0,), (0,)), ((), ())), preferred_element_type=F32
    )


def matmul_right_t(left, right):
    return lax.dot_general(
        left, right, (((1,), (1,)), ((), ())), preferred_element_type=F32
    )


def rms_scale(values):
    return lax.rsqrt(jnp.mean(values * values, axis=-1, keepdims=True) + EPS)


def finish_kernel(widths, shard_ref, *refs):
    pieces, rest = refs[0], refs[1:]
    weights, gain_ref = rest[: len(widths)], rest[len(widths)]
    outs, gain_out = rest[len(widths) + 1 : -1], rest[-1]
    shard = shard_ref[0]
    total = jnp.zeros(gain_out.shape, F32)
    for mask in range(S):
        piece = pieces.at[mask]
        owner = shard ^ mask
        start = 0
        for width, weight, out in zip(widths, weights, outs):
            if width % LANES == 0:
                cols = pl.ds(pl.multiple_of(owner * width, LANES), width)
                part = piece[:, start : start + width].astype(F32)
                out[:, cols] = part
                total += jnp.sum(
                    part * weight[:, cols].astype(F32), axis=1, keepdims=True
                )
            else:
                base = start // LANES * LANES
                part = piece[:, base : base + LANES].astype(F32)
                lane = lax.broadcasted_iota(jnp.int32, part.shape, 1) // HD
                turned_part = pltpu.roll(part, HD, 1)
                side = owner % 2
                part = jnp.where(side == (start - base) // HD, part, turned_part)
                part = jnp.where(lane == side, part, 0.0)
                cols = pl.ds(pl.multiple_of(owner // 2 * LANES, LANES), LANES)
                out[:, cols] = jnp.where(lane == side, part, out[:, cols])
                total += jnp.sum(
                    part * weight[:, cols].astype(F32), axis=1, keepdims=True
                )
            start += width
    gain_out[...] = total / gain_ref[...]


def finish(pieces, weights, gain, shard, replica):
    rows = pieces.shape[1]
    widths = tuple(w.shape[1] // S for w in weights)
    own = [lax.dynamic_slice_in_dim(w, replica * rows, rows, 0) for w in weights]
    own_gain = lax.dynamic_slice_in_dim(gain, replica * rows, rows, 0)
    vmem = pl.BlockSpec(memory_space=pltpu.VMEM)
    result = pl.pallas_call(
        functools.partial(finish_kernel, widths),
        out_shape=[jax.ShapeDtypeStruct(w.shape, F32) for w in own]
        + [jax.ShapeDtypeStruct((rows, 1), F32)],
        in_specs=[pl.BlockSpec(memory_space=pltpu.SMEM)]
        + [vmem] * (len(weights) + 2),
        out_specs=[vmem] * (len(weights) + 1),
        compiler_params=pltpu.CompilerParams(vmem_limit_bytes=32 * 2**20),
    )(
        shard.reshape(1).astype(jnp.int32),
        pieces,
        *own,
        own_gain.astype(F32).reshape(rows, 1),
    )
    return result[:-1], result[-1].reshape(rows)


def rope_tables(seq_len):
    half = HD // 2
    freq = THETA ** (-2.0 * np.arange(half, dtype=np.float64) / HD)
    angles = np.arange(seq_len, dtype=np.float64)[:, None] * freq[None, :]
    cos, sin = np.cos(angles), np.sin(angles)
    one, zero = np.ones((seq_len, HD)), np.zeros((seq_len, HD))
    cos_head = np.concatenate([cos, cos], 1)
    sin_head = np.concatenate([-sin, sin], 1)
    tables = [
        np.concatenate([cos_head, cos_head], 1),
        np.concatenate([sin_head, sin_head], 1),
        np.concatenate([cos_head, one], 1),
        np.concatenate([sin_head, zero], 1),
    ]
    return np.stack(tables).astype(np.float32)


def turned(values):
    lane = lax.broadcasted_iota(jnp.int32, values.shape, 1)
    return jnp.where(
        lane % HD < HD // 2,
        pltpu.roll(values, LANES - HD // 2, 1),
        pltpu.roll(values, HD // 2, 1),
    )


def both(first, second):
    lane = lax.broadcasted_iota(jnp.int32, first.shape, 1)
    return jnp.where(lane < HD, first, second)


def two_heads(pair):
    zero = jnp.zeros_like(pair)
    return jnp.concatenate([both(pair, zero), both(zero, pair)], axis=0)


def causal_mask(scores, first_row):
    rows, cols = scores.shape
    row = lax.broadcasted_iota(jnp.int32, scores.shape, 0) % QB + first_row
    col = lax.broadcasted_iota(jnp.int32, scores.shape, 1)
    return jnp.where(col <= row, scores, -1e30)


MESH_ID = pl.DeviceIdType.MESH
ANY = pl.BlockSpec(memory_space=pl.ANY)
VMEM = pl.BlockSpec(memory_space=pltpu.VMEM)


class Copy:
    def __init__(self, describe):
        self.describe = describe
        describe().start()

    def wait(self):
        self.describe().wait()

    def wait_recv(self):
        self.describe().wait_recv()

    def wait_send(self):
        self.describe().wait_send()


class Links:
    def __init__(self, shard, replica, send, recv, local):
        self.shard, self.replica = shard, replica
        self.send, self.recv, self.local = send, recv, local
        self.used, self.used_local = 0, 0
        self.open = []

    def to(self, source, target, shard=0, replica=0):
        n, self.used = self.used, self.used + 1
        copy = Copy(
            lambda: pltpu.make_async_remote_copy(
                src_ref=source,
                dst_ref=target,
                send_sem=self.send.at[n],
                recv_sem=self.recv.at[n],
                device_id={
                    "shard": self.shard ^ shard,
                    "replica": self.replica ^ replica,
                },
                device_id_type=MESH_ID,
            )
        )
        self.open.append(copy)
        return copy

    def here(self, source, target):
        n, self.used_local = self.used_local, self.used_local + 1
        return Copy(
            lambda: pltpu.make_async_copy(source, target, self.local.at[n])
        )

    def sent(self, copy):
        copy.wait_send()
        self.open = [other for other in self.open if other is not copy]

    def close(self):
        for copy in self.open:
            copy.wait_send()


def greet(shard, replica, shard_masks, replica_masks):
    barrier = pltpu.get_barrier_semaphore()
    for mask in shard_masks:
        pl.semaphore_signal(
            barrier,
            inc=1,
            device_id={"shard": shard ^ mask, "replica": replica},
            device_id_type=MESH_ID,
        )
    for mask in replica_masks:
        pl.semaphore_signal(
            barrier,
            inc=1,
            device_id={"shard": shard, "replica": replica ^ mask},
            device_id_type=MESH_ID,
        )
    pl.semaphore_wait(barrier, len(shard_masks) + len(replica_masks))


def norm_rows(source, target, gains, which, start, count):
    model = source.shape[1]
    part = model // S

    def step(i, carry):
        rows = pl.ds(pl.multiple_of(start + i * 16, 16), 16)
        values = source[rows, :].astype(F32)
        scale = rms_scale(values)
        for j in range(S):
            gain = gains[j, which : which + 1, :].astype(F32)
            cols = slice(j * part, (j + 1) * part)
            target[rows, cols] = (values[:, cols] * scale * gain).astype(BF)
        return carry

    lax.fori_loop(0, count // 16, step, 0, unroll=2)


def front_kernel(
    x_ref, cot_ref, gain_ref, wq_ref, wk_ref, wv_ref, wo_ref, gate_ref, up_ref, table_ref,
    norm1_ref, heads_ref, log_ref, mixed_ref, w_heads_ref, mid_ref, norm2_ref, w_ff_ref, cot_all_ref, gains_ref,
    x_all, gains, kv_parts, near_q, near_kv, near_gate, near_up, w_heads, norm1, pre, kk_ref, vv_ref,
    far_out, far_in, across_out, across_in, beside_out, beside_in, term, norm2, send, recv, local,
):
    shard, replica = lax.axis_index("shard"), lax.axis_index("replica")
    x, core, quarter = shard // 2, shard % 2, replica % 4
    tokens, model = x_ref.shape
    seq_len = S * tokens
    rows = wq_ref.shape[0]
    q_cols, ff_cols = wq_ref.shape[1] // S, gate_ref.shape[1] // S
    width = q_cols + LANES
    q_rows, half = rows // 4, tokens // 2
    links = Links(shard, replica, send, recv, local)

    def lanes(index, size):
        return pl.ds(pl.multiple_of(index * size, LANES), size)

    def block(index, size=tokens, extra=0):
        return pl.ds(pl.multiple_of(index * size + extra, 16), size)

    for j in range(S):
        keys = wk_ref[:, j // 2 * LANES : (j // 2 + 1) * LANES].astype(F32)
        vals = wv_ref[:, j // 2 * LANES : (j // 2 + 1) * LANES].astype(F32)
        if j % 2 == 0:
            pair = both(keys, pltpu.roll(vals, HD, 1))
        else:
            pair = both(pltpu.roll(keys, HD, 1), vals)
        kv_parts[j] = pair.astype(BF)

    greet(shard, replica, (1, 2, 3), (1, 2))

    mine = pl.ds(pl.multiple_of(quarter * q_rows, q_rows), q_rows)
    other_chip = 1 - x
    across_q = links.to(wq_ref.at[mine, lanes(other_chip, 2 * q_cols)], near_q, 2)
    across_kv = links.to(kv_parts.at[pl.ds(2 * other_chip, 2), mine], near_kv, 2)
    gain_copies = [links.to(gain_ref, gains.at[shard], m) for m in (1, 2, 3)]
    own_rows = [
        pl.ds(pl.multiple_of(shard * tokens + i * half, half), half) for i in range(2)
    ]
    x_across = [
        links.to(x_ref.at[pl.ds(i * half, half)], x_all.at[own_rows[i]], 2)
        for i in range(2)
    ]
    x_beside = links.to(x_ref, x_all.at[block(shard)], 1)
    own_w = pl.ds(pl.multiple_of(shard * rows, rows), rows)
    pair_shard = shard ^ 1
    w_beside = [
        links.to(
            wq_ref.at[:, lanes(pair_shard, q_cols)], w_heads.at[own_w, :q_cols], 1
        ),
        links.to(kv_parts.at[pair_shard], w_heads.at[own_w, q_cols:], 1),
    ]
    here = [
        links.here(x_ref, x_all.at[block(shard)]),
        links.here(gain_ref, gains.at[shard]),
        links.here(wq_ref.at[:, lanes(shard, q_cols)], w_heads.at[own_w, :q_cols]),
        links.here(kv_parts.at[shard], w_heads.at[own_w, q_cols:]),
    ]
    here_late = [
        links.here(gate_ref.at[:, lanes(shard, ff_cols)], w_ff_ref.at[own_w, :ff_cols]),
        links.here(up_ref.at[:, lanes(shard, ff_cols)], w_ff_ref.at[own_w, ff_cols:]),
        links.here(cot_ref, cot_all_ref.at[block(shard)]),
    ]

    def rows_from(mask, of):
        return pl.ds(
            pl.multiple_of((shard ^ mask) * rows + (quarter ^ of) * q_rows, q_rows),
            q_rows,
        )

    across_q.wait_recv()
    across_kv.wait_recv()
    near_rows, far_rows = rows_from(2, 0), rows_from(3, 0)
    pair_lanes = lanes(1 - core, q_cols)
    core_q = links.to(near_q.at[:, pair_lanes], w_heads.at[near_rows, :q_cols], 1)
    core_kv = links.to(near_kv.at[1 - core], w_heads.at[near_rows, q_cols:], 1)
    near_copies = [
        links.here(near_q.at[:, lanes(core, q_cols)], w_heads.at[near_rows, :q_cols]),
        links.here(near_kv.at[core], w_heads.at[near_rows, q_cols:]),
    ]
    for copy in near_copies:
        copy.wait()
    y_near, z_near = (
        links.to(w_heads.at[near_rows], w_heads.at[near_rows], 0, m) for m in (1, 2)
    )
    core_q.wait_recv()
    core_kv.wait_recv()
    y_far, z_far = (
        links.to(w_heads.at[far_rows], w_heads.at[far_rows], 0, m) for m in (1, 2)
    )
    ff_across = [
        links.to(ref.at[mine, lanes(other_chip, 2 * ff_cols)], near, 2)
        for ref, near in ((gate_ref, near_gate), (up_ref, near_up))
    ]

    for copy in here:
        copy.wait()
    for copy in gain_copies:
        copy.wait_recv()
    gains_ref[...] = gains[...]
    norm_rows(x_all, norm1, gains, 0, shard * tokens, tokens)
    x_beside.wait_recv()
    norm_rows(x_all, norm1, gains, 0, (shard ^ 1) * tokens, tokens)

    y_near.wait_recv()
    y_far.wait_recv()
    z_forward = [
        links.to(w_heads.at[r], w_heads.at[r], 0, 2)
        for r in (rows_from(2, 1), rows_from(3, 1))
    ]
    x_core = []
    for i in range(2):
        x_across[i].wait_recv()
        got = pl.ds(pl.multiple_of((shard ^ 2) * tokens + i * half, half), half)
        x_core.append(links.to(x_all.at[got], x_all.at[got], 1))
        norm_rows(x_all, norm1, gains, 0, (shard ^ 2) * tokens + i * half, half)
    for i in range(2):
        x_core[i].wait_recv()
        norm_rows(x_all, norm1, gains, 0, (shard ^ 3) * tokens + i * half, half)
    norm1_out = links.here(norm1, norm1_ref)
    w_beside_ff = [
        links.to(ref.at[:, lanes(pair_shard, ff_cols)], w_ff_ref.at[own_w, cols], 1)
        for ref, cols in (
            (gate_ref, slice(0, ff_cols)),
            (up_ref, slice(ff_cols, 2 * ff_cols)),
        )
    ]
    cot_beside = links.to(cot_ref, cot_all_ref.at[block(shard)], 1)

    for copy in w_beside + [z_near, z_far] + z_forward:
        copy.wait_recv()
    w_heads_out = links.here(w_heads, w_heads_ref)

    def project(b, carry):
        r = pl.ds(pl.multiple_of(b * tokens, tokens), tokens)
        pre[r, :] = matmul(norm1[r, :], w_heads[...])
        return carry

    lax.fori_loop(0, S, project, 0)

    for copy in ff_across:
        copy.wait_recv()
    pair_ff = lanes(1 - core, ff_cols)
    ff_parts = ((near_gate, slice(0, ff_cols)), (near_up, slice(ff_cols, 2 * ff_cols)))
    ff_core = [
        links.to(near.at[:, pair_ff], w_ff_ref.at[near_rows, cols], 1)
        for near, cols in ff_parts
    ]
    ff_here = [
        links.here(near.at[:, lanes(core, ff_cols)], w_ff_ref.at[near_rows, cols])
        for near, cols in ff_parts
    ]
    cot_across = links.to(cot_ref, cot_all_ref.at[block(shard)], 2)

    kv = pre[:, q_cols:]
    kv = (kv * table_ref[2] + turned(kv) * table_ref[3]).astype(BF)
    heads_ref[:, q_cols:] = kv
    kv = kv.astype(F32)
    swapped = pltpu.roll(kv, HD, 1)
    kk_ref[...] = both(kv, swapped).astype(BF)
    vv_ref[...] = both(swapped, kv).astype(BF)
    log_ref[...] = jnp.zeros_like(log_ref)

    for copy in ff_here:
        copy.wait()
    ff_y = [links.to(w_ff_ref.at[near_rows], w_ff_ref.at[near_rows], 0, 1)]
    ff_z = [links.to(w_ff_ref.at[near_rows], w_ff_ref.at[near_rows], 0, 2)]
    for copy in ff_core:
        copy.wait_recv()
    ff_y.append(links.to(w_ff_ref.at[far_rows], w_ff_ref.at[far_rows], 0, 1))
    ff_z.append(links.to(w_ff_ref.at[far_rows], w_ff_ref.at[far_rows], 0, 2))

    def attend_rows(i):
        q_rows_i = slice(i * tokens, (i + 1) * tokens)
        seen = (i + 1) * tokens

        def pair_step(j, carry):
            cols = pl.ds(pl.multiple_of(j * LANES, LANES), LANES)
            q = pre[q_rows_i, cols]
            q = q * table_ref[0, q_rows_i] + turned(q) * table_ref[1, q_rows_i]
            q = (q.astype(BF).astype(F32) * HD**-0.5).astype(BF)
            heads_ref[q_rows_i, cols] = q
            scores = matmul_right_t(two_heads(q), kk_ref[:seen])
            scores = causal_mask(scores, i * tokens)
            peak = jnp.max(scores, axis=-1, keepdims=True)
            exps = jnp.exp(scores - peak)
            total = jnp.sum(exps, axis=-1, keepdims=True)
            out = matmul(exps.astype(BF), vv_ref[:seen]) / total
            mixed_ref[q_rows_i, cols] = both(out[:tokens], out[tokens:]).astype(BF)
            logs = peak + jnp.log(total)
            lane = lax.broadcasted_iota(jnp.int32, (tokens, LANES), 1)
            old = log_ref[q_rows_i]
            old = jnp.where(lane == 2 * j, logs[:tokens], old)
            log_ref[q_rows_i] = jnp.where(lane == 2 * j + 1, logs[tokens:], old)
            return carry

        lax.fori_loop(0, q_cols // LANES, pair_step, 0)

    def out_term(index):
        r = block(index)

        def step(j, carry):
            cols = pl.ds(pl.multiple_of(j * 512, 512), 512)
            term[:, cols] = matmul(mixed_ref[r, :], wo_ref[:, cols])
            return carry

        lax.fori_loop(0, model // 512, step, 0)

    def attend_block(index):
        for i in range(S):
            pl.when(index == i)(functools.partial(attend_rows, i))

    attend_block(shard ^ 3)
    out_term(shard ^ 3)
    far_out[...] = term[...].astype(BF)
    far = links.to(far_out, far_in, 1)
    attend_block(shard ^ 2)
    out_term(shard ^ 2)
    far.wait_recv()
    across = []
    for i in range(2):
        r = slice(i * half, (i + 1) * half)
        across_out[r] = (term[r] + far_in[r].astype(F32)).astype(BF)
        across.append(links.to(across_out.at[r], across_in.at[r], 2))
    attend_block(shard ^ 1)
    out_term(shard ^ 1)
    beside_out[...] = term[...].astype(BF)
    beside = links.to(beside_out, beside_in, 1)
    for copy in ff_y:
        copy.wait_recv()
    ff_forward = [
        links.to(w_ff_ref.at[r], w_ff_ref.at[r], 0, 2)
        for r in (rows_from(2, 1), rows_from(3, 1))
    ]
    attend_block(shard)
    out_term(shard)
    beside.wait_recv()
    term[...] += x_ref[...].astype(F32) + beside_in[...].astype(F32)
    n2_across, n2_beside, n2_here = [], [], []
    for i in range(2):
        r = slice(i * half, (i + 1) * half)
        across[i].wait_recv()
        mid_ref[r] = term[r] + across_in[r].astype(F32)
        norm_rows(mid_ref, norm2, gains, 1, i * half, half)
        n2_across.append(links.to(norm2.at[r], norm2_ref.at[own_rows[i]], 2))
        n2_beside.append(links.to(norm2.at[r], norm2_ref.at[own_rows[i]], 1))
        n2_here.append(links.here(norm2.at[r], norm2_ref.at[own_rows[i]]))
    n2_core = []
    for i in range(2):
        n2_across[i].wait_recv()
        got = pl.ds(pl.multiple_of((shard ^ 2) * tokens + i * half, half), half)
        n2_core.append(links.to(norm2_ref.at[got], norm2_ref.at[got], 1))
    cot_across.wait_recv()
    got = block(shard ^ 2)
    cot_core = links.to(cot_all_ref.at[got], cot_all_ref.at[got], 1)
    for copy in (
        w_beside_ff + [cot_beside] + ff_z + ff_forward + n2_beside + n2_core + [cot_core]
    ):
        copy.wait_recv()
    for copy in here_late + n2_here + [norm1_out, w_heads_out]:
        copy.wait()
    links.close()


def front(x, cot, gains, wq, wk, wv, wo, gate, up, tables):
    tokens, model = x.shape
    seq_len, rows = S * tokens, wq.shape[0]
    q_cols, ff_cols = wq.shape[1] // S, gate.shape[1] // S
    width, q_rows = q_cols + LANES, rows // 4
    shape = jax.ShapeDtypeStruct
    chip_ff = (q_rows, 2 * ff_cols)
    row_block = pltpu.VMEM((tokens, model), BF)
    return pl.pallas_call(
        front_kernel,
        out_shape=(
            shape((seq_len, model), BF),
            shape((seq_len, width), BF),
            shape((seq_len, LANES), F32),
            shape((seq_len, q_cols), BF),
            shape((S * rows, width), BF),
            shape((tokens, model), F32),
            shape((seq_len, model), BF),
            shape((S * rows, 2 * ff_cols), BF),
            shape((seq_len, model), BF),
            shape((S, 16, rows), BF),
        ),
        in_specs=[VMEM, ANY, VMEM, ANY, VMEM, VMEM, VMEM, ANY, ANY, VMEM],
        out_specs=[ANY, VMEM, VMEM, VMEM, ANY, VMEM, ANY, ANY, ANY, VMEM],
        scratch_shapes=[
            pltpu.VMEM((seq_len, model), BF),
            pltpu.VMEM((S, 16, rows), BF),
            pltpu.VMEM((S, rows, LANES), BF),
            pltpu.VMEM((q_rows, 2 * q_cols), BF),
            pltpu.VMEM((2, q_rows, LANES), BF),
            pltpu.VMEM(chip_ff, BF),
            pltpu.VMEM(chip_ff, BF),
            pltpu.VMEM((S * rows, width), BF),
            pltpu.VMEM((seq_len, model), BF),
            pltpu.VMEM((seq_len, width), F32),
            pltpu.VMEM((seq_len, LANES), BF),
            pltpu.VMEM((seq_len, LANES), BF),
            row_block,
            row_block,
            row_block,
            row_block,
            row_block,
            row_block,
            pltpu.VMEM((tokens, model), F32),
            row_block,
            pltpu.SemaphoreType.DMA((48,)),
            pltpu.SemaphoreType.DMA((48,)),
            pltpu.SemaphoreType.DMA((24,)),
        ],
        compiler_params=pltpu.CompilerParams(
            collective_id=0, has_side_effects=True, vmem_limit_bytes=60 * 2**20
        ),
    )(x, cot, gains, wq, wk, wv, wo, gate, up, tables)


def by_rows(count, body, step=16):
    if count % step:
        body(pl.ds(0, count))
        return

    def one(i, carry):
        body(pl.ds(pl.multiple_of(i * step, step), step))
        return carry

    lax.fori_loop(0, count // step, one, 0)


class Scatter:
    def __init__(self, links, term, far_in, across_out, across_in, beside_in):
        self.links, self.term = links, term
        self.far_in, self.across_out = far_in, across_out
        self.across_in, self.beside_in = across_in, beside_in
        self.tokens = far_in.shape[0]
        self.half = self.tokens // 2
        self.starts = [
            [
                pl.multiple_of((links.shard ^ mask) * self.tokens + extra, 16)
                for extra in (0, self.half)
            ]
            for mask in range(S)
        ]

    def rows(self, mask, part=None):
        if part is None:
            return pl.ds(self.starts[mask][0], self.tokens)
        return pl.ds(self.starts[mask][part], self.half)

    def send_far(self):
        self.far = self.links.to(self.term.at[self.rows(3)], self.far_in, 1)

    def send_across(self):
        self.far.wait_recv()
        self.across = []
        base = self.starts[2][0]
        for i in range(2):

            def add(rows):
                start = i * self.half + rows.start
                here = pl.ds(pl.multiple_of(start, 16), rows.size)
                there = pl.ds(pl.multiple_of(base + start, 16), rows.size)
                total = self.term[there, :].astype(F32)
                total += self.far_in[here, :].astype(F32)
                self.across_out[here, :] = total.astype(BF)

            by_rows(self.half, add)
            part = pl.ds(i * self.half, self.half)
            self.across.append(
                self.links.to(self.across_out.at[part], self.across_in.at[part], 2)
            )

    def send_beside(self):
        self.beside = self.links.to(self.term.at[self.rows(1)], self.beside_in, 1)

    def finish(self, i, use):
        if i == 0:
            self.beside.wait_recv()
        self.across[i].wait_recv()
        base = self.starts[0][0]

        def one(rows):
            start = i * self.half + rows.start
            here = pl.ds(pl.multiple_of(start, 16), rows.size)
            there = pl.ds(pl.multiple_of(base + start, 16), rows.size)
            total = self.term[there, :].astype(F32)
            total += self.beside_in[here, :].astype(F32)
            total += self.across_in[here, :].astype(F32)
            use(here, total)

        by_rows(self.half, one)

    def release(self):
        for copy in [self.far, self.beside] + self.across:
            self.links.sent(copy)


class Flow:
    def __init__(self, links, order, arrive, sends):
        self.links, self.arrive, self.sends = links, list(arrive), list(sends)
        self.bits = len(self.arrive)
        self.order = [b for b in order if b < self.bits]
        self.order += list(range(len(order), self.bits))
        self.left = list(range(self.bits - 1, -1, -1))
        self.sides = [(links.replica >> b) % 2 for b in range(self.bits)]
        self.others = [1 - side for side in self.sides]
        self.at = 0

    def begin(self, term):
        self.parts = [term]
        self.step()

    def pick(self, bit, side):
        where = (slice(None),) * self.left.index(bit) + (side,)
        return [part.at[where] for part in self.parts]

    def step(self):
        bit = self.order[self.at]
        mine = self.sides[bit]
        if self.at:
            self.copy.wait_recv()
        other = self.pick(bit, self.others[bit])
        source = other[0]
        if self.at:
            source = self.sends[self.at - 1]
            self.add(other, source, len(self.left) - 1)
        self.copy = self.links.to(source, self.arrive[self.at], 0, 1 << bit)
        self.parts = self.pick(bit, mine) + [self.arrive[self.at]]
        self.left.remove(bit)
        self.at += 1

    def end(self, target):
        self.copy.wait_recv()
        self.add(self.parts, target, 0)

    def add(self, parts, target, free):
        ways = list(itertools.product(range(2), repeat=free))
        rest = parts[0].shape[free:]
        jobs = [(way, part) for way in ways for part in parts]

        def inner(fetch, sems):
            copies = []
            for n, (way, part) in enumerate(jobs):
                source = part.at[way] if way else part
                copy = pltpu.make_async_copy(source, fetch.at[n], sems.at[n])
                copy.start()
                copies.append(copy)
            for w, way in enumerate(ways):
                first = w * len(parts)
                for k in range(len(parts)):
                    copies[first + k].wait()
                leads = [()] if len(rest) == 2 else [(g,) for g in range(rest[0])]
                for lead in leads:

                    def one(rows):
                        total = fetch[(first,) + lead + (rows,)].astype(F32)
                        for k in range(1, len(parts)):
                            more = fetch[(first + k,) + lead + (rows,)]
                            total += more.astype(F32)
                        target[way + lead + (rows,)] = total.astype(target.dtype)

                    by_rows(rest[-2], one)

        pl.run_scoped(
            inner,
            pltpu.VMEM((len(jobs),) + tuple(rest), BF),
            pltpu.SemaphoreType.DMA((len(jobs),)),
        )


def bits_of(index, count):
    return tuple((index >> b) & 1 for b in reversed(range(count.bit_length() - 1)))


def turn(source, cols, target):
    rows = source.shape[0]
    for i in range(0, rows, 256):
        part = source[i : i + 256, cols]
        target[:, i : i + 256] = part.astype(F32).T.astype(BF)


def produce(left_t, right, first, size, stage, replicas, lead=(), tile=256):
    share = left_t.shape[0] // replicas

    def one(t, carry):
        start = pl.multiple_of(t * tile, LANES)
        cols = pl.ds(pl.multiple_of(first + start, LANES), tile)
        result = matmul(left_t[...], right[:, cols])
        for r in range(replicas):
            where = bits_of(r, replicas) + lead + (slice(None), pl.ds(start, tile))
            stage[where] = result[r * share : (r + 1) * share].astype(BF)
        return carry

    lax.fori_loop(0, size // tile, one, 0)


def stream(count, copies_of, use):
    for copy in copies_of(0, 0):
        copy.start()

    def one(t, carry):
        slot = t % 2

        @pl.when(t + 1 < count)
        def _():
            for copy in copies_of(t + 1, 1 - slot):
                copy.start()

        for copy in copies_of(t, slot):
            copy.wait()
        use(t, slot)
        return carry

    lax.fori_loop(0, count, one, 0)


def norm_back_rows(grad, values, gain_row):
    scale = rms_scale(values)
    weighted = grad * gain_row
    mean = jnp.mean(weighted * values, axis=-1, keepdims=True)
    return scale * weighted - values * (scale * scale * scale * mean)


def rear_kernel(
    norm2_hbm, cot_hbm, w_ff_hbm, w_down_hbm, norm1_hbm, mixed_hbm, w_out_hbm, heads_hbm, logs_hbm,
    table_hbm, w_heads_hbm, mid_ref, cot_ref, x_ref, gain_ref,
    output_ref, input_grad_ref, grad_out_ref, grad_down_ref, pieces_ff, pieces_heads, *others,
):
    shard, replica = lax.axis_index("shard"), lax.axis_index("replica")
    tokens, model = mid_ref.shape
    seq_len = S * tokens
    ff_cols, rows = w_down_hbm.shape[0], model // S
    width = heads_hbm.shape[1]
    q_cols = width - LANES
    replicas = model // (S * pieces_ff.shape[1])
    bits = replicas.bit_length() - 1
    share, share_down = pieces_ff.shape[1], grad_down_ref.shape[0]
    half, half_model = tokens // 2, model // 2
    others = list(others)

    def take(count):
        taken = others[:count]
        del others[:count]
        return taken

    hbm = {name: take(1 + bits) for name in ("ff", "down", "out", "heads")}
    cot_all, term, far_in, across_out, across_in, beside_in, grad_mid, grad_mid_b = take(8)
    sends = {name: take(bits) for name in ("ff", "down", "out", "heads")}
    send, recv, local, slots = take(4)
    links = Links(shard, replica, send, recv, local)
    other_chip = 1 - shard // 2

    def flow(name, order, index=None):
        pick = (lambda ref: ref) if index is None else (lambda ref: ref.at[index])
        made = Flow(
            links,
            order,
            [pick(ref) for ref in hbm[name][1:]],
            [pick(ref) for ref in sends[name][:-1]],
        )
        made.term, made.last = pick(hbm[name][0]), pick(sends[name][-1])
        return made

    flows_ff = [flow("ff", (0, 1, 2), m) for m in range(S)]
    flows_down = [flow("down", (1, 0, 2), i) for i in range(2)]
    flow_out, flow_heads = flow("out", (1, 0, 2)), flow("heads", (0, 1, 2))

    def end_ff(mask):
        flows_ff[mask].end(flows_ff[mask].last)
        if mask:
            return links.to(flows_ff[mask].last, pieces_ff.at[mask], mask)
        return links.here(flows_ff[mask].last, pieces_ff.at[mask])

    def end_down(i):
        flows_down[i].end(flows_down[i].last)
        cols = pl.ds(i * half_model, half_model)
        return links.here(flows_down[i].last, grad_down_ref.at[:, cols])

    def stored(stage, flow):
        copy = links.here(stage, flow.term)
        return copy

    greet(shard, replica, (1, 2, 3), [1 << b for b in range(bits)])
    gain_one, gain_two = (
        jnp.concatenate(
            [gain_ref[j, i : i + 1, :].astype(F32) for j in range(S)], axis=1
        )
        for i in range(2)
    )
    sums = Scatter(links, term, far_in, across_out, across_in, beside_in)
    ended = []

    def first_half(norm2, hidden, grad_ff):
        norm2_in = links.here(norm2_hbm, norm2)
        cot_in = links.here(cot_hbm, cot_all)

        def feed_forward(gates, ups, downs):
            tile = 256
            tiles = [(i, min(tile, ff_cols - i)) for i in range(0, ff_cols, tile)]

            def copies_of(t):
                start, size = tiles[t]
                slot = t % 2
                cols = slice(start, start + size)
                up_cols = slice(ff_cols + start, ff_cols + start + size)
                return [
                    pltpu.make_async_copy(*pair, slots.at[slot, n])
                    for n, pair in enumerate(
                        (
                            (w_ff_hbm.at[:, cols], gates.at[slot, :, :size]),
                            (w_ff_hbm.at[:, up_cols], ups.at[slot, :, :size]),
                            (w_down_hbm.at[cols], downs.at[slot, :size]),
                        )
                    )
                ]

            for copy in copies_of(0):
                copy.start()
            norm2_in.wait()
            cot_in.wait()
            for t, (start, size) in enumerate(tiles):
                if t + 1 < len(tiles):
                    for copy in copies_of(t + 1):
                        copy.start()
                for copy in copies_of(t):
                    copy.wait()
                slot = t % 2

                def block(b, carry):
                    r = pl.ds(pl.multiple_of(b * 512, 512), 512)
                    gate = matmul(norm2[r, :], gates[slot, :, :size])
                    up = matmul(norm2[r, :], ups[slot, :, :size])
                    grad = matmul_right_t(cot_all[r, :], downs[slot, :size])
                    sigmoid = 1.0 / (1.0 + jnp.exp(-gate))
                    silu = gate * sigmoid
                    hidden[r, start : start + size] = (silu * up).astype(BF)
                    grad_gate = grad * up * (sigmoid * (1.0 + gate * (1.0 - sigmoid)))
                    grad_ff[r, start : start + size] = grad_gate.astype(BF)
                    grad_ff[r, ff_cols + start : ff_cols + start + size] = (
                        grad * silu
                    ).astype(BF)
                    return carry

                lax.fori_loop(0, seq_len // 512, block, 0)

        weight_tile = pltpu.VMEM((2, model, 256), BF)
        pl.run_scoped(
            feed_forward, weight_tile, weight_tile, pltpu.VMEM((2, 256, model), BF)
        )

        def down_terms(left_t, stage):
            turn(hidden, slice(None), left_t)
            for i in range(2):
                produce(left_t, cot_all, i * half_model, half_model, stage, replicas)
                links.here(stage, flows_down[i].term).wait()
                flows_down[i].begin(flows_down[i].term)

        pl.run_scoped(
            down_terms,
            pltpu.VMEM((ff_cols, seq_len), BF),
            pltpu.VMEM((2,) * bits + (share_down, half_model), BF),
        )

        def norm_terms(chip):
            def inner(tiles):
                r = pl.ds(pl.multiple_of(chip * 2 * tokens, 2 * tokens), 2 * tokens)

                def copies_of(t, slot):
                    part = pl.ds(pl.multiple_of(t * 256, 256), 256)
                    return [
                        pltpu.make_async_copy(
                            w_ff_hbm.at[part], tiles.at[slot], slots.at[slot, 0]
                        )
                    ]

                def use(t, slot):
                    cols = pl.ds(pl.multiple_of(t * 256, 256), 256)
                    product = matmul_right_t(grad_ff[r, :], tiles[slot])
                    term[r, cols] = product.astype(BF)

                stream(model // 256, copies_of, use)

            pl.run_scoped(inner, pltpu.VMEM((2, 256, 2 * ff_cols), BF))

        norm_terms(other_chip)
        sums.send_far()

        def ff_terms(left_t, stages):
            copies = {}
            for n, mask in enumerate((3, 2, 1, 0)):
                cols = pl.ds(pl.multiple_of((shard ^ mask) * rows, rows), rows)
                turn(norm2, cols, left_t)
                if n >= 2:
                    copies[n - 2][0].wait()
                    copies[n - 2][1].begin(copies[n - 2][1].term)
                produce(left_t, grad_ff, 0, 2 * ff_cols, stages.at[n % 2], replicas)
                copies[n] = (
                    links.here(stages.at[n % 2], flows_ff[mask].term),
                    flows_ff[mask],
                )
                if n == 0:
                    sums.send_across()
            for n in (2, 3):
                copies[n][0].wait()
                copies[n][1].begin(copies[n][1].term)

        pl.run_scoped(
            ff_terms,
            pltpu.VMEM((rows, seq_len), BF),
            pltpu.VMEM((2,) + (2,) * bits + (share, 2 * ff_cols), BF),
        )
        norm_terms(1 - other_chip)
        sums.send_beside()

        def to_mid(r, grad):
            values = mid_ref[r, :]
            total = cot_ref[r, :].astype(F32)
            total += norm_back_rows(grad, values, gain_two)
            grad_mid[r, :] = total
            grad_mid_b[r, :] = total.astype(BF)

        gathered = []
        for i in range(2):
            sums.finish(i, to_mid)
            part = slice(i * half, (i + 1) * half)
            there = sums.rows(0, i)
            gathered.append(
                [
                    links.to(grad_mid_b.at[part], cot_all.at[there], 2),
                    links.to(grad_mid_b.at[part], cot_all.at[there], 1),
                    links.here(grad_mid_b.at[part], cot_all.at[there]),
                ]
            )
        sums.release()
        flows_down[0].step()

        def out_terms(tiles):
            def copies_of(t, slot):
                part = pl.ds(pl.multiple_of(t * 256, 256), 256)
                return [
                    pltpu.make_async_copy(
                        w_down_hbm.at[:, part], tiles.at[slot], slots.at[slot, 0]
                    )
                ]

            def use(t, slot):
                cols = pl.ds(pl.multiple_of(t * 256, 256), 256)
                term[:, cols] = matmul(hidden[...], tiles[slot]).astype(BF)

            stream(model // 256, copies_of, use)

        pl.run_scoped(out_terms, pltpu.VMEM((2, ff_cols, 256), BF))
        return gathered

    gathered = []
    pl.run_scoped(
        lambda *refs: gathered.extend(first_half(*refs)),
        pltpu.VMEM((seq_len, model), BF),
        pltpu.VMEM((seq_len, ff_cols), BF),
        pltpu.VMEM((seq_len, 2 * ff_cols), BF),
    )

    def second_half(mixed, w_out, heads, logs, table, w_heads, grad_mixed, grad_heads,
                    kk_ref, vv_ref, dk_ref, dv_ref):
        loads = [
            links.here(*pair)
            for pair in (
                (w_out_hbm, w_out),
                (heads_hbm, heads),
                (logs_hbm, logs),
                (table_hbm, table),
                (mixed_hbm, mixed),
                (w_heads_hbm, w_heads),
            )
        ]
        for i in range(2):
            gathered[i][1].wait_recv()
            gathered[i][2].wait()
        sums.send_far()
        sums.send_beside()
        for copy in loads:
            copy.wait()

        def mix(mask, part=None):
            r = sums.rows(mask, part)
            grad_mixed[r, :] = matmul_right_t(cot_all[r, :], w_out[...]).astype(BF)

        mix(0)
        mix(1)
        kv = heads[:, q_cols:].astype(F32)
        swapped = pltpu.roll(kv, HD, 1)
        kk_ref[...] = both(kv, swapped).astype(BF)
        vv_ref[...] = both(swapped, kv).astype(BF)
        dk_ref[...] = jnp.zeros_like(dk_ref)
        dv_ref[...] = jnp.zeros_like(dv_ref)
        flows_ff[3].step()
        forward = []
        for i in range(2):
            gathered[i][0].wait_recv()
            r = sums.rows(2, i)
            forward.append(links.to(cot_all.at[r], cot_all.at[r], 1))
            mix(2, i)
        sums.send_across()
        flows_down[1].step()
        for i in range(2):
            forward[i].wait_recv()
            mix(3, i)

        def out_grad(left_t, stage):
            turn(mixed, slice(None), left_t)
            produce(left_t, cot_all, 0, model, stage, replicas)
            links.here(stage, flow_out.term).wait()
            flow_out.begin(flow_out.term)

        pl.run_scoped(
            out_grad,
            pltpu.VMEM((rows, seq_len), BF),
            pltpu.VMEM((2,) * bits + (share, model), BF),
        )

        def attend_rows(i):
            r = slice(i * tokens, (i + 1) * tokens)
            seen = (i + 1) * tokens

            def pair_step(j, carry):
                cols = pl.ds(pl.multiple_of(j * LANES, LANES), LANES)
                q = two_heads(heads[r, cols])
                grad = two_heads(grad_mixed[r, cols])
                lane = lax.broadcasted_iota(jnp.int32, (tokens, LANES), 1)
                log_col = jnp.concatenate(
                    [
                        jnp.sum(
                            jnp.where(lane == 2 * j + n, logs[r], 0.0), -1, keepdims=True
                        )
                        for n in (0, 1)
                    ],
                    axis=0,
                )
                scores = matmul_right_t(q, kk_ref[:seen])
                soft = jnp.exp(causal_mask(scores, i * tokens) - log_col)
                grad_soft = matmul_right_t(grad, vv_ref[:seen])
                inner = jnp.sum(soft * grad_soft, axis=-1, keepdims=True)
                grad_scores = (soft * (grad_soft - inner)).astype(BF)
                dq = matmul(grad_scores, kk_ref[:seen])
                dq = both(dq[:tokens], dq[tokens:]) * HD**-0.5
                dq = dq * table[0, r] - turned(dq) * table[1, r]
                grad_heads[r, cols] = dq.astype(BF)
                dk_ref[:seen] += matmul_left_t(grad_scores, q)
                dv_ref[:seen] += matmul_left_t(soft.astype(BF), grad)
                return carry

            lax.fori_loop(0, q_cols // LANES, pair_step, 0)

        attend_rows(0)
        attend_rows(1)
        flows_down[0].step()
        flows_ff[2].step()
        attend_rows(2)
        flows_ff[3].step()
        attend_rows(3)
        dk, dv = dk_ref[...], dv_ref[...]
        dk, dv = dk + pltpu.roll(dk, HD, 1), dv + pltpu.roll(dv, HD, 1)
        dkv = both(dk, dv)
        dkv = dkv * table[2] - turned(dkv) * table[3]
        grad_heads[:, q_cols:] = dkv.astype(BF)

        def to_output(r, total):
            output_ref[r, :] = (mid_ref[r, :] + total).astype(BF)

        for i in range(2):
            sums.finish(i, to_output)
        sums.release()
        for mask in (1, 2):
            pl.semaphore_signal(
                credit.at[mask - 1],
                inc=1,
                device_id={"shard": shard ^ mask, "replica": replica},
                device_id_type=MESH_ID,
            )

        def head_terms(chip):
            r = pl.ds(pl.multiple_of(chip * 2 * tokens, 2 * tokens), 2 * tokens)

            def one(t, carry):
                cols = pl.ds(pl.multiple_of(t * 256, 256), 256)
                product = matmul_right_t(grad_heads[r, :], w_heads[cols, :])
                term[r, cols] = product.astype(BF)
                return carry

            lax.fori_loop(0, model // 256, one, 0)

        def head_grads(norm1, left_t, stage):
            norm1_in = links.here(norm1_hbm, norm1)
            head_terms(other_chip)
            pl.semaphore_wait(credit.at[0], 1)
            sums.send_far()
            norm1_in.wait()
            for s in range(S):
                turn(norm1, slice(s * rows, (s + 1) * rows), left_t)
                produce(left_t, grad_heads, 0, width, stage, replicas, (s,), LANES)
            stage_out = links.here(stage, flow_heads.term)
            pl.semaphore_wait(credit.at[1], 1)
            sums.send_across()
            stage_out.wait()
            flow_heads.begin(flow_heads.term)
            head_terms(1 - other_chip)
            sums.send_beside()

        pl.run_scoped(
            head_grads,
            pltpu.VMEM((seq_len, model), BF),
            pltpu.VMEM((rows, seq_len), BF),
            pltpu.VMEM((2,) * bits + (S, share, width), BF),
        )

    credit = take(1)[0]
    pl.run_scoped(
        second_half,
        pltpu.VMEM((seq_len, q_cols), BF),
        pltpu.VMEM((q_cols, model), BF),
        pltpu.VMEM((seq_len, width), BF),
        pltpu.VMEM((seq_len, LANES), F32),
        pltpu.VMEM((4, seq_len, LANES), F32),
        pltpu.VMEM((model, width), BF),
        pltpu.VMEM((seq_len, q_cols), BF),
        pltpu.VMEM((seq_len, width), BF),
        pltpu.VMEM((seq_len, LANES), BF),
        pltpu.VMEM((seq_len, LANES), BF),
        pltpu.VMEM((seq_len, LANES), F32),
        pltpu.VMEM((seq_len, LANES), F32),
    )

    def to_input_grad(r, grad):
        total = grad_mid[r, :]
        total += norm_back_rows(grad, x_ref[r, :].astype(F32), gain_one)
        input_grad_ref[r, :] = total.astype(BF)

    pending = flows_down + [flow_out] + [flows_ff[m] for m in (3, 2, 1, 0)]
    finals = []
    flows_ff[1].step()
    flows_ff[2].step()
    flows_down[1].step()
    flow_out.step()
    flows_ff[0].step()
    flows_ff[1].step()
    for i in range(2):
        sums.finish(i, to_input_grad)
    flow_out.step()
    flows_ff[0].step()
    flow_heads.step()
    for f in pending:
        while f.at < bits:
            f.step()
    finals.append(end_ff(3))
    finals.append(end_ff(2))
    end_down(0).wait()
    end_down(1).wait()
    flow_out.end(flow_out.last)
    out_here = links.here(flow_out.last, grad_out_ref)
    finals.append(end_ff(1))
    own_ff = end_ff(0)
    while flow_heads.at < bits:
        flow_heads.step()
    flow_heads.end(flow_heads.last)
    own_heads = links.here(flow_heads.last.at[shard], pieces_heads.at[0])
    for mask in (3, 2, 1):
        finals.append(
            links.to(flow_heads.last.at[shard ^ mask], pieces_heads.at[mask], mask)
        )
    for copy in finals:
        copy.wait_recv()
    for copy in (out_here, own_ff, own_heads):
        copy.wait()
    links.close()


def rear(norm2, cot_all, w_ff, w_down, norm1, mixed, w_out, heads, logs, tables, w_heads, mid, cot, x, gains, replicas):
    tokens, model = mid.shape
    seq_len, rows, ff_cols = S * tokens, model // S, w_down.shape[0]
    width = heads.shape[1]
    bits = replicas.bit_length() - 1
    share, share_down = rows // replicas, ff_cols // replicas
    shape = jax.ShapeDtypeStruct
    rests = {
        "ff": ((S,), (share, 2 * ff_cols), BF),
        "down": ((2,), (share_down, model // 2), F32),
        "out": ((), (share, model), F32),
        "heads": ((), (S, share, width), BF),
    }
    work, sends = [], []
    for many, rest, last in rests.values():
        work += [shape(many + (2,) * bits + rest, BF)]
        work += [shape(many + (2,) * n + rest, BF) for n in reversed(range(bits))]
        sends += [
            pltpu.VMEM(many + (2,) * n + rest, BF) for n in reversed(range(bits - 1))
        ]
        sends += [pltpu.VMEM(many + rest, last)]
    outs = (
        shape((tokens, model), BF),
        shape((tokens, model), BF),
        shape((share, model), F32),
        shape((share_down, model), F32),
        shape((S, share, 2 * ff_cols), BF),
        shape((S, share, width), BF),
    )
    row_block = pltpu.VMEM((tokens, model), BF)
    result = pl.pallas_call(
        rear_kernel,
        out_shape=outs + tuple(work),
        in_specs=[ANY] * 11 + [VMEM] * 4,
        out_specs=[VMEM] * 2 + [ANY] * (4 + len(work)),
        scratch_shapes=[
            pltpu.VMEM((seq_len, model), BF),
            pltpu.VMEM((seq_len, model), BF),
            row_block,
            row_block,
            row_block,
            row_block,
            pltpu.VMEM((tokens, model), F32),
            row_block,
        ]
        + sends
        + [
            pltpu.SemaphoreType.DMA((96,)),
            pltpu.SemaphoreType.DMA((96,)),
            pltpu.SemaphoreType.DMA((48,)),
            pltpu.SemaphoreType.DMA((2, 3)),
            pltpu.SemaphoreType.REGULAR((2,)),
        ],
        compiler_params=pltpu.CompilerParams(
            collective_id=1, has_side_effects=True, vmem_limit_bytes=62 * 2**20
        ),
    )(norm2, cot_all, w_ff, w_down, norm1, mixed, w_out, heads, logs, tables, w_heads, mid, cot, x, gains)
    return result[: len(outs)]


def on_device(
    inputs, cotangent, gain_attn, w_query, w_key, w_value, w_output, gain_mlp, w_gate, w_up, w_down
):
    shard, replica = lax.axis_index("shard"), lax.axis_index("replica")
    x, cot = inputs[0], cotangent[0]
    tables = jnp.asarray(rope_tables(S * x.shape[0]))
    gains = jnp.concatenate(
        [jnp.stack([gain_attn, gain_mlp]), jnp.zeros((14, w_query.shape[0]), BF)]
    )
    norm1, heads, logs, mixed, w_heads, mid, norm2, w_ff, cot_all, gains = front(
        x, cot, gains, w_query, w_key, w_value, w_output, w_gate, w_up, tables
    )
    output, input_grad, grad_output, grad_down, pieces_ff, pieces_heads = rear(
        norm2, cot_all, w_ff, w_down, norm1, mixed, w_output, heads, logs, tables,
        w_heads, mid, cot, x, gains, lax.axis_size("replica"),
    )
    (grad_gate, grad_up), grad_gain_two = finish(
        pieces_ff, (w_gate, w_up), gain_mlp, shard, replica
    )
    (grad_query, grad_key, grad_value), grad_gain_one = finish(
        pieces_heads, (w_query, w_key, w_value), gain_attn, shard, replica
    )
    return (
        output[None],
        input_grad[None],
        grad_gain_one,
        grad_query,
        grad_key,
        grad_value,
        grad_output,
        grad_gain_two,
        grad_gate,
        grad_up,
        grad_down,
    )


def solution(mesh):
    placed = (
        P("replica", "shard", None),
        P("replica", "shard", None),
        P("shard"),
        P("shard", None),
        P("shard", None),
        P("shard", None),
        P("shard", None),
        P("shard"),
        P("shard", None),
        P("shard", None),
        P("shard", None),
    )
    both_axes = ("shard", "replica")
    return jax.shard_map(
        on_device,
        mesh=mesh,
        in_specs=placed,
        out_specs=(
            P("replica", "shard", None),
            P("replica", "shard", None),
            P(both_axes),
            P(both_axes, None),
            P(both_axes, None),
            P(both_axes, None),
            P(both_axes, None),
            P(both_axes),
            P(both_axes, None),
            P(both_axes, None),
            P(both_axes, None),
        ),
        check_vma=False,
    )
```

```python
import functools
import itertools

import jax
import jax.numpy as jnp
import numpy as np
from jax import lax
from jax.experimental import pallas as pl
from jax.experimental.pallas import tpu as pltpu
from jax.sharding import PartitionSpec as P

H = 32
KV = 4
HD = 64
EPS = 1e-05
THETA = 10000.0
S = 4
BF = jnp.bfloat16
F32 = jnp.float32
LANES = 128
QB = 256


def matmul(left, right):
    return jnp.dot(left, right, preferred_element_type=F32)


def matmul_left_t(left, right):
    return lax.dot_general(
        left, right, (((0,), (0,)), ((), ())), preferred_element_type=F32
    )


def matmul_right_t(left, right):
    return lax.dot_general(
        left, right, (((1,), (1,)), ((), ())), preferred_element_type=F32
    )


def rms_scale(values):
    return lax.rsqrt(jnp.mean(values * values, axis=-1, keepdims=True) + EPS)


def finish_kernel(groups, moved, place_ref, *refs):
    refs = list(refs)

    def take(count):
        taken = refs[:count]
        del refs[:count]
        return taken

    many = [len(widths) for widths in groups]
    pieces, gains = take(len(groups)), take(len(groups))
    weights = [take(n) for n in many]
    sources = take(moved)
    outs, gain_outs = [take(n) for n in many], take(len(groups))
    targets = take(moved)
    held = [take(n) for n in many]
    sems = refs[0]
    shard, replica = place_ref[0], place_ref[1]
    copies = []

    def start(source, target):
        copies.append(pltpu.make_async_copy(source, target, sems.at[len(copies)]))
        copies[-1].start()

    for mine, kept in zip(weights, held):
        for weight, here in zip(mine, kept):
            rows = here.shape[0]
            start(weight.at[pl.ds(pl.multiple_of(replica * rows, rows), rows)], here)
    loads = list(copies)
    for source, target in zip(sources, targets):
        start(source, target)
    for copy in loads:
        copy.wait()
    for g, widths in enumerate(groups):
        total = jnp.zeros(gain_outs[g].shape, F32)
        for mask in range(S):
            piece = pieces[g].at[mask]
            owner = shard ^ mask
            begin = 0
            for width, weight, out in zip(widths, held[g], outs[g]):
                if width % LANES == 0:
                    cols = pl.ds(pl.multiple_of(owner * width, LANES), width)
                    part = piece[:, begin : begin + width].astype(F32)
                    out[:, cols] = part
                else:
                    base = begin // LANES * LANES
                    part = piece[:, base : base + LANES].astype(F32)
                    lane = lax.broadcasted_iota(jnp.int32, part.shape, 1) // HD
                    side = owner % 2
                    part = jnp.where(
                        side == (begin - base) // HD, part, pltpu.roll(part, HD, 1)
                    )
                    part = jnp.where(lane == side, part, 0.0)
                    cols = pl.ds(pl.multiple_of(owner // 2 * LANES, LANES), LANES)
                    out[:, cols] = jnp.where(lane == side, part, out[:, cols])
                total += jnp.sum(
                    part * weight[:, cols].astype(F32), axis=1, keepdims=True
                )
                begin += width
        gain_outs[g][...] = total / gains[g][...]
    for copy in copies[len(loads) :]:
        copy.wait()


def finish(pieces, weights, gains, moved, shard, replica):
    rows = pieces[0].shape[1]
    groups = [tuple(w.shape[1] // S for w in mine) for mine in weights]
    flat = [w for mine in weights for w in mine]
    own_gains = [
        lax.dynamic_slice_in_dim(gain, replica * rows, rows, 0)
        .astype(F32)
        .reshape(rows, 1)
        for gain in gains
    ]
    shapes = [jax.ShapeDtypeStruct((rows, w.shape[1]), F32) for w in flat]
    shapes += [jax.ShapeDtypeStruct((rows, 1), F32)] * len(groups)
    shapes += [jax.ShapeDtypeStruct(a.shape, a.dtype) for a in moved]
    vmem, hbm = (pl.BlockSpec(memory_space=m) for m in (pltpu.VMEM, pl.ANY))
    held = len(flat) + len(groups)
    result = pl.pallas_call(
        functools.partial(finish_kernel, groups, len(moved)),
        out_shape=shapes,
        in_specs=[pl.BlockSpec(memory_space=pltpu.SMEM)]
        + [vmem] * (2 * len(groups))
        + [hbm] * (len(flat) + len(moved)),
        out_specs=[vmem] * held + [hbm] * len(moved),
        scratch_shapes=[pltpu.VMEM((rows, w.shape[1]), BF) for w in flat]
        + [pltpu.SemaphoreType.DMA((len(flat) + len(moved),))],
        compiler_params=pltpu.CompilerParams(vmem_limit_bytes=62 * 2**20),
    )(
        jnp.stack([shard, replica]).astype(jnp.int32),
        *pieces,
        *own_gains,
        *flat,
        *moved,
    )
    return (
        result[: len(flat)],
        [gain.reshape(rows) for gain in result[len(flat) : held]],
        result[held:],
    )


def rope_tables(seq_len):
    half = HD // 2
    freq = THETA ** (-2.0 * np.arange(half, dtype=np.float64) / HD)
    angles = np.arange(seq_len, dtype=np.float64)[:, None] * freq[None, :]
    cos, sin = np.cos(angles), np.sin(angles)
    one, zero = np.ones((seq_len, HD)), np.zeros((seq_len, HD))
    cos_head = np.concatenate([cos, cos], 1)
    sin_head = np.concatenate([-sin, sin], 1)
    tables = [
        np.concatenate([cos_head, cos_head], 1),
        np.concatenate([sin_head, sin_head], 1),
        np.concatenate([cos_head, one], 1),
        np.concatenate([sin_head, zero], 1),
    ]
    return np.stack(tables).astype(np.float32)


def turned(values):
    lane = lax.broadcasted_iota(jnp.int32, values.shape, 1)
    return jnp.where(
        lane % HD < HD // 2,
        pltpu.roll(values, LANES - HD // 2, 1),
        pltpu.roll(values, HD // 2, 1),
    )


def both(first, second):
    lane = lax.broadcasted_iota(jnp.int32, first.shape, 1)
    return jnp.where(lane < HD, first, second)


def two_heads(pair):
    zero = jnp.zeros_like(pair)
    return jnp.concatenate([both(pair, zero), both(zero, pair)], axis=0)


def causal_mask(scores, first_row):
    block = scores.shape[0] // 2
    last = scores[:, first_row:]
    row = lax.broadcasted_iota(jnp.int32, last.shape, 0) % block
    col = lax.broadcasted_iota(jnp.int32, last.shape, 1)
    last = jnp.where(col <= row, last, -1e30)
    if not first_row:
        return last
    return jnp.concatenate([scores[:, :first_row], last], axis=1)


MESH_ID = pl.DeviceIdType.MESH
ANY = pl.BlockSpec(memory_space=pl.ANY)
VMEM = pl.BlockSpec(memory_space=pltpu.VMEM)


class Copy:
    def __init__(self, describe):
        self.describe = describe
        describe().start()

    def wait(self):
        self.describe().wait()

    def wait_recv(self):
        self.describe().wait_recv()

    def wait_send(self):
        self.describe().wait_send()


class Links:
    def __init__(self, shard, replica, send, recv, local):
        self.shard, self.replica = shard, replica
        self.send, self.recv, self.local = send, recv, local
        self.used, self.used_local = 0, 0
        self.open = []

    def to(self, source, target, shard=0, replica=0):
        n, self.used = self.used, self.used + 1
        copy = Copy(
            lambda: pltpu.make_async_remote_copy(
                src_ref=source,
                dst_ref=target,
                send_sem=self.send.at[n],
                recv_sem=self.recv.at[n],
                device_id={
                    "shard": self.shard ^ shard,
                    "replica": self.replica ^ replica,
                },
                device_id_type=MESH_ID,
            )
        )
        self.open.append(copy)
        return copy

    def here(self, source, target):
        n, self.used_local = self.used_local, self.used_local + 1
        return Copy(
            lambda: pltpu.make_async_copy(source, target, self.local.at[n])
        )

    def sent(self, copy):
        copy.wait_send()
        self.open = [other for other in self.open if other is not copy]

    def close(self):
        for copy in self.open:
            copy.wait_send()


def greet(shard, replica, shard_masks, replica_masks):
    barrier = pltpu.get_barrier_semaphore()
    for mask in shard_masks:
        pl.semaphore_signal(
            barrier,
            inc=1,
            device_id={"shard": shard ^ mask, "replica": replica},
            device_id_type=MESH_ID,
        )
    for mask in replica_masks:
        pl.semaphore_signal(
            barrier,
            inc=1,
            device_id={"shard": shard, "replica": replica ^ mask},
            device_id_type=MESH_ID,
        )
    pl.semaphore_wait(barrier, len(shard_masks) + len(replica_masks))


def norm_rows(source, target, gains, which, start, count):
    model = source.shape[1]
    part = model // S

    def step(i, carry):
        rows = pl.ds(pl.multiple_of(start + i * 16, 16), 16)
        values = source[rows, :].astype(F32)
        scale = rms_scale(values)
        for j in range(S):
            gain = gains[j, which : which + 1, :].astype(F32)
            cols = slice(j * part, (j + 1) * part)
            target[rows, cols] = (values[:, cols] * scale * gain).astype(BF)
        return carry

    lax.fori_loop(0, count // 16, step, 0, unroll=2)


def front_kernel(
    x_ref, cot_ref, gain_ref, wq_ref, wk_ref, wv_ref, wo_ref, gate_ref, up_ref, table_ref,
    norm1_ref, heads_ref, log_ref, mixed_ref, w_heads_ref, mid_ref, norm2_ref, w_ff_ref, cot_all_ref, gains_ref,
    x_all, gains, kv_parts, near_q, near_kv, near_gate, near_up, w_heads, norm1, pre, kk_ref, vv_ref,
    far_out, far_in, across_out, across_in, beside_out, beside_in, term, norm2, send, recv, local,
):
    shard, replica = lax.axis_index("shard"), lax.axis_index("replica")
    x, core, quarter = shard // 2, shard % 2, replica % 4
    tokens, model = x_ref.shape
    seq_len = S * tokens
    rows = wq_ref.shape[0]
    q_cols, ff_cols = wq_ref.shape[1] // S, gate_ref.shape[1] // S
    width = q_cols + LANES
    q_rows, half = rows // 4, tokens // 2
    links = Links(shard, replica, send, recv, local)

    def lanes(index, size):
        return pl.ds(pl.multiple_of(index * size, LANES), size)

    def block(index, size=tokens, extra=0):
        return pl.ds(pl.multiple_of(index * size + extra, 16), size)

    for j in range(S):
        keys = wk_ref[:, j // 2 * LANES : (j // 2 + 1) * LANES].astype(F32)
        vals = wv_ref[:, j // 2 * LANES : (j // 2 + 1) * LANES].astype(F32)
        if j % 2 == 0:
            pair = both(keys, pltpu.roll(vals, HD, 1))
        else:
            pair = both(pltpu.roll(keys, HD, 1), vals)
        kv_parts[j] = pair.astype(BF)

    greet(shard, replica, (1, 2, 3), (1, 2))

    mine = pl.ds(pl.multiple_of(quarter * q_rows, q_rows), q_rows)
    other_chip = 1 - x
    across_q = links.to(wq_ref.at[mine, lanes(other_chip, 2 * q_cols)], near_q, 2)
    across_kv = links.to(kv_parts.at[pl.ds(2 * other_chip, 2), mine], near_kv, 2)
    gain_copies = [links.to(gain_ref, gains.at[shard], m) for m in (1, 2, 3)]
    own_rows = [
        pl.ds(pl.multiple_of(shard * tokens + i * half, half), half) for i in range(2)
    ]
    x_across = [
        links.to(x_ref.at[pl.ds(i * half, half)], x_all.at[own_rows[i]], 2)
        for i in range(2)
    ]
    x_beside = links.to(x_ref, x_all.at[block(shard)], 1)
    own_w = pl.ds(pl.multiple_of(shard * rows, rows), rows)
    pair_shard = shard ^ 1
    w_beside = [
        links.to(
            wq_ref.at[:, lanes(pair_shard, q_cols)], w_heads.at[own_w, :q_cols], 1
        ),
        links.to(kv_parts.at[pair_shard], w_heads.at[own_w, q_cols:], 1),
    ]
    here = [
        links.here(x_ref, x_all.at[block(shard)]),
        links.here(gain_ref, gains.at[shard]),
        links.here(wq_ref.at[:, lanes(shard, q_cols)], w_heads.at[own_w, :q_cols]),
        links.here(kv_parts.at[shard], w_heads.at[own_w, q_cols:]),
    ]
    here_late = [
        links.here(gate_ref.at[:, lanes(shard, ff_cols)], w_ff_ref.at[own_w, :ff_cols]),
        links.here(up_ref.at[:, lanes(shard, ff_cols)], w_ff_ref.at[own_w, ff_cols:]),
        links.here(cot_ref, cot_all_ref.at[block(shard)]),
    ]

    def rows_from(mask, of):
        return pl.ds(
            pl.multiple_of((shard ^ mask) * rows + (quarter ^ of) * q_rows, q_rows),
            q_rows,
        )

    across_q.wait_recv()
    across_kv.wait_recv()
    near_rows, far_rows = rows_from(2, 0), rows_from(3, 0)
    pair_lanes = lanes(1 - core, q_cols)
    core_q = links.to(near_q.at[:, pair_lanes], w_heads.at[near_rows, :q_cols], 1)
    core_kv = links.to(near_kv.at[1 - core], w_heads.at[near_rows, q_cols:], 1)
    near_copies = [
        links.here(near_q.at[:, lanes(core, q_cols)], w_heads.at[near_rows, :q_cols]),
        links.here(near_kv.at[core], w_heads.at[near_rows, q_cols:]),
    ]
    for copy in near_copies:
        copy.wait()
    y_near, z_near = (
        links.to(w_heads.at[near_rows], w_heads.at[near_rows], 0, m) for m in (1, 2)
    )
    core_q.wait_recv()
    core_kv.wait_recv()
    y_far, z_far = (
        links.to(w_heads.at[far_rows], w_heads.at[far_rows], 0, m) for m in (1, 2)
    )
    ff_across = [
        links.to(ref.at[mine, lanes(other_chip, 2 * ff_cols)], near, 2)
        for ref, near in ((gate_ref, near_gate), (up_ref, near_up))
    ]

    for copy in here:
        copy.wait()
    for copy in gain_copies:
        copy.wait_recv()
    gains_ref[...] = gains[...]
    norm_rows(x_all, norm1, gains, 0, shard * tokens, tokens)
    x_beside.wait_recv()
    norm_rows(x_all, norm1, gains, 0, (shard ^ 1) * tokens, tokens)

    y_near.wait_recv()
    y_far.wait_recv()
    z_forward = [
        links.to(w_heads.at[r], w_heads.at[r], 0, 2)
        for r in (rows_from(2, 1), rows_from(3, 1))
    ]
    x_core = []
    for i in range(2):
        x_across[i].wait_recv()
        got = pl.ds(pl.multiple_of((shard ^ 2) * tokens + i * half, half), half)
        x_core.append(links.to(x_all.at[got], x_all.at[got], 1))
        norm_rows(x_all, norm1, gains, 0, (shard ^ 2) * tokens + i * half, half)
    for i in range(2):
        x_core[i].wait_recv()
        norm_rows(x_all, norm1, gains, 0, (shard ^ 3) * tokens + i * half, half)
    norm1_out = links.here(norm1, norm1_ref)
    w_beside_ff = [
        links.to(ref.at[:, lanes(pair_shard, ff_cols)], w_ff_ref.at[own_w, cols], 1)
        for ref, cols in (
            (gate_ref, slice(0, ff_cols)),
            (up_ref, slice(ff_cols, 2 * ff_cols)),
        )
    ]
    cot_beside = links.to(cot_ref, cot_all_ref.at[block(shard)], 1)

    for copy in w_beside + [z_near, z_far] + z_forward:
        copy.wait_recv()
    w_heads_out = links.here(w_heads, w_heads_ref)

    def project(b, carry):
        r = pl.ds(pl.multiple_of(b * tokens, tokens), tokens)
        pre[r, :] = matmul(norm1[r, :], w_heads[...])
        return carry

    lax.fori_loop(0, S, project, 0)

    for copy in ff_across:
        copy.wait_recv()
    pair_ff = lanes(1 - core, ff_cols)
    ff_parts = ((near_gate, slice(0, ff_cols)), (near_up, slice(ff_cols, 2 * ff_cols)))
    ff_core = [
        links.to(near.at[:, pair_ff], w_ff_ref.at[near_rows, cols], 1)
        for near, cols in ff_parts
    ]
    ff_here = [
        links.here(near.at[:, lanes(core, ff_cols)], w_ff_ref.at[near_rows, cols])
        for near, cols in ff_parts
    ]
    cot_across = links.to(cot_ref, cot_all_ref.at[block(shard)], 2)

    kv = pre[:, q_cols:]
    kv = (kv * table_ref[2] + turned(kv) * table_ref[3]).astype(BF)
    heads_ref[:, q_cols:] = kv
    kv = kv.astype(F32)
    swapped = pltpu.roll(kv, HD, 1)
    kk_ref[...] = both(kv, swapped).astype(BF)
    vv_ref[...] = both(swapped, jnp.ones_like(kv)).astype(BF)

    for copy in ff_here:
        copy.wait()
    ff_y = [links.to(w_ff_ref.at[near_rows], w_ff_ref.at[near_rows], 0, 1)]
    ff_z = [links.to(w_ff_ref.at[near_rows], w_ff_ref.at[near_rows], 0, 2)]
    for copy in ff_core:
        copy.wait_recv()
    ff_y.append(links.to(w_ff_ref.at[far_rows], w_ff_ref.at[far_rows], 0, 1))
    ff_z.append(links.to(w_ff_ref.at[far_rows], w_ff_ref.at[far_rows], 0, 2))

    def attend_rows(i):
        q_rows_i = slice(i * tokens, (i + 1) * tokens)
        seen = (i + 1) * tokens

        def pair_step(j, carry):
            cols = pl.ds(pl.multiple_of(j * LANES, LANES), LANES)
            q = pre[q_rows_i, cols]
            q = q * table_ref[0, q_rows_i] + turned(q) * table_ref[1, q_rows_i]
            q = (q.astype(BF).astype(F32) * HD**-0.5).astype(BF)
            heads_ref[q_rows_i, cols] = q
            scores = matmul_right_t(two_heads(q), kk_ref[:seen])
            scores = causal_mask(scores, i * tokens)
            peak = jnp.max(scores, axis=-1, keepdims=True)
            exps = jnp.exp(scores - peak).astype(BF)
            out = matmul(exps, vv_ref[:seen])
            first, second = out[:tokens], out[tokens:]
            first_r, second_r = pltpu.roll(first, HD, 1), pltpu.roll(second, HD, 1)
            total = both(first_r, second)
            mixed_ref[q_rows_i, cols] = (both(first, second_r) / total).astype(BF)
            peaks = [
                jnp.broadcast_to(p, (tokens, LANES)) for p in (peak[:tokens], peak[tokens:])
            ]
            log_ref[q_rows_i, cols] = both(*peaks) + jnp.log(total)
            return carry

        lax.fori_loop(0, q_cols // LANES, pair_step, 0)

    def out_term(index):
        r = block(index)

        def step(j, carry):
            cols = pl.ds(pl.multiple_of(j * 512, 512), 512)
            term[:, cols] = matmul(mixed_ref[r, :], wo_ref[:, cols])
            return carry

        lax.fori_loop(0, model // 512, step, 0)

    def attend_block(index):
        for i in range(S):
            pl.when(index == i)(functools.partial(attend_rows, i))

    attend_block(shard ^ 3)
    out_term(shard ^ 3)
    far_out[...] = term[...].astype(BF)
    far = links.to(far_out, far_in, 1)
    attend_block(shard ^ 2)
    out_term(shard ^ 2)
    far.wait_recv()
    across = []
    for i in range(2):
        r = slice(i * half, (i + 1) * half)
        across_out[r] = (term[r] + far_in[r].astype(F32)).astype(BF)
        across.append(links.to(across_out.at[r], across_in.at[r], 2))
    attend_block(shard ^ 1)
    out_term(shard ^ 1)
    beside_out[...] = term[...].astype(BF)
    beside = links.to(beside_out, beside_in, 1)
    for copy in ff_y:
        copy.wait_recv()
    ff_forward = [
        links.to(w_ff_ref.at[r], w_ff_ref.at[r], 0, 2)
        for r in (rows_from(2, 1), rows_from(3, 1))
    ]
    attend_block(shard)
    out_term(shard)
    beside.wait_recv()
    term[...] += x_ref[...].astype(F32) + beside_in[...].astype(F32)
    n2_across, n2_beside, n2_here = [], [], []
    for i in range(2):
        r = slice(i * half, (i + 1) * half)
        across[i].wait_recv()
        mid_ref[r] = term[r] + across_in[r].astype(F32)
        norm_rows(mid_ref, norm2, gains, 1, i * half, half)
        n2_across.append(links.to(norm2.at[r], norm2_ref.at[own_rows[i]], 2))
        n2_beside.append(links.to(norm2.at[r], norm2_ref.at[own_rows[i]], 1))
        n2_here.append(links.here(norm2.at[r], norm2_ref.at[own_rows[i]]))
    n2_core = []
    for i in range(2):
        n2_across[i].wait_recv()
        got = pl.ds(pl.multiple_of((shard ^ 2) * tokens + i * half, half), half)
        n2_core.append(links.to(norm2_ref.at[got], norm2_ref.at[got], 1))
    cot_across.wait_recv()
    got = block(shard ^ 2)
    cot_core = links.to(cot_all_ref.at[got], cot_all_ref.at[got], 1)
    for copy in (
        w_beside_ff + [cot_beside] + ff_z + ff_forward + n2_beside + n2_core + [cot_core]
    ):
        copy.wait_recv()
    for copy in here_late + n2_here + [norm1_out, w_heads_out]:
        copy.wait()
    links.close()


def front(x, cot, gains, wq, wk, wv, wo, gate, up, tables):
    tokens, model = x.shape
    seq_len, rows = S * tokens, wq.shape[0]
    q_cols, ff_cols = wq.shape[1] // S, gate.shape[1] // S
    width, q_rows = q_cols + LANES, rows // 4
    shape = jax.ShapeDtypeStruct
    chip_ff = (q_rows, 2 * ff_cols)
    row_block = pltpu.VMEM((tokens, model), BF)
    return pl.pallas_call(
        front_kernel,
        out_shape=(
            shape((seq_len, model), BF),
            shape((seq_len, width), BF),
            shape((seq_len, q_cols), F32),
            shape((seq_len, q_cols), BF),
            shape((S * rows, width), BF),
            shape((tokens, model), F32),
            shape((seq_len, model), BF),
            shape((S * rows, 2 * ff_cols), BF),
            shape((seq_len, model), BF),
            shape((S, 16, rows), BF),
        ),
        in_specs=[VMEM, ANY, VMEM, ANY, VMEM, VMEM, VMEM, ANY, ANY, VMEM],
        out_specs=[ANY, VMEM, VMEM, VMEM, ANY, VMEM, ANY, ANY, ANY, VMEM],
        scratch_shapes=[
            pltpu.VMEM((seq_len, model), BF),
            pltpu.VMEM((S, 16, rows), BF),
            pltpu.VMEM((S, rows, LANES), BF),
            pltpu.VMEM((q_rows, 2 * q_cols), BF),
            pltpu.VMEM((2, q_rows, LANES), BF),
            pltpu.VMEM(chip_ff, BF),
            pltpu.VMEM(chip_ff, BF),
            pltpu.VMEM((S * rows, width), BF),
            pltpu.VMEM((seq_len, model), BF),
            pltpu.VMEM((seq_len, width), F32),
            pltpu.VMEM((seq_len, LANES), BF),
            pltpu.VMEM((seq_len, LANES), BF),
            row_block,
            row_block,
            row_block,
            row_block,
            row_block,
            row_block,
            pltpu.VMEM((tokens, model), F32),
            row_block,
            pltpu.SemaphoreType.DMA((48,)),
            pltpu.SemaphoreType.DMA((48,)),
            pltpu.SemaphoreType.DMA((24,)),
        ],
        compiler_params=pltpu.CompilerParams(
            collective_id=0, has_side_effects=True, vmem_limit_bytes=60 * 2**20
        ),
    )(x, cot, gains, wq, wk, wv, wo, gate, up, tables)


def by_rows(count, body, step=16):
    if count % step:
        body(pl.ds(0, count))
        return

    def one(i, carry):
        body(pl.ds(pl.multiple_of(i * step, step), step))
        return carry

    lax.fori_loop(0, count // step, one, 0)


class Scatter:
    def __init__(self, links, term, far_in, across_out, across_in, beside_in):
        self.links, self.term = links, term
        self.far_in, self.across_out = far_in, across_out
        self.across_in, self.beside_in = across_in, beside_in
        self.tokens = far_in.shape[0]
        self.half = self.tokens // 2
        self.starts = [
            [
                pl.multiple_of((links.shard ^ mask) * self.tokens + extra, 16)
                for extra in (0, self.half)
            ]
            for mask in range(S)
        ]

    def rows(self, mask, part=None):
        if part is None:
            return pl.ds(self.starts[mask][0], self.tokens)
        return pl.ds(self.starts[mask][part], self.half)

    def send_far(self):
        self.far = self.links.to(self.term.at[self.rows(3)], self.far_in, 1)

    def send_across(self):
        self.far.wait_recv()
        self.across = []
        base = self.starts[2][0]
        for i in range(2):

            def add(rows):
                start = i * self.half + rows.start
                here = pl.ds(pl.multiple_of(start, 16), rows.size)
                there = pl.ds(pl.multiple_of(base + start, 16), rows.size)
                total = self.term[there, :].astype(F32)
                total += self.far_in[here, :].astype(F32)
                self.across_out[here, :] = total.astype(BF)

            by_rows(self.half, add)
            part = pl.ds(i * self.half, self.half)
            self.across.append(
                self.links.to(self.across_out.at[part], self.across_in.at[part], 2)
            )

    def send_beside(self):
        self.beside = self.links.to(self.term.at[self.rows(1)], self.beside_in, 1)

    def finish(self, i, use):
        if i == 0:
            self.beside.wait_recv()
        self.across[i].wait_recv()
        base = self.starts[0][0]

        def one(rows):
            start = i * self.half + rows.start
            here = pl.ds(pl.multiple_of(start, 16), rows.size)
            there = pl.ds(pl.multiple_of(base + start, 16), rows.size)
            total = self.term[there, :].astype(F32)
            total += self.beside_in[here, :].astype(F32)
            total += self.across_in[here, :].astype(F32)
            use(here, total)

        by_rows(self.half, one)

    def release(self):
        for copy in [self.far, self.beside] + self.across:
            self.links.sent(copy)


STEPS = {
    "tff2": ("down0", "down1"),
    "pout": ("ff3",),
    "mix": ("ff2",),
    "gath1": ("down0",),
    "att0": ("ff1",),
    "att3": ("ff2", "ff3", "down1"),
    "w_rf3": ("down0",),
    "heads": ("ff1", "ff0"),
    "last": (
        ("ff2", "out0", "ff3", "down1", "ff0", "ff1", "heads0", "out0", "heads1")
        + ("heads0", "ff0", "out0", "heads1", "heads0", "heads1")
    ),
}


class Flow:
    def __init__(self, links, order, arrive, sends):
        self.links, self.arrive, self.sends = links, list(arrive), list(sends)
        self.bits = len(self.arrive)
        self.order = [b for b in order if b < self.bits]
        self.order += list(range(len(order), self.bits))
        self.left = list(range(self.bits - 1, -1, -1))
        self.sides = [(links.replica >> b) % 2 for b in range(self.bits)]
        self.others = [1 - side for side in self.sides]
        self.at = 0
        self.done = False

    def begin(self, term):
        self.parts = [term]
        self.step()

    def pick(self, bit, side):
        where = (slice(None),) * self.left.index(bit) + (side,)
        return [part.at[where] for part in self.parts]

    def step(self):
        bit = self.order[self.at]
        mine = self.sides[bit]
        if self.at:
            self.copy.wait_recv()
        other = self.pick(bit, self.others[bit])
        source = other[0]
        if self.at:
            source = self.sends[self.at - 1]
            self.add(other, source, len(self.left) - 1)
        self.copy = self.links.to(source, self.arrive[self.at], 0, 1 << bit)
        self.parts = self.pick(bit, mine) + [self.arrive[self.at]]
        self.left.remove(bit)
        self.at += 1

    def advance(self):
        if self.at < self.bits:
            self.step()
        elif not self.done:
            self.done = True
            self.conclude(self)

    def end(self, target):
        self.copy.wait_recv()
        self.add(self.parts, target, 0)

    def add(self, parts, target, free):
        ways = list(itertools.product(range(2), repeat=free))
        rest = parts[0].shape[free:]
        jobs = [(way, part) for way in ways for part in parts]

        def inner(fetch, sems):
            copies = []
            for n, (way, part) in enumerate(jobs):
                source = part.at[way] if way else part
                copy = pltpu.make_async_copy(source, fetch.at[n], sems.at[n])
                copy.start()
                copies.append(copy)
            for w, way in enumerate(ways):
                first = w * len(parts)
                for k in range(len(parts)):
                    copies[first + k].wait()
                leads = [()] if len(rest) == 2 else [(g,) for g in range(rest[0])]
                for lead in leads:

                    def one(rows):
                        total = fetch[(first,) + lead + (rows,)].astype(F32)
                        for k in range(1, len(parts)):
                            more = fetch[(first + k,) + lead + (rows,)]
                            total += more.astype(F32)
                        target[way + lead + (rows,)] = total.astype(target.dtype)

                    by_rows(rest[-2], one)

        pl.run_scoped(
            inner,
            pltpu.VMEM((len(jobs),) + tuple(rest), BF),
            pltpu.SemaphoreType.DMA((len(jobs),)),
        )


def bits_of(index, count):
    return tuple((index >> b) & 1 for b in reversed(range(count.bit_length() - 1)))


def turn(source, cols, target):
    rows = source.shape[0]
    for i in range(0, rows, 256):
        part = source[i : i + 256, cols]
        target[:, i : i + 256] = part.astype(F32).T.astype(BF)


def produce(left_t, right, first, size, stage, replicas, lead=(), tile=256):
    share = left_t.shape[0] // replicas

    def one(t, carry):
        start = pl.multiple_of(t * tile, LANES)
        cols = pl.ds(pl.multiple_of(first + start, LANES), tile)
        result = matmul(left_t[...], right[:, cols])
        for r in range(replicas):
            where = bits_of(r, replicas) + lead + (slice(None), pl.ds(start, tile))
            stage[where] = result[r * share : (r + 1) * share].astype(BF)
        return carry

    lax.fori_loop(0, size // tile, one, 0)


def stream(count, copies_of, use):
    for copy in copies_of(0, 0):
        copy.start()

    def one(t, carry):
        slot = t % 2

        @pl.when(t + 1 < count)
        def _():
            for copy in copies_of(t + 1, 1 - slot):
                copy.start()

        for copy in copies_of(t, slot):
            copy.wait()
        use(t, slot)
        return carry

    lax.fori_loop(0, count, one, 0)


def norm_back_rows(grad, values, gain_row):
    scale = rms_scale(values)
    weighted = grad * gain_row
    mean = jnp.mean(weighted * values, axis=-1, keepdims=True)
    return scale * weighted - values * (scale * scale * scale * mean)


def rear_kernel(
    norm2_hbm, cot_hbm, w_ff_hbm, w_down_hbm, norm1_hbm, mixed_hbm, w_out_hbm, heads_hbm, logs_hbm,
    table_hbm, w_heads_hbm, mid_ref, cot_ref, x_ref, gain_ref,
    output_ref, input_grad_ref, grad_out_ref, grad_down_ref, pieces_ff, pieces_heads, *others,
):
    shard, replica = lax.axis_index("shard"), lax.axis_index("replica")
    tokens, model = mid_ref.shape
    seq_len = S * tokens
    ff_cols, rows = w_down_hbm.shape[0], model // S
    width = heads_hbm.shape[1]
    q_cols = width - LANES
    replicas = model // (S * pieces_ff.shape[1])
    bits = replicas.bit_length() - 1
    share, share_down = pieces_ff.shape[1], grad_down_ref.shape[0]
    half, half_model = tokens // 2, model // 2
    others = list(others)

    def take(count):
        taken = others[:count]
        del others[:count]
        return taken

    hbm = {name: take(1 + bits) for name in ("ff", "down", "out", "heads")}
    cot_all, term, far_in, across_out, across_in, beside_in, grad_mid, grad_mid_b = take(8)
    sends = {name: take(bits) for name in ("ff", "down", "out", "heads")}
    send, recv, local, slots = take(4)
    links = Links(shard, replica, send, recv, local)
    other_chip = 1 - shard // 2

    def flow(name, order, index=None):
        pick = (lambda ref: ref) if index is None else (lambda ref: ref.at[index])
        made = Flow(
            links,
            order,
            [pick(ref) for ref in hbm[name][1:]],
            [pick(ref) for ref in sends[name][:-1]],
        )
        made.term, made.last = pick(hbm[name][0]), pick(sends[name][-1])
        return made

    ff_order = ((0, 1, 2), (0, 1, 2), (1, 0, 2), (0, 1, 2))
    flows_ff = [flow("ff", ff_order[m], m) for m in range(S)]
    flows_down = [flow("down", order, i) for i, order in enumerate(((0, 1, 2), (1, 2, 0)))]
    flow_out = flow("out", (0, 1, 2))
    flows_heads = [flow("heads", (0, 1, 2), i) for i in range(2)]
    flows = {"out0": flow_out}
    for name, many in (("ff", flows_ff), ("down", flows_down), ("heads", flows_heads)):
        flows.update({f"{name}{i}": made for i, made in enumerate(many)})
    finals, finals_here = [], []

    def deliver(piece, pieces, mask):
        if mask:
            finals.append(links.to(piece, pieces.at[mask], mask))
        else:
            finals_here.append(links.here(piece, pieces.at[mask]))

    def end_ff(mask, made):
        made.end(made.last)
        deliver(made.last, pieces_ff, mask)

    def end_down(i, made):
        made.end(made.last)
        cols = pl.ds(i * half_model, half_model)
        finals_here.append(links.here(made.last, grad_down_ref.at[:, cols]))

    def end_out(made):
        made.end(made.last)
        finals_here.append(links.here(made.last, grad_out_ref))

    def end_heads(i, made):
        made.end(made.last)
        for n, mask in enumerate(((3, 2), (1, 0))[i]):
            deliver(made.last.at[n], pieces_heads, mask)

    for i in range(S):
        flows_ff[i].conclude = functools.partial(end_ff, i)
    for i in range(2):
        flows_down[i].conclude = functools.partial(end_down, i)
        flows_heads[i].conclude = functools.partial(end_heads, i)
    flow_out.conclude = end_out

    def pump(point):
        for name in STEPS.get(point, ()):
            flows[name].advance()

    greet(shard, replica, (1, 2, 3), [1 << b for b in range(bits)])
    gain_one, gain_two = (
        jnp.concatenate(
            [gain_ref[j, i : i + 1, :].astype(F32) for j in range(S)], axis=1
        )
        for i in range(2)
    )
    sums = Scatter(links, term, far_in, across_out, across_in, beside_in)
    ended = []

    def first_half(norm2, hidden, grad_ff):
        norm2_in = links.here(norm2_hbm, norm2)
        cot_in = links.here(cot_hbm, cot_all)

        tile = 256
        tiles = [(i, min(tile, ff_cols - i)) for i in range(0, ff_cols, tile)]

        def over_tiles(copies_of, use):
            for copy in copies_of(0):
                copy.start()
            for t, (start, size) in enumerate(tiles):
                if t + 1 < len(tiles):
                    for copy in copies_of(t + 1):
                        copy.start()
                for copy in copies_of(t):
                    copy.wait()

                def block(b, carry):
                    use(pl.ds(pl.multiple_of(b * 512, 512), 512), start, size, t % 2)
                    return carry

                lax.fori_loop(0, seq_len // 512, block, 0)

        def gate_up(gates, ups):
            def copies_of(t):
                start, size = tiles[t]
                slot = t % 2
                cols = slice(start, start + size)
                up_cols = slice(ff_cols + start, ff_cols + start + size)
                return [
                    pltpu.make_async_copy(*pair, slots.at[slot, n])
                    for n, pair in enumerate(
                        (
                            (w_ff_hbm.at[:, cols], gates.at[slot, :, :size]),
                            (w_ff_hbm.at[:, up_cols], ups.at[slot, :, :size]),
                        )
                    )
                ]

            def use(r, start, size, slot):
                gate = matmul(norm2[r, :], gates[slot, :, :size])
                up = matmul(norm2[r, :], ups[slot, :, :size])
                silu = gate * (1.0 / (1.0 + jnp.exp(-gate)))
                hidden[r, start : start + size] = (silu * up).astype(BF)
                grad_ff[r, start : start + size] = gate.astype(BF)
                grad_ff[r, ff_cols + start : ff_cols + start + size] = up.astype(BF)

            norm2_in.wait()
            over_tiles(copies_of, use)

        weight_tile = pltpu.VMEM((2, model, tile), BF)
        pl.run_scoped(gate_up, weight_tile, weight_tile)
        cot_in.wait()

        def down_terms(left_t, stage):
            turn(hidden, slice(None), left_t)
            for i in range(2):
                produce(left_t, cot_all, i * half_model, half_model, stage, replicas)
                links.here(stage, flows_down[i].term).wait()
                flows_down[i].begin(flows_down[i].term)

        pl.run_scoped(
            down_terms,
            pltpu.VMEM((ff_cols, seq_len), BF),
            pltpu.VMEM((2,) * bits + (share_down, half_model), BF),
        )

        def hidden_grads(downs):
            def copies_of(t):
                start, size = tiles[t]
                slot = t % 2
                return [
                    pltpu.make_async_copy(
                        w_down_hbm.at[slice(start, start + size)],
                        downs.at[slot, :size],
                        slots.at[slot, 0],
                    )
                ]

            def use(r, start, size, slot):
                grad = matmul_right_t(cot_all[r, :], downs[slot, :size])
                cols = slice(start, start + size)
                up_cols = slice(ff_cols + start, ff_cols + start + size)
                gate, up = grad_ff[r, cols].astype(F32), grad_ff[r, up_cols].astype(F32)
                sigmoid = 1.0 / (1.0 + jnp.exp(-gate))
                slope = sigmoid * (1.0 + gate * (1.0 - sigmoid))
                grad_ff[r, cols] = (grad * up * slope).astype(BF)
                grad_ff[r, up_cols] = (grad * gate * sigmoid).astype(BF)

            over_tiles(copies_of, use)

        pl.run_scoped(hidden_grads, pltpu.VMEM((2, tile, model), BF))
        pump("hid")

        def norm_terms(chip):
            def inner(tiles):
                r = pl.ds(pl.multiple_of(chip * 2 * tokens, 2 * tokens), 2 * tokens)

                def copies_of(t, slot):
                    part = pl.ds(pl.multiple_of(t * 256, 256), 256)
                    return [
                        pltpu.make_async_copy(
                            w_ff_hbm.at[part], tiles.at[slot], slots.at[slot, 0]
                        )
                    ]

                def use(t, slot):
                    cols = pl.ds(pl.multiple_of(t * 256, 256), 256)
                    product = matmul_right_t(grad_ff[r, :], tiles[slot])
                    term[r, cols] = product.astype(BF)

                stream(model // 256, copies_of, use)

            pl.run_scoped(inner, pltpu.VMEM((2, 256, 2 * ff_cols), BF))

        norm_terms(other_chip)
        sums.send_far()
        pump("far")

        def ff_terms(left_t, stages):
            copies = {}

            def launch(n):
                copies[n][0].wait()
                if copies[n][1] is not flows_ff[0]:
                    copies[n][1].begin(copies[n][1].term)

            for n, mask in enumerate((3, 2, 1, 0)):
                cols = pl.ds(pl.multiple_of((shard ^ mask) * rows, rows), rows)
                turn(norm2, cols, left_t)
                if n:
                    launch(n - 1)
                produce(left_t, grad_ff, 0, 2 * ff_cols, stages.at[n % 2], replicas)
                copies[n] = (
                    links.here(stages.at[n % 2], flows_ff[mask].term),
                    flows_ff[mask],
                )
                if n == 0:
                    pump("w_rf")
                    sums.send_across()
                pump(f"tff{n}")
            launch(3)

        pl.run_scoped(
            ff_terms,
            pltpu.VMEM((rows, seq_len), BF),
            pltpu.VMEM((2,) + (2,) * bits + (share, 2 * ff_cols), BF),
        )
        norm_terms(1 - other_chip)
        sums.send_beside()
        pump("near")

        def to_mid(r, grad):
            values = mid_ref[r, :]
            total = cot_ref[r, :].astype(F32)
            total += norm_back_rows(grad, values, gain_two)
            grad_mid[r, :] = total
            grad_mid_b[r, :] = total.astype(BF)

        gathered = []
        for i in range(2):
            sums.finish(i, to_mid)
            part = slice(i * half, (i + 1) * half)
            there = sums.rows(0, i)
            gathered.append(
                [
                    links.to(grad_mid_b.at[part], cot_all.at[there], 2),
                    links.to(grad_mid_b.at[part], cot_all.at[there], 1),
                    links.here(grad_mid_b.at[part], cot_all.at[there]),
                ]
            )
        sums.release()
        pump("mid")

        def out_terms(tiles):
            def copies_of(t, slot):
                part = pl.ds(pl.multiple_of(t * 256, 256), 256)
                return [
                    pltpu.make_async_copy(
                        w_down_hbm.at[:, part], tiles.at[slot], slots.at[slot, 0]
                    )
                ]

            def use(t, slot):
                cols = pl.ds(pl.multiple_of(t * 256, 256), 256)
                term[:, cols] = matmul(hidden[...], tiles[slot]).astype(BF)

            stream(model // 256, copies_of, use)

        pl.run_scoped(out_terms, pltpu.VMEM((2, ff_cols, 256), BF))
        pump("pout")
        return gathered

    gathered = []
    pl.run_scoped(
        lambda *refs: gathered.extend(first_half(*refs)),
        pltpu.VMEM((seq_len, model), BF),
        pltpu.VMEM((seq_len, ff_cols), BF),
        pltpu.VMEM((seq_len, 2 * ff_cols), BF),
    )

    def second_half(mixed, w_out, heads, logs, table, w_heads, grad_mixed, grad_heads,
                    kk_ref, vv_ref, dk_ref, dv_ref):
        loads = [
            links.here(*pair)
            for pair in (
                (w_out_hbm, w_out),
                (heads_hbm, heads),
                (logs_hbm, logs),
                (table_hbm, table),
                (mixed_hbm, mixed),
                (w_heads_hbm, w_heads),
            )
        ]
        for i in range(2):
            gathered[i][1].wait_recv()
            gathered[i][2].wait()
        sums.send_far()
        sums.send_beside()
        for copy in loads:
            copy.wait()

        def mix(mask, part=None):
            r = sums.rows(mask, part)
            grad_mixed[r, :] = matmul_right_t(cot_all[r, :], w_out[...]).astype(BF)

        mix(0)
        mix(1)
        kv = heads[:, q_cols:].astype(F32)
        swapped = pltpu.roll(kv, HD, 1)
        kk_ref[...] = both(kv, swapped).astype(BF)
        vv_ref[...] = both(swapped, kv).astype(BF)
        dk_ref[...] = jnp.zeros_like(dk_ref)
        dv_ref[...] = jnp.zeros_like(dv_ref)
        pump("mix")
        forward = []
        for i in range(2):
            gathered[i][0].wait_recv()
            r = sums.rows(2, i)
            forward.append(links.to(cot_all.at[r], cot_all.at[r], 1))
            mix(2, i)
            pump(f"gath{i}")
        sums.send_across()
        flows_ff[0].begin(flows_ff[0].term)
        pump("across2")
        for i in range(2):
            forward[i].wait_recv()
            mix(3, i)

        def out_grad(left_t, stage):
            turn(mixed, slice(None), left_t)
            produce(left_t, cot_all, 0, model, stage, replicas)
            links.here(stage, flow_out.term).wait()
            flow_out.begin(flow_out.term)

        pl.run_scoped(
            out_grad,
            pltpu.VMEM((rows, seq_len), BF),
            pltpu.VMEM((2,) * bits + (share, model), BF),
        )

        def attend_rows(i):
            r = slice(i * tokens, (i + 1) * tokens)
            seen = (i + 1) * tokens

            def pair_step(j, carry):
                cols = pl.ds(pl.multiple_of(j * LANES, LANES), LANES)
                q = two_heads(heads[r, cols])
                grad = two_heads(grad_mixed[r, cols])
                log_pair = logs[r, cols]
                log_col = jnp.concatenate(
                    [log_pair[:, :1], log_pair[:, HD : HD + 1]], axis=0
                )
                mixed_pair = mixed[r, cols].astype(F32)
                product = grad.astype(F32) * jnp.concatenate([mixed_pair] * 2, axis=0)
                inner = jnp.sum(product, axis=-1, keepdims=True)
                scores = matmul_right_t(q, kk_ref[:seen])
                soft = jnp.exp(causal_mask(scores, i * tokens) - log_col)
                grad_soft = matmul_right_t(grad, vv_ref[:seen])
                grad_scores = (soft * (grad_soft - inner)).astype(BF)
                dq = matmul(grad_scores, kk_ref[:seen])
                dq = both(dq[:tokens], dq[tokens:]) * HD**-0.5
                dq = dq * table[0, r] - turned(dq) * table[1, r]
                grad_heads[r, cols] = dq.astype(BF)
                dk_ref[:seen] += matmul_left_t(grad_scores, q)
                dv_ref[:seen] += matmul_left_t(soft.astype(BF), grad)
                return carry

            lax.fori_loop(0, q_cols // LANES, pair_step, 0)

        pump("out")
        for i in range(S):
            attend_rows(i)
            pump(f"att{i}")
        dk, dv = dk_ref[...], dv_ref[...]
        dk, dv = dk + pltpu.roll(dk, HD, 1), dv + pltpu.roll(dv, HD, 1)
        dkv = both(dk, dv)
        dkv = dkv * table[2] - turned(dkv) * table[3]
        grad_heads[:, q_cols:] = dkv.astype(BF)

        def to_output(r, total):
            output_ref[r, :] = (mid_ref[r, :] + total).astype(BF)

        for i in range(2):
            sums.finish(i, to_output)
        sums.release()
        for mask in (1, 2):
            pl.semaphore_signal(
                credit.at[mask - 1],
                inc=1,
                device_id={"shard": shard ^ mask, "replica": replica},
                device_id_type=MESH_ID,
            )

        def head_terms(chip):
            r = pl.ds(pl.multiple_of(chip * 2 * tokens, 2 * tokens), 2 * tokens)

            def one(t, carry):
                cols = pl.ds(pl.multiple_of(t * 256, 256), 256)
                product = matmul_right_t(grad_heads[r, :], w_heads[cols, :])
                term[r, cols] = product.astype(BF)
                return carry

            lax.fori_loop(0, model // 256, one, 0)

        def head_grads(norm1, left_t, stages):
            norm1_in = links.here(norm1_hbm, norm1)
            head_terms(other_chip)
            pl.semaphore_wait(credit.at[0], 1)
            sums.send_far()
            norm1_in.wait()
            stage_out = []
            for i, masks in enumerate(((3, 2), (1, 0))):
                for n, mask in enumerate(masks):
                    cols = pl.ds(pl.multiple_of((shard ^ mask) * rows, rows), rows)
                    turn(norm1, cols, left_t)
                    produce(
                        left_t, grad_heads, 0, width, stages.at[i], replicas, (n,), LANES
                    )
                stage_out.append(links.here(stages.at[i], flows_heads[i].term))
                if i == 0:
                    pump("w_rf3")
                    pl.semaphore_wait(credit.at[1], 1)
                    sums.send_across()
                    stage_out[0].wait()
                    flows_heads[0].begin(flows_heads[0].term)
            stage_out[1].wait()
            flows_heads[1].begin(flows_heads[1].term)
            head_terms(1 - other_chip)
            sums.send_beside()

        pl.run_scoped(
            head_grads,
            pltpu.VMEM((seq_len, model), BF),
            pltpu.VMEM((rows, seq_len), BF),
            pltpu.VMEM((2,) + (2,) * bits + (2, share, width), BF),
        )
        pump("heads")

    credit = take(1)[0]
    pl.run_scoped(
        second_half,
        pltpu.VMEM((seq_len, q_cols), BF),
        pltpu.VMEM((q_cols, model), BF),
        pltpu.VMEM((seq_len, width), BF),
        pltpu.VMEM((seq_len, q_cols), F32),
        pltpu.VMEM((4, seq_len, LANES), F32),
        pltpu.VMEM((model, width), BF),
        pltpu.VMEM((seq_len, q_cols), BF),
        pltpu.VMEM((seq_len, width), BF),
        pltpu.VMEM((seq_len, LANES), BF),
        pltpu.VMEM((seq_len, LANES), BF),
        pltpu.VMEM((seq_len, LANES), F32),
        pltpu.VMEM((seq_len, LANES), F32),
    )

    def to_input_grad(r, grad):
        total = grad_mid[r, :]
        total += norm_back_rows(grad, x_ref[r, :].astype(F32), gain_one)
        input_grad_ref[r, :] = total.astype(BF)

    for i in range(2):
        sums.finish(i, to_input_grad)
    pump("last")
    waiting = list(flows.values())
    while waiting:
        for made in waiting:
            made.advance()
        waiting = [made for made in waiting if not made.done]
    for copy in finals:
        copy.wait_recv()
    for copy in finals_here:
        copy.wait()
    links.close()


def rear(norm2, cot_all, w_ff, w_down, norm1, mixed, w_out, heads, logs, tables, w_heads, mid, cot, x, gains, replicas):
    tokens, model = mid.shape
    seq_len, rows, ff_cols = S * tokens, model // S, w_down.shape[0]
    width = heads.shape[1]
    bits = replicas.bit_length() - 1
    share, share_down = rows // replicas, ff_cols // replicas
    shape = jax.ShapeDtypeStruct
    rests = {
        "ff": ((S,), (share, 2 * ff_cols), BF),
        "down": ((2,), (share_down, model // 2), F32),
        "out": ((), (share, model), F32),
        "heads": ((2,), (2, share, width), BF),
    }
    work, sends = [], []
    for many, rest, last in rests.values():
        work += [shape(many + (2,) * bits + rest, BF)]
        work += [shape(many + (2,) * n + rest, BF) for n in reversed(range(bits))]
        sends += [
            pltpu.VMEM(many + (2,) * n + rest, BF) for n in reversed(range(bits - 1))
        ]
        sends += [pltpu.VMEM(many + rest, last)]
    outs = (
        shape((tokens, model), BF),
        shape((tokens, model), BF),
        shape((share, model), F32),
        shape((share_down, model), F32),
        shape((S, share, 2 * ff_cols), BF),
        shape((S, share, width), BF),
    )
    row_block = pltpu.VMEM((tokens, model), BF)
    result = pl.pallas_call(
        rear_kernel,
        out_shape=outs + tuple(work),
        in_specs=[ANY] * 11 + [VMEM] * 4,
        out_specs=[VMEM] * 2 + [ANY] * (4 + len(work)),
        scratch_shapes=[
            pltpu.VMEM((seq_len, model), BF),
            pltpu.VMEM((seq_len, model), BF),
            row_block,
            row_block,
            row_block,
            row_block,
            pltpu.VMEM((tokens, model), F32),
            row_block,
        ]
        + sends
        + [
            pltpu.SemaphoreType.DMA((96,)),
            pltpu.SemaphoreType.DMA((96,)),
            pltpu.SemaphoreType.DMA((48,)),
            pltpu.SemaphoreType.DMA((2, 3)),
            pltpu.SemaphoreType.REGULAR((2,)),
        ],
        compiler_params=pltpu.CompilerParams(
            collective_id=1, has_side_effects=True, vmem_limit_bytes=62 * 2**20
        ),
    )(norm2, cot_all, w_ff, w_down, norm1, mixed, w_out, heads, logs, tables, w_heads, mid, cot, x, gains)
    return result[: len(outs)]


def on_device(
    inputs, cotangent, gain_attn, w_query, w_key, w_value, w_output, gain_mlp, w_gate, w_up, w_down
):
    shard, replica = lax.axis_index("shard"), lax.axis_index("replica")
    x, cot = inputs[0], cotangent[0]
    tables = jnp.asarray(rope_tables(S * x.shape[0]))
    gains = jnp.concatenate(
        [jnp.stack([gain_attn, gain_mlp]), jnp.zeros((14, w_query.shape[0]), BF)]
    )
    norm1, heads, logs, mixed, w_heads, mid, norm2, w_ff, cot_all, gains = front(
        x, cot, gains, w_query, w_key, w_value, w_output, w_gate, w_up, tables
    )
    output, input_grad, grad_output, grad_down, pieces_ff, pieces_heads = rear(
        norm2, cot_all, w_ff, w_down, norm1, mixed, w_output, heads, logs, tables,
        w_heads, mid, cot, x, gains, lax.axis_size("replica"),
    )
    grads, (grad_gain_two, grad_gain_one), moved = finish(
        (pieces_ff, pieces_heads),
        ((w_gate, w_up), (w_query, w_key, w_value)),
        (gain_mlp, gain_attn),
        (output, input_grad, grad_output, grad_down),
        shard,
        replica,
    )
    grad_gate, grad_up, grad_query, grad_key, grad_value = grads
    output, input_grad, grad_output, grad_down = moved
    return (
        output[None],
        input_grad[None],
        grad_gain_one,
        grad_query,
        grad_key,
        grad_value,
        grad_output,
        grad_gain_two,
        grad_gate,
        grad_up,
        grad_down,
    )


def solution(mesh):
    placed = (
        P("replica", "shard", None),
        P("replica", "shard", None),
        P("shard"),
        P("shard", None),
        P("shard", None),
        P("shard", None),
        P("shard", None),
        P("shard"),
        P("shard", None),
        P("shard", None),
        P("shard", None),
    )
    both_axes = ("shard", "replica")
    return jax.shard_map(
        on_device,
        mesh=mesh,
        in_specs=placed,
        out_specs=(
            P("replica", "shard", None),
            P("replica", "shard", None),
            P(both_axes),
            P(both_axes, None),
            P(both_axes, None),
            P(both_axes, None),
            P(both_axes, None),
            P(both_axes),
            P(both_axes, None),
            P(both_axes, None),
            P(both_axes, None),
        ),
        check_vma=False,
    )
```

```python
import functools
import itertools

import jax
import jax.numpy as jnp
import numpy as np
from jax import lax
from jax.experimental import pallas as pl
from jax.experimental.pallas import tpu as pltpu
from jax.sharding import PartitionSpec as P

H = 32
KV = 4
HD = 64
EPS = 1e-05
THETA = 10000.0
S = 4
BF = jnp.bfloat16
F32 = jnp.float32
LANES = 128
QB = 256


def matmul(left, right):
    return jnp.dot(left, right, preferred_element_type=F32)


def matmul_left_t(left, right):
    return lax.dot_general(
        left, right, (((0,), (0,)), ((), ())), preferred_element_type=F32
    )


def matmul_right_t(left, right):
    return lax.dot_general(
        left, right, (((1,), (1,)), ((), ())), preferred_element_type=F32
    )


def rms_scale(values):
    return lax.rsqrt(jnp.mean(values * values, axis=-1, keepdims=True) + EPS)


def finish_kernel(groups, moved, place_ref, *refs):
    refs = list(refs)

    def take(count):
        taken = refs[:count]
        del refs[:count]
        return taken

    many = [len(widths) for widths in groups]
    pieces, gains = take(len(groups)), take(len(groups))
    weights = [take(n) for n in many]
    sources = take(moved)
    outs, gain_outs = [take(n) for n in many], take(len(groups))
    targets = take(moved)
    held, staged = [take(n) for n in many], take(moved)
    sems = refs[0]
    shard, replica = place_ref[0], place_ref[1]
    copies = []

    def start(source, target):
        copies.append(pltpu.make_async_copy(source, target, sems.at[len(copies)]))
        copies[-1].start()

    for mine, kept in zip(weights, held):
        for weight, here in zip(mine, kept):
            rows = here.shape[0]
            start(weight.at[pl.ds(pl.multiple_of(replica * rows, rows), rows)], here)
    loads = list(copies)
    for source, stage in zip(sources, staged):
        start(source, stage)
    stages = copies[len(loads) :]
    for copy in loads:
        copy.wait()
    for copy, stage, target in zip(stages, staged, targets):
        copy.wait()
        start(stage, target)
    for g, widths in enumerate(groups):
        total = jnp.zeros(gain_outs[g].shape, F32)
        for mask in range(S):
            piece = pieces[g].at[mask]
            owner = shard ^ mask
            begin = 0
            for width, weight, out in zip(widths, held[g], outs[g]):
                if width % LANES == 0:
                    cols = pl.ds(pl.multiple_of(owner * width, LANES), width)
                    part = piece[:, begin : begin + width].astype(F32)
                    out[:, cols] = part
                else:
                    base = begin // LANES * LANES
                    part = piece[:, base : base + LANES].astype(F32)
                    lane = lax.broadcasted_iota(jnp.int32, part.shape, 1) // HD
                    side = owner % 2
                    part = jnp.where(
                        side == (begin - base) // HD, part, pltpu.roll(part, HD, 1)
                    )
                    part = jnp.where(lane == side, part, 0.0)
                    cols = pl.ds(pl.multiple_of(owner // 2 * LANES, LANES), LANES)
                    out[:, cols] = jnp.where(lane == side, part, out[:, cols])
                total += jnp.sum(
                    part * weight[:, cols].astype(F32), axis=1, keepdims=True
                )
                begin += width
        gain_outs[g][...] = total / gains[g][...]
    for copy in copies[len(loads) + moved :]:
        copy.wait()


def finish(pieces, weights, gains, moved, shard, replica):
    rows = pieces[0].shape[1]
    groups = [tuple(w.shape[1] // S for w in mine) for mine in weights]
    flat = [w for mine in weights for w in mine]
    own_gains = [
        lax.dynamic_slice_in_dim(gain, replica * rows, rows, 0)
        .astype(F32)
        .reshape(rows, 1)
        for gain in gains
    ]
    shapes = [jax.ShapeDtypeStruct((rows, w.shape[1]), F32) for w in flat]
    shapes += [jax.ShapeDtypeStruct((rows, 1), F32)] * len(groups)
    shapes += [jax.ShapeDtypeStruct(a.shape, a.dtype) for a in moved]
    vmem, hbm = (pl.BlockSpec(memory_space=m) for m in (pltpu.VMEM, pl.ANY))
    held = len(flat) + len(groups)
    result = pl.pallas_call(
        functools.partial(finish_kernel, groups, len(moved)),
        out_shape=shapes,
        in_specs=[pl.BlockSpec(memory_space=pltpu.SMEM)]
        + [vmem] * (2 * len(groups))
        + [hbm] * (len(flat) + len(moved)),
        out_specs=[vmem] * held + [hbm] * len(moved),
        scratch_shapes=[pltpu.VMEM((rows, w.shape[1]), BF) for w in flat]
        + [pltpu.VMEM(a.shape, a.dtype) for a in moved]
        + [pltpu.SemaphoreType.DMA((len(flat) + 2 * len(moved),))],
        compiler_params=pltpu.CompilerParams(vmem_limit_bytes=62 * 2**20),
    )(
        jnp.stack([shard, replica]).astype(jnp.int32),
        *pieces,
        *own_gains,
        *flat,
        *moved,
    )
    return (
        result[: len(flat)],
        [gain.reshape(rows) for gain in result[len(flat) : held]],
        result[held:],
    )


def rope_tables(seq_len):
    half = HD // 2
    freq = THETA ** (-2.0 * np.arange(half, dtype=np.float64) / HD)
    angles = np.arange(seq_len, dtype=np.float64)[:, None] * freq[None, :]
    cos, sin = np.cos(angles), np.sin(angles)
    one, zero = np.ones((seq_len, HD)), np.zeros((seq_len, HD))
    cos_head = np.concatenate([cos, cos], 1)
    sin_head = np.concatenate([-sin, sin], 1)
    tables = [
        np.concatenate([cos_head, cos_head], 1),
        np.concatenate([sin_head, sin_head], 1),
        np.concatenate([cos_head, one], 1),
        np.concatenate([sin_head, zero], 1),
    ]
    return np.stack(tables).astype(np.float32)


def turned(values):
    lane = lax.broadcasted_iota(jnp.int32, values.shape, 1)
    return jnp.where(
        lane % HD < HD // 2,
        pltpu.roll(values, LANES - HD // 2, 1),
        pltpu.roll(values, HD // 2, 1),
    )


def both(first, second):
    lane = lax.broadcasted_iota(jnp.int32, first.shape, 1)
    return jnp.where(lane < HD, first, second)


def two_heads(pair):
    zero = jnp.zeros_like(pair)
    return jnp.concatenate([both(pair, zero), both(zero, pair)], axis=0)


def causal_mask(scores, first_row):
    block = scores.shape[0] // 2
    last = scores[:, first_row:]
    row = lax.broadcasted_iota(jnp.int32, last.shape, 0) % block
    col = lax.broadcasted_iota(jnp.int32, last.shape, 1)
    last = jnp.where(col <= row, last, -1e30)
    if not first_row:
        return last
    return jnp.concatenate([scores[:, :first_row], last], axis=1)


MESH_ID = pl.DeviceIdType.MESH
ANY = pl.BlockSpec(memory_space=pl.ANY)
VMEM = pl.BlockSpec(memory_space=pltpu.VMEM)


class Copy:
    def __init__(self, describe):
        self.describe = describe
        describe().start()

    def wait(self):
        self.describe().wait()

    def wait_recv(self):
        self.describe().wait_recv()

    def wait_send(self):
        self.describe().wait_send()


class Links:
    def __init__(self, shard, replica, send, recv, local):
        self.shard, self.replica = shard, replica
        self.send, self.recv, self.local = send, recv, local
        self.used, self.used_local = 0, 0
        self.open = []

    def to(self, source, target, shard=0, replica=0):
        n, self.used = self.used, self.used + 1
        copy = Copy(
            lambda: pltpu.make_async_remote_copy(
                src_ref=source,
                dst_ref=target,
                send_sem=self.send.at[n],
                recv_sem=self.recv.at[n],
                device_id={
                    "shard": self.shard ^ shard,
                    "replica": self.replica ^ replica,
                },
                device_id_type=MESH_ID,
            )
        )
        self.open.append(copy)
        return copy

    def here(self, source, target):
        n, self.used_local = self.used_local, self.used_local + 1
        return Copy(
            lambda: pltpu.make_async_copy(source, target, self.local.at[n])
        )

    def sent(self, copy):
        copy.wait_send()
        self.open = [other for other in self.open if other is not copy]

    def close(self):
        for copy in self.open:
            copy.wait_send()


def greet(shard, replica, shard_masks, replica_masks):
    barrier = pltpu.get_barrier_semaphore()
    for mask in shard_masks:
        pl.semaphore_signal(
            barrier,
            inc=1,
            device_id={"shard": shard ^ mask, "replica": replica},
            device_id_type=MESH_ID,
        )
    for mask in replica_masks:
        pl.semaphore_signal(
            barrier,
            inc=1,
            device_id={"shard": shard, "replica": replica ^ mask},
            device_id_type=MESH_ID,
        )
    pl.semaphore_wait(barrier, len(shard_masks) + len(replica_masks))


def norm_rows(source, target, gains, which, start, count):
    model = source.shape[1]
    part = model // S

    def step(i, carry):
        rows = pl.ds(pl.multiple_of(start + i * 16, 16), 16)
        values = source[rows, :].astype(F32)
        scale = rms_scale(values)
        for j in range(S):
            gain = gains[j, which : which + 1, :].astype(F32)
            cols = slice(j * part, (j + 1) * part)
            target[rows, cols] = (values[:, cols] * scale * gain).astype(BF)
        return carry

    lax.fori_loop(0, count // 16, step, 0, unroll=2)


def front_kernel(
    x_ref, cot_ref, gain_ref, wq_ref, wk_ref, wv_ref, wo_ref, gate_ref, up_ref, table_ref,
    norm1_ref, heads_ref, log_ref, mixed_ref, w_heads_ref, mid_ref, norm2_ref, w_ff_ref, cot_all_ref, gains_ref,
    x_all, gains, kv_parts, near_q, near_kv, near_gate, near_up, w_heads, norm1, pre, kk_ref, vv_ref,
    far_out, far_in, across_out, across_in, beside_out, beside_in, term, norm2, own_ff, send, recv, local,
):
    shard, replica = lax.axis_index("shard"), lax.axis_index("replica")
    x, core, quarter = shard // 2, shard % 2, replica % 4
    tokens, model = x_ref.shape
    seq_len = S * tokens
    rows = wq_ref.shape[0]
    q_cols, ff_cols = wq_ref.shape[1] // S, gate_ref.shape[1] // S
    width = q_cols + LANES
    q_rows, half = rows // 4, tokens // 2
    links = Links(shard, replica, send, recv, local)

    def lanes(index, size):
        return pl.ds(pl.multiple_of(index * size, LANES), size)

    def block(index, size=tokens, extra=0):
        return pl.ds(pl.multiple_of(index * size + extra, 16), size)

    for j in range(S):
        keys = wk_ref[:, j // 2 * LANES : (j // 2 + 1) * LANES].astype(F32)
        vals = wv_ref[:, j // 2 * LANES : (j // 2 + 1) * LANES].astype(F32)
        if j % 2 == 0:
            pair = both(keys, pltpu.roll(vals, HD, 1))
        else:
            pair = both(pltpu.roll(keys, HD, 1), vals)
        kv_parts[j] = pair.astype(BF)

    greet(shard, replica, (1, 2, 3), (1, 2))

    mine = pl.ds(pl.multiple_of(quarter * q_rows, q_rows), q_rows)
    other_chip = 1 - x
    across_q = links.to(wq_ref.at[mine, lanes(other_chip, 2 * q_cols)], near_q, 2)
    across_kv = links.to(kv_parts.at[pl.ds(2 * other_chip, 2), mine], near_kv, 2)
    gain_copies = [links.to(gain_ref, gains.at[shard], m) for m in (1, 2, 3)]
    own_rows = [
        pl.ds(pl.multiple_of(shard * tokens + i * half, half), half) for i in range(2)
    ]
    x_across = [
        links.to(x_ref.at[pl.ds(i * half, half)], x_all.at[own_rows[i]], 2)
        for i in range(2)
    ]
    x_beside = links.to(x_ref, x_all.at[block(shard)], 1)
    own_w = pl.ds(pl.multiple_of(shard * rows, rows), rows)
    pair_shard = shard ^ 1
    w_beside = [
        links.to(
            wq_ref.at[:, lanes(pair_shard, q_cols)], w_heads.at[own_w, :q_cols], 1
        ),
        links.to(kv_parts.at[pair_shard], w_heads.at[own_w, q_cols:], 1),
    ]
    here = [
        links.here(x_ref, x_all.at[block(shard)]),
        links.here(gain_ref, gains.at[shard]),
        links.here(wq_ref.at[:, lanes(shard, q_cols)], w_heads.at[own_w, :q_cols]),
        links.here(kv_parts.at[shard], w_heads.at[own_w, q_cols:]),
    ]
    own_ff_in = [
        links.here(ref.at[:, lanes(shard, ff_cols)], own_ff.at[i])
        for i, ref in enumerate((gate_ref, up_ref))
    ]
    here_late = [links.here(cot_ref, cot_all_ref.at[block(shard)])]

    def rows_from(mask, of):
        return pl.ds(
            pl.multiple_of((shard ^ mask) * rows + (quarter ^ of) * q_rows, q_rows),
            q_rows,
        )

    across_q.wait_recv()
    across_kv.wait_recv()
    near_rows, far_rows = rows_from(2, 0), rows_from(3, 0)
    pair_lanes = lanes(1 - core, q_cols)
    core_q = links.to(near_q.at[:, pair_lanes], w_heads.at[near_rows, :q_cols], 1)
    core_kv = links.to(near_kv.at[1 - core], w_heads.at[near_rows, q_cols:], 1)
    near_copies = [
        links.here(near_q.at[:, lanes(core, q_cols)], w_heads.at[near_rows, :q_cols]),
        links.here(near_kv.at[core], w_heads.at[near_rows, q_cols:]),
    ]
    for copy in near_copies:
        copy.wait()
    y_near, z_near = (
        links.to(w_heads.at[near_rows], w_heads.at[near_rows], 0, m) for m in (1, 2)
    )
    core_q.wait_recv()
    core_kv.wait_recv()
    y_far, z_far = (
        links.to(w_heads.at[far_rows], w_heads.at[far_rows], 0, m) for m in (1, 2)
    )
    ff_across = [
        links.to(ref.at[mine, lanes(other_chip, 2 * ff_cols)], near, 2)
        for ref, near in ((gate_ref, near_gate), (up_ref, near_up))
    ]

    for copy in here:
        copy.wait()
    for copy in gain_copies:
        copy.wait_recv()
    gains_ref[...] = gains[...]
    norm_rows(x_all, norm1, gains, 0, shard * tokens, tokens)
    x_beside.wait_recv()
    norm_rows(x_all, norm1, gains, 0, (shard ^ 1) * tokens, tokens)

    y_near.wait_recv()
    y_far.wait_recv()
    z_forward = [
        links.to(w_heads.at[r], w_heads.at[r], 0, 2)
        for r in (rows_from(2, 1), rows_from(3, 1))
    ]
    x_core = []
    for i in range(2):
        x_across[i].wait_recv()
        got = pl.ds(pl.multiple_of((shard ^ 2) * tokens + i * half, half), half)
        x_core.append(links.to(x_all.at[got], x_all.at[got], 1))
        norm_rows(x_all, norm1, gains, 0, (shard ^ 2) * tokens + i * half, half)
    for i in range(2):
        x_core[i].wait_recv()
        norm_rows(x_all, norm1, gains, 0, (shard ^ 3) * tokens + i * half, half)
    norm1_out = links.here(norm1, norm1_ref)
    for i in range(2):
        own_ff_in[i].wait()
        cols = slice(i * ff_cols, (i + 1) * ff_cols)
        here_late.append(links.here(own_ff.at[i], w_ff_ref.at[own_w, cols]))
    w_beside_ff = [
        links.to(ref.at[:, lanes(pair_shard, ff_cols)], w_ff_ref.at[own_w, cols], 1)
        for ref, cols in (
            (gate_ref, slice(0, ff_cols)),
            (up_ref, slice(ff_cols, 2 * ff_cols)),
        )
    ]
    cot_beside = links.to(cot_ref, cot_all_ref.at[block(shard)], 1)

    for copy in w_beside + [z_near, z_far] + z_forward:
        copy.wait_recv()
    w_heads_out = links.here(w_heads, w_heads_ref)

    def project(b, carry):
        r = pl.ds(pl.multiple_of(b * tokens, tokens), tokens)
        pre[r, :] = matmul(norm1[r, :], w_heads[...])
        return carry

    lax.fori_loop(0, S, project, 0)

    for copy in ff_across:
        copy.wait_recv()
    pair_ff = lanes(1 - core, ff_cols)
    ff_parts = ((near_gate, slice(0, ff_cols)), (near_up, slice(ff_cols, 2 * ff_cols)))
    ff_core = [
        links.to(near.at[:, pair_ff], w_ff_ref.at[near_rows, cols], 1)
        for near, cols in ff_parts
    ]
    ff_here = [
        links.here(near.at[:, lanes(core, ff_cols)], w_ff_ref.at[near_rows, cols])
        for near, cols in ff_parts
    ]
    cot_across = links.to(cot_ref, cot_all_ref.at[block(shard)], 2)

    kv = pre[:, q_cols:]
    kv = (kv * table_ref[2] + turned(kv) * table_ref[3]).astype(BF)
    heads_ref[:, q_cols:] = kv
    kv = kv.astype(F32)
    swapped = pltpu.roll(kv, HD, 1)
    kk_ref[...] = both(kv, swapped).astype(BF)
    vv_ref[...] = both(swapped, jnp.ones_like(kv)).astype(BF)

    for copy in ff_here:
        copy.wait()
    ff_y = [links.to(w_ff_ref.at[near_rows], w_ff_ref.at[near_rows], 0, 1)]
    ff_z = [links.to(w_ff_ref.at[near_rows], w_ff_ref.at[near_rows], 0, 2)]
    for copy in ff_core:
        copy.wait_recv()
    ff_y.append(links.to(w_ff_ref.at[far_rows], w_ff_ref.at[far_rows], 0, 1))
    ff_z.append(links.to(w_ff_ref.at[far_rows], w_ff_ref.at[far_rows], 0, 2))

    def attend_rows(i):
        q_rows_i = slice(i * tokens, (i + 1) * tokens)
        seen = (i + 1) * tokens

        def pair_step(j, carry):
            cols = pl.ds(pl.multiple_of(j * LANES, LANES), LANES)
            q = pre[q_rows_i, cols]
            q = q * table_ref[0, q_rows_i] + turned(q) * table_ref[1, q_rows_i]
            q = (q.astype(BF).astype(F32) * HD**-0.5).astype(BF)
            heads_ref[q_rows_i, cols] = q
            scores = matmul_right_t(two_heads(q), kk_ref[:seen])
            scores = causal_mask(scores, i * tokens)
            peak = jnp.max(scores, axis=-1, keepdims=True)
            exps = jnp.exp(scores - peak).astype(BF)
            out = matmul(exps, vv_ref[:seen])
            first, second = out[:tokens], out[tokens:]
            first_r, second_r = pltpu.roll(first, HD, 1), pltpu.roll(second, HD, 1)
            total = both(first_r, second)
            mixed_ref[q_rows_i, cols] = (both(first, second_r) / total).astype(BF)
            peaks = [
                jnp.broadcast_to(p, (tokens, LANES)) for p in (peak[:tokens], peak[tokens:])
            ]
            log_ref[q_rows_i, cols] = both(*peaks) + jnp.log(total)
            return carry

        lax.fori_loop(0, q_cols // LANES, pair_step, 0)

    def out_term(index):
        r = block(index)

        def step(j, carry):
            cols = pl.ds(pl.multiple_of(j * 512, 512), 512)
            term[:, cols] = matmul(mixed_ref[r, :], wo_ref[:, cols])
            return carry

        lax.fori_loop(0, model // 512, step, 0)

    def attend_block(index):
        for i in range(S):
            pl.when(index == i)(functools.partial(attend_rows, i))

    attend_block(shard ^ 3)
    out_term(shard ^ 3)
    far_out[...] = term[...].astype(BF)
    far = links.to(far_out, far_in, 1)
    attend_block(shard ^ 2)
    out_term(shard ^ 2)
    far.wait_recv()
    across = []
    for i in range(2):
        r = slice(i * half, (i + 1) * half)
        across_out[r] = (term[r] + far_in[r].astype(F32)).astype(BF)
        across.append(links.to(across_out.at[r], across_in.at[r], 2))
    attend_block(shard ^ 1)
    out_term(shard ^ 1)
    beside_out[...] = term[...].astype(BF)
    beside = links.to(beside_out, beside_in, 1)
    for copy in ff_y:
        copy.wait_recv()
    ff_forward = [
        links.to(w_ff_ref.at[r], w_ff_ref.at[r], 0, 2)
        for r in (rows_from(2, 1), rows_from(3, 1))
    ]
    attend_block(shard)
    out_term(shard)
    beside.wait_recv()
    term[...] += x_ref[...].astype(F32) + beside_in[...].astype(F32)
    n2_across, n2_beside, n2_here = [], [], []
    for i in range(2):
        r = slice(i * half, (i + 1) * half)
        across[i].wait_recv()
        mid_ref[r] = term[r] + across_in[r].astype(F32)
        norm_rows(mid_ref, norm2, gains, 1, i * half, half)
        n2_across.append(links.to(norm2.at[r], norm2_ref.at[own_rows[i]], 2))
        n2_beside.append(links.to(norm2.at[r], norm2_ref.at[own_rows[i]], 1))
        n2_here.append(links.here(norm2.at[r], norm2_ref.at[own_rows[i]]))
    n2_core = []
    for i in range(2):
        n2_across[i].wait_recv()
        got = pl.ds(pl.multiple_of((shard ^ 2) * tokens + i * half, half), half)
        n2_core.append(links.to(norm2_ref.at[got], norm2_ref.at[got], 1))
    cot_across.wait_recv()
    got = block(shard ^ 2)
    cot_core = links.to(cot_all_ref.at[got], cot_all_ref.at[got], 1)
    for copy in (
        w_beside_ff + [cot_beside] + ff_z + ff_forward + n2_beside + n2_core + [cot_core]
    ):
        copy.wait_recv()
    for copy in here_late + n2_here + [norm1_out, w_heads_out]:
        copy.wait()
    links.close()


def front(x, cot, gains, wq, wk, wv, wo, gate, up, tables):
    tokens, model = x.shape
    seq_len, rows = S * tokens, wq.shape[0]
    q_cols, ff_cols = wq.shape[1] // S, gate.shape[1] // S
    width, q_rows = q_cols + LANES, rows // 4
    shape = jax.ShapeDtypeStruct
    chip_ff = (q_rows, 2 * ff_cols)
    row_block = pltpu.VMEM((tokens, model), BF)
    return pl.pallas_call(
        front_kernel,
        out_shape=(
            shape((seq_len, model), BF),
            shape((seq_len, width), BF),
            shape((seq_len, q_cols), F32),
            shape((seq_len, q_cols), BF),
            shape((S * rows, width), BF),
            shape((tokens, model), F32),
            shape((seq_len, model), BF),
            shape((S * rows, 2 * ff_cols), BF),
            shape((seq_len, model), BF),
            shape((S, 16, rows), BF),
        ),
        in_specs=[VMEM, VMEM, VMEM, ANY, VMEM, VMEM, VMEM, ANY, ANY, VMEM],
        out_specs=[ANY, VMEM, VMEM, VMEM, ANY, VMEM, ANY, ANY, ANY, VMEM],
        scratch_shapes=[
            pltpu.VMEM((seq_len, model), BF),
            pltpu.VMEM((S, 16, rows), BF),
            pltpu.VMEM((S, rows, LANES), BF),
            pltpu.VMEM((q_rows, 2 * q_cols), BF),
            pltpu.VMEM((2, q_rows, LANES), BF),
            pltpu.VMEM(chip_ff, BF),
            pltpu.VMEM(chip_ff, BF),
            pltpu.VMEM((S * rows, width), BF),
            pltpu.VMEM((seq_len, model), BF),
            pltpu.VMEM((seq_len, width), F32),
            pltpu.VMEM((seq_len, LANES), BF),
            pltpu.VMEM((seq_len, LANES), BF),
            row_block,
            row_block,
            row_block,
            row_block,
            row_block,
            row_block,
            pltpu.VMEM((tokens, model), F32),
            row_block,
            pltpu.VMEM((2, rows, ff_cols), BF),
            pltpu.SemaphoreType.DMA((48,)),
            pltpu.SemaphoreType.DMA((48,)),
            pltpu.SemaphoreType.DMA((24,)),
        ],
        compiler_params=pltpu.CompilerParams(
            collective_id=0, has_side_effects=True, vmem_limit_bytes=60 * 2**20
        ),
    )(x, cot, gains, wq, wk, wv, wo, gate, up, tables)


def by_rows(count, body, step=16):
    if count % step:
        body(pl.ds(0, count))
        return

    def one(i, carry):
        body(pl.ds(pl.multiple_of(i * step, step), step))
        return carry

    lax.fori_loop(0, count // step, one, 0)


class Scatter:
    def __init__(self, links, term, far_in, across_out, across_in, beside_in):
        self.links, self.term = links, term
        self.far_in, self.across_out = far_in, across_out
        self.across_in, self.beside_in = across_in, beside_in
        self.tokens = far_in.shape[0]
        self.half = self.tokens // 2
        self.starts = [
            [
                pl.multiple_of((links.shard ^ mask) * self.tokens + extra, 16)
                for extra in (0, self.half)
            ]
            for mask in range(S)
        ]

    def rows(self, mask, part=None):
        if part is None:
            return pl.ds(self.starts[mask][0], self.tokens)
        return pl.ds(self.starts[mask][part], self.half)

    def send_far(self):
        self.far = self.links.to(self.term.at[self.rows(3)], self.far_in, 1)

    def send_across(self):
        self.far.wait_recv()
        self.across = []
        base = self.starts[2][0]
        for i in range(2):

            def add(rows):
                start = i * self.half + rows.start
                here = pl.ds(pl.multiple_of(start, 16), rows.size)
                there = pl.ds(pl.multiple_of(base + start, 16), rows.size)
                total = self.term[there, :].astype(F32)
                total += self.far_in[here, :].astype(F32)
                self.across_out[here, :] = total.astype(BF)

            by_rows(self.half, add)
            part = pl.ds(i * self.half, self.half)
            self.across.append(
                self.links.to(self.across_out.at[part], self.across_in.at[part], 2)
            )

    def send_beside(self):
        self.beside = self.links.to(self.term.at[self.rows(1)], self.beside_in, 1)

    def finish(self, i, use):
        if i == 0:
            self.beside.wait_recv()
        self.across[i].wait_recv()
        base = self.starts[0][0]

        def one(rows):
            start = i * self.half + rows.start
            here = pl.ds(pl.multiple_of(start, 16), rows.size)
            there = pl.ds(pl.multiple_of(base + start, 16), rows.size)
            total = self.term[there, :].astype(F32)
            total += self.beside_in[here, :].astype(F32)
            total += self.across_in[here, :].astype(F32)
            use(here, total)

        by_rows(self.half, one)

    def release(self):
        for copy in [self.far, self.beside] + self.across:
            self.links.sent(copy)


STEPS = {
    "tff2": ("down0", "down1"),
    "pout": ("ff3",),
    "mix": ("ff2",),
    "gath1": ("down0",),
    "att0": ("ff1",),
    "att3": ("ff2", "ff3", "down1"),
    "w_rf3": ("down0",),
    "heads": ("ff1", "ff0"),
    "last": (
        ("ff2", "out0", "ff3", "down1", "ff0", "ff1", "heads0", "out0", "heads1")
        + ("heads0", "ff0", "out0", "heads1", "heads0", "heads1")
    ),
}


class Flow:
    def __init__(self, links, order, arrive, sends):
        self.links, self.arrive, self.sends = links, list(arrive), list(sends)
        self.bits = len(self.arrive)
        self.order = [b for b in order if b < self.bits]
        self.order += list(range(len(order), self.bits))
        self.left = list(range(self.bits - 1, -1, -1))
        self.sides = [(links.replica >> b) % 2 for b in range(self.bits)]
        self.others = [1 - side for side in self.sides]
        self.at = 0
        self.done = False

    def begin(self, term):
        self.parts = [term]
        self.step()

    def pick(self, bit, side):
        where = (slice(None),) * self.left.index(bit) + (side,)
        return [part.at[where] for part in self.parts]

    def step(self):
        bit = self.order[self.at]
        mine = self.sides[bit]
        if self.at:
            self.copy.wait_recv()
        other = self.pick(bit, self.others[bit])
        source = other[0]
        if self.at:
            source = self.sends[self.at - 1]
            self.add(other, source, len(self.left) - 1)
        self.copy = self.links.to(source, self.arrive[self.at], 0, 1 << bit)
        self.parts = self.pick(bit, mine) + [self.arrive[self.at]]
        self.left.remove(bit)
        self.at += 1

    def advance(self):
        if self.at < self.bits:
            self.step()
        elif not self.done:
            self.done = True
            self.conclude(self)

    def end(self, target):
        self.copy.wait_recv()
        self.add(self.parts, target, 0)

    def add(self, parts, target, free):
        ways = list(itertools.product(range(2), repeat=free))
        rest = parts[0].shape[free:]
        jobs = [(way, part) for way in ways for part in parts]

        def inner(fetch, sems):
            copies = []
            for n, (way, part) in enumerate(jobs):
                source = part.at[way] if way else part
                copy = pltpu.make_async_copy(source, fetch.at[n], sems.at[n])
                copy.start()
                copies.append(copy)
            for w, way in enumerate(ways):
                first = w * len(parts)
                for k in range(len(parts)):
                    copies[first + k].wait()
                leads = [()] if len(rest) == 2 else [(g,) for g in range(rest[0])]
                for lead in leads:

                    def one(rows):
                        total = fetch[(first,) + lead + (rows,)].astype(F32)
                        for k in range(1, len(parts)):
                            more = fetch[(first + k,) + lead + (rows,)]
                            total += more.astype(F32)
                        target[way + lead + (rows,)] = total.astype(target.dtype)

                    by_rows(rest[-2], one)

        pl.run_scoped(
            inner,
            pltpu.VMEM((len(jobs),) + tuple(rest), BF),
            pltpu.SemaphoreType.DMA((len(jobs),)),
        )


def bits_of(index, count):
    return tuple((index >> b) & 1 for b in reversed(range(count.bit_length() - 1)))


def turn(source, cols, target):
    rows = source.shape[0]
    for i in range(0, rows, 256):
        part = source[i : i + 256, cols]
        target[:, i : i + 256] = part.astype(F32).T.astype(BF)


def produce(left_t, right, first, size, stage, replicas, lead=(), tile=256):
    share = left_t.shape[0] // replicas

    def one(t, carry):
        start = pl.multiple_of(t * tile, LANES)
        cols = pl.ds(pl.multiple_of(first + start, LANES), tile)
        result = matmul(left_t[...], right[:, cols])
        for r in range(replicas):
            where = bits_of(r, replicas) + lead + (slice(None), pl.ds(start, tile))
            stage[where] = result[r * share : (r + 1) * share].astype(BF)
        return carry

    lax.fori_loop(0, size // tile, one, 0)


def stream(count, copies_of, use):
    for copy in copies_of(0, 0):
        copy.start()

    def one(t, carry):
        slot = t % 2

        @pl.when(t + 1 < count)
        def _():
            for copy in copies_of(t + 1, 1 - slot):
                copy.start()

        for copy in copies_of(t, slot):
            copy.wait()
        use(t, slot)
        return carry

    lax.fori_loop(0, count, one, 0)


def norm_back_rows(grad, values, gain_row):
    scale = rms_scale(values)
    weighted = grad * gain_row
    mean = jnp.mean(weighted * values, axis=-1, keepdims=True)
    return scale * weighted - values * (scale * scale * scale * mean)


def rear_kernel(
    norm2_hbm, cot_hbm, w_ff_hbm, w_down_hbm, norm1_hbm, mixed_hbm, w_out_hbm, heads_hbm, logs_hbm,
    table_hbm, w_heads_hbm, mid_ref, cot_ref, x_ref, gain_ref,
    output_ref, input_grad_ref, grad_out_ref, grad_down_ref, pieces_ff, pieces_heads, *others,
):
    shard, replica = lax.axis_index("shard"), lax.axis_index("replica")
    tokens, model = mid_ref.shape
    seq_len = S * tokens
    ff_cols, rows = w_down_hbm.shape[0], model // S
    width = heads_hbm.shape[1]
    q_cols = width - LANES
    replicas = model // (S * pieces_ff.shape[1])
    bits = replicas.bit_length() - 1
    share, share_down = pieces_ff.shape[1], grad_down_ref.shape[0]
    half, half_model = tokens // 2, model // 2
    others = list(others)

    def take(count):
        taken = others[:count]
        del others[:count]
        return taken

    hbm = {name: take(1 + bits) for name in ("ff", "down", "out", "heads")}
    cot_all, term, far_in, across_out, across_in, beside_in, grad_mid, grad_mid_b = take(8)
    sends = {name: take(bits) for name in ("ff", "down", "out", "heads")}
    send, recv, local, slots = take(4)
    links = Links(shard, replica, send, recv, local)
    other_chip = 1 - shard // 2

    def flow(name, order, index=None):
        pick = (lambda ref: ref) if index is None else (lambda ref: ref.at[index])
        made = Flow(
            links,
            order,
            [pick(ref) for ref in hbm[name][1:]],
            [pick(ref) for ref in sends[name][:-1]],
        )
        made.term, made.last = pick(hbm[name][0]), pick(sends[name][-1])
        return made

    ff_order = ((0, 1, 2), (0, 1, 2), (1, 0, 2), (0, 1, 2))
    flows_ff = [flow("ff", ff_order[m], m) for m in range(S)]
    flows_down = [flow("down", order, i) for i, order in enumerate(((0, 1, 2), (1, 2, 0)))]
    flow_out = flow("out", (0, 1, 2))
    flows_heads = [flow("heads", (0, 1, 2), i) for i in range(2)]
    flows = {"out0": flow_out}
    for name, many in (("ff", flows_ff), ("down", flows_down), ("heads", flows_heads)):
        flows.update({f"{name}{i}": made for i, made in enumerate(many)})
    finals, finals_here = [], []

    def deliver(piece, pieces, mask):
        if mask:
            finals.append(links.to(piece, pieces.at[mask], mask))
        else:
            finals_here.append(links.here(piece, pieces.at[mask]))

    def end_ff(mask, made):
        made.end(made.last)
        deliver(made.last, pieces_ff, mask)

    def end_down(i, made):
        made.end(made.last)
        cols = pl.ds(i * half_model, half_model)
        finals_here.append(links.here(made.last, grad_down_ref.at[:, cols]))

    def end_out(made):
        made.end(made.last)
        finals_here.append(links.here(made.last, grad_out_ref))

    def end_heads(i, made):
        made.end(made.last)
        for n, mask in enumerate(((3, 2), (1, 0))[i]):
            deliver(made.last.at[n], pieces_heads, mask)

    for i in range(S):
        flows_ff[i].conclude = functools.partial(end_ff, i)
    for i in range(2):
        flows_down[i].conclude = functools.partial(end_down, i)
        flows_heads[i].conclude = functools.partial(end_heads, i)
    flow_out.conclude = end_out

    def pump(point):
        for name in STEPS.get(point, ()):
            flows[name].advance()

    greet(shard, replica, (1, 2, 3), [1 << b for b in range(bits)])
    gain_one, gain_two = (
        jnp.concatenate(
            [gain_ref[j, i : i + 1, :].astype(F32) for j in range(S)], axis=1
        )
        for i in range(2)
    )
    sums = Scatter(links, term, far_in, across_out, across_in, beside_in)
    ended = []

    def first_half(norm2, hidden, grad_ff):
        norm2_in = links.here(norm2_hbm, norm2)
        cot_in = links.here(cot_hbm, cot_all)

        tile = 256
        tiles = [(i, min(tile, ff_cols - i)) for i in range(0, ff_cols, tile)]

        def over_tiles(copies_of, use):
            for copy in copies_of(0):
                copy.start()
            for t, (start, size) in enumerate(tiles):
                if t + 1 < len(tiles):
                    for copy in copies_of(t + 1):
                        copy.start()
                for copy in copies_of(t):
                    copy.wait()

                def block(b, carry):
                    use(pl.ds(pl.multiple_of(b * 512, 512), 512), start, size, t % 2)
                    return carry

                lax.fori_loop(0, seq_len // 512, block, 0)

        def gate_up(gates, ups):
            def copies_of(t):
                start, size = tiles[t]
                slot = t % 2
                cols = slice(start, start + size)
                up_cols = slice(ff_cols + start, ff_cols + start + size)
                return [
                    pltpu.make_async_copy(*pair, slots.at[slot, n])
                    for n, pair in enumerate(
                        (
                            (w_ff_hbm.at[:, cols], gates.at[slot, :, :size]),
                            (w_ff_hbm.at[:, up_cols], ups.at[slot, :, :size]),
                        )
                    )
                ]

            def use(r, start, size, slot):
                gate = matmul(norm2[r, :], gates[slot, :, :size])
                up = matmul(norm2[r, :], ups[slot, :, :size])
                silu = gate * (1.0 / (1.0 + jnp.exp(-gate)))
                hidden[r, start : start + size] = (silu * up).astype(BF)
                grad_ff[r, start : start + size] = gate.astype(BF)
                grad_ff[r, ff_cols + start : ff_cols + start + size] = up.astype(BF)

            norm2_in.wait()
            over_tiles(copies_of, use)

        weight_tile = pltpu.VMEM((2, model, tile), BF)
        pl.run_scoped(gate_up, weight_tile, weight_tile)
        cot_in.wait()

        def down_terms(left_t, stage):
            turn(hidden, slice(None), left_t)
            for i in range(2):
                produce(left_t, cot_all, i * half_model, half_model, stage, replicas)
                links.here(stage, flows_down[i].term).wait()
                flows_down[i].begin(flows_down[i].term)

        pl.run_scoped(
            down_terms,
            pltpu.VMEM((ff_cols, seq_len), BF),
            pltpu.VMEM((2,) * bits + (share_down, half_model), BF),
        )

        def hidden_grads(downs):
            def copies_of(t):
                start, size = tiles[t]
                slot = t % 2
                return [
                    pltpu.make_async_copy(
                        w_down_hbm.at[slice(start, start + size)],
                        downs.at[slot, :size],
                        slots.at[slot, 0],
                    )
                ]

            def use(r, start, size, slot):
                grad = matmul_right_t(cot_all[r, :], downs[slot, :size])
                cols = slice(start, start + size)
                up_cols = slice(ff_cols + start, ff_cols + start + size)
                gate, up = grad_ff[r, cols].astype(F32), grad_ff[r, up_cols].astype(F32)
                sigmoid = 1.0 / (1.0 + jnp.exp(-gate))
                slope = sigmoid * (1.0 + gate * (1.0 - sigmoid))
                grad_ff[r, cols] = (grad * up * slope).astype(BF)
                grad_ff[r, up_cols] = (grad * gate * sigmoid).astype(BF)

            over_tiles(copies_of, use)

        pl.run_scoped(hidden_grads, pltpu.VMEM((2, tile, model), BF))
        pump("hid")

        def norm_terms(chip):
            def inner(tiles):
                r = pl.ds(pl.multiple_of(chip * 2 * tokens, 2 * tokens), 2 * tokens)

                def copies_of(t, slot):
                    part = pl.ds(pl.multiple_of(t * 256, 256), 256)
                    return [
                        pltpu.make_async_copy(
                            w_ff_hbm.at[part], tiles.at[slot], slots.at[slot, 0]
                        )
                    ]

                def use(t, slot):
                    cols = pl.ds(pl.multiple_of(t * 256, 256), 256)
                    product = matmul_right_t(grad_ff[r, :], tiles[slot])
                    term[r, cols] = product.astype(BF)

                stream(model // 256, copies_of, use)

            pl.run_scoped(inner, pltpu.VMEM((2, 256, 2 * ff_cols), BF))

        norm_terms(other_chip)
        sums.send_far()
        pump("far")

        def ff_terms(left_t, stages):
            copies = {}

            def launch(n):
                copies[n][0].wait()
                if copies[n][1] is not flows_ff[0]:
                    copies[n][1].begin(copies[n][1].term)

            for n, mask in enumerate((3, 2, 1, 0)):
                cols = pl.ds(pl.multiple_of((shard ^ mask) * rows, rows), rows)
                turn(norm2, cols, left_t)
                if n:
                    launch(n - 1)
                produce(left_t, grad_ff, 0, 2 * ff_cols, stages.at[n % 2], replicas)
                copies[n] = (
                    links.here(stages.at[n % 2], flows_ff[mask].term),
                    flows_ff[mask],
                )
                if n == 0:
                    pump("w_rf")
                    sums.send_across()
                pump(f"tff{n}")
            launch(3)

        pl.run_scoped(
            ff_terms,
            pltpu.VMEM((rows, seq_len), BF),
            pltpu.VMEM((2,) + (2,) * bits + (share, 2 * ff_cols), BF),
        )
        norm_terms(1 - other_chip)
        sums.send_beside()
        pump("near")

        def to_mid(r, grad):
            values = mid_ref[r, :]
            total = cot_ref[r, :].astype(F32)
            total += norm_back_rows(grad, values, gain_two)
            grad_mid[r, :] = total
            grad_mid_b[r, :] = total.astype(BF)

        gathered = []
        for i in range(2):
            sums.finish(i, to_mid)
            part = slice(i * half, (i + 1) * half)
            there = sums.rows(0, i)
            gathered.append(
                [
                    links.to(grad_mid_b.at[part], cot_all.at[there], 2),
                    links.to(grad_mid_b.at[part], cot_all.at[there], 1),
                    links.here(grad_mid_b.at[part], cot_all.at[there]),
                ]
            )
        sums.release()
        pump("mid")

        def out_terms(tiles):
            def copies_of(t, slot):
                part = pl.ds(pl.multiple_of(t * 256, 256), 256)
                return [
                    pltpu.make_async_copy(
                        w_down_hbm.at[:, part], tiles.at[slot], slots.at[slot, 0]
                    )
                ]

            def use(t, slot):
                cols = pl.ds(pl.multiple_of(t * 256, 256), 256)
                term[:, cols] = matmul(hidden[...], tiles[slot]).astype(BF)

            stream(model // 256, copies_of, use)

        pl.run_scoped(out_terms, pltpu.VMEM((2, ff_cols, 256), BF))
        pump("pout")
        return gathered

    gathered = []
    pl.run_scoped(
        lambda *refs: gathered.extend(first_half(*refs)),
        pltpu.VMEM((seq_len, model), BF),
        pltpu.VMEM((seq_len, ff_cols), BF),
        pltpu.VMEM((seq_len, 2 * ff_cols), BF),
    )

    def second_half(mixed, w_out, heads, logs, table, w_heads, grad_mixed, grad_heads,
                    kk_ref, vv_ref, dk_ref, dv_ref):
        loads = [
            links.here(*pair)
            for pair in (
                (w_out_hbm, w_out),
                (heads_hbm, heads),
                (logs_hbm, logs),
                (table_hbm, table),
                (mixed_hbm, mixed),
                (w_heads_hbm, w_heads),
            )
        ]
        for i in range(2):
            gathered[i][1].wait_recv()
            gathered[i][2].wait()
        sums.send_far()
        sums.send_beside()
        for copy in loads:
            copy.wait()

        def mix(mask, part=None):
            r = sums.rows(mask, part)
            grad_mixed[r, :] = matmul_right_t(cot_all[r, :], w_out[...]).astype(BF)

        mix(0)
        mix(1)
        kv = heads[:, q_cols:].astype(F32)
        swapped = pltpu.roll(kv, HD, 1)
        kk_ref[...] = both(kv, swapped).astype(BF)
        vv_ref[...] = both(swapped, kv).astype(BF)
        dk_ref[...] = jnp.zeros_like(dk_ref)
        dv_ref[...] = jnp.zeros_like(dv_ref)
        pump("mix")
        forward = []
        for i in range(2):
            gathered[i][0].wait_recv()
            r = sums.rows(2, i)
            forward.append(links.to(cot_all.at[r], cot_all.at[r], 1))
            mix(2, i)
            pump(f"gath{i}")
        sums.send_across()
        flows_ff[0].begin(flows_ff[0].term)
        pump("across2")
        for i in range(2):
            forward[i].wait_recv()
            mix(3, i)

        def out_grad(left_t, stage):
            turn(mixed, slice(None), left_t)
            produce(left_t, cot_all, 0, model, stage, replicas)
            links.here(stage, flow_out.term).wait()
            flow_out.begin(flow_out.term)

        pl.run_scoped(
            out_grad,
            pltpu.VMEM((rows, seq_len), BF),
            pltpu.VMEM((2,) * bits + (share, model), BF),
        )

        def attend_rows(i):
            r = slice(i * tokens, (i + 1) * tokens)
            seen = (i + 1) * tokens

            def pair_step(j, carry):
                cols = pl.ds(pl.multiple_of(j * LANES, LANES), LANES)
                q = two_heads(heads[r, cols])
                grad = two_heads(grad_mixed[r, cols])
                log_pair = logs[r, cols]
                log_col = jnp.concatenate(
                    [log_pair[:, :1], log_pair[:, HD : HD + 1]], axis=0
                )
                mixed_pair = mixed[r, cols].astype(F32)
                product = grad.astype(F32) * jnp.concatenate([mixed_pair] * 2, axis=0)
                inner = jnp.sum(product, axis=-1, keepdims=True)
                scores = matmul_right_t(q, kk_ref[:seen])
                soft = jnp.exp(causal_mask(scores, i * tokens) - log_col)
                grad_soft = matmul_right_t(grad, vv_ref[:seen])
                grad_scores = (soft * (grad_soft - inner)).astype(BF)
                dq = matmul(grad_scores, kk_ref[:seen])
                dq = both(dq[:tokens], dq[tokens:]) * HD**-0.5
                dq = dq * table[0, r] - turned(dq) * table[1, r]
                grad_heads[r, cols] = dq.astype(BF)
                dk_ref[:seen] += matmul_left_t(grad_scores, q)
                dv_ref[:seen] += matmul_left_t(soft.astype(BF), grad)
                return carry

            lax.fori_loop(0, q_cols // LANES, pair_step, 0)

        pump("out")
        for i in range(S):
            attend_rows(i)
            pump(f"att{i}")
        dk, dv = dk_ref[...], dv_ref[...]
        dk, dv = dk + pltpu.roll(dk, HD, 1), dv + pltpu.roll(dv, HD, 1)
        dkv = both(dk, dv)
        dkv = dkv * table[2] - turned(dkv) * table[3]
        grad_heads[:, q_cols:] = dkv.astype(BF)

        def to_output(r, total):
            output_ref[r, :] = (mid_ref[r, :] + total).astype(BF)

        for i in range(2):
            sums.finish(i, to_output)
        sums.release()
        for mask in (1, 2):
            pl.semaphore_signal(
                credit.at[mask - 1],
                inc=1,
                device_id={"shard": shard ^ mask, "replica": replica},
                device_id_type=MESH_ID,
            )

        def head_terms(chip):
            r = pl.ds(pl.multiple_of(chip * 2 * tokens, 2 * tokens), 2 * tokens)

            def one(t, carry):
                cols = pl.ds(pl.multiple_of(t * 256, 256), 256)
                product = matmul_right_t(grad_heads[r, :], w_heads[cols, :])
                term[r, cols] = product.astype(BF)
                return carry

            lax.fori_loop(0, model // 256, one, 0)

        def head_grads(norm1, left_t, stages):
            norm1_in = links.here(norm1_hbm, norm1)
            head_terms(other_chip)
            pl.semaphore_wait(credit.at[0], 1)
            sums.send_far()
            norm1_in.wait()
            stage_out = []
            for i, masks in enumerate(((3, 2), (1, 0))):
                for n, mask in enumerate(masks):
                    cols = pl.ds(pl.multiple_of((shard ^ mask) * rows, rows), rows)
                    turn(norm1, cols, left_t)
                    produce(
                        left_t, grad_heads, 0, width, stages.at[i], replicas, (n,), LANES
                    )
                stage_out.append(links.here(stages.at[i], flows_heads[i].term))
                if i == 0:
                    pump("w_rf3")
                    pl.semaphore_wait(credit.at[1], 1)
                    sums.send_across()
                    stage_out[0].wait()
                    flows_heads[0].begin(flows_heads[0].term)
            stage_out[1].wait()
            flows_heads[1].begin(flows_heads[1].term)
            head_terms(1 - other_chip)
            sums.send_beside()

        pl.run_scoped(
            head_grads,
            pltpu.VMEM((seq_len, model), BF),
            pltpu.VMEM((rows, seq_len), BF),
            pltpu.VMEM((2,) + (2,) * bits + (2, share, width), BF),
        )
        pump("heads")

    credit = take(1)[0]
    pl.run_scoped(
        second_half,
        pltpu.VMEM((seq_len, q_cols), BF),
        pltpu.VMEM((q_cols, model), BF),
        pltpu.VMEM((seq_len, width), BF),
        pltpu.VMEM((seq_len, q_cols), F32),
        pltpu.VMEM((4, seq_len, LANES), F32),
        pltpu.VMEM((model, width), BF),
        pltpu.VMEM((seq_len, q_cols), BF),
        pltpu.VMEM((seq_len, width), BF),
        pltpu.VMEM((seq_len, LANES), BF),
        pltpu.VMEM((seq_len, LANES), BF),
        pltpu.VMEM((seq_len, LANES), F32),
        pltpu.VMEM((seq_len, LANES), F32),
    )

    def to_input_grad(r, grad):
        total = grad_mid[r, :]
        total += norm_back_rows(grad, x_ref[r, :].astype(F32), gain_one)
        input_grad_ref[r, :] = total.astype(BF)

    for i in range(2):
        sums.finish(i, to_input_grad)
    pump("last")
    waiting = list(flows.values())
    while waiting:
        for made in waiting:
            made.advance()
        waiting = [made for made in waiting if not made.done]
    for copy in finals:
        copy.wait_recv()
    for copy in finals_here:
        copy.wait()
    links.close()


def rear(norm2, cot_all, w_ff, w_down, norm1, mixed, w_out, heads, logs, tables, w_heads, mid, cot, x, gains, replicas):
    tokens, model = mid.shape
    seq_len, rows, ff_cols = S * tokens, model // S, w_down.shape[0]
    width = heads.shape[1]
    bits = replicas.bit_length() - 1
    share, share_down = rows // replicas, ff_cols // replicas
    shape = jax.ShapeDtypeStruct
    rests = {
        "ff": ((S,), (share, 2 * ff_cols), BF),
        "down": ((2,), (share_down, model // 2), F32),
        "out": ((), (share, model), F32),
        "heads": ((2,), (2, share, width), BF),
    }
    work, sends = [], []
    for many, rest, last in rests.values():
        work += [shape(many + (2,) * bits + rest, BF)]
        work += [shape(many + (2,) * n + rest, BF) for n in reversed(range(bits))]
        sends += [
            pltpu.VMEM(many + (2,) * n + rest, BF) for n in reversed(range(bits - 1))
        ]
        sends += [pltpu.VMEM(many + rest, last)]
    outs = (
        shape((tokens, model), BF),
        shape((tokens, model), BF),
        shape((share, model), F32),
        shape((share_down, model), F32),
        shape((S, share, 2 * ff_cols), BF),
        shape((S, share, width), BF),
    )
    row_block = pltpu.VMEM((tokens, model), BF)
    result = pl.pallas_call(
        rear_kernel,
        out_shape=outs + tuple(work),
        in_specs=[ANY] * 11 + [VMEM] * 4,
        out_specs=[VMEM] * 2 + [ANY] * (4 + len(work)),
        scratch_shapes=[
            pltpu.VMEM((seq_len, model), BF),
            pltpu.VMEM((seq_len, model), BF),
            row_block,
            row_block,
            row_block,
            row_block,
            pltpu.VMEM((tokens, model), F32),
            row_block,
        ]
        + sends
        + [
            pltpu.SemaphoreType.DMA((96,)),
            pltpu.SemaphoreType.DMA((96,)),
            pltpu.SemaphoreType.DMA((48,)),
            pltpu.SemaphoreType.DMA((2, 3)),
            pltpu.SemaphoreType.REGULAR((2,)),
        ],
        compiler_params=pltpu.CompilerParams(
            collective_id=1, has_side_effects=True, vmem_limit_bytes=62 * 2**20
        ),
    )(norm2, cot_all, w_ff, w_down, norm1, mixed, w_out, heads, logs, tables, w_heads, mid, cot, x, gains)
    return result[: len(outs)]


def on_device(
    inputs, cotangent, gain_attn, w_query, w_key, w_value, w_output, gain_mlp, w_gate, w_up, w_down
):
    shard, replica = lax.axis_index("shard"), lax.axis_index("replica")
    x, cot = inputs[0], cotangent[0]
    tables = jnp.asarray(rope_tables(S * x.shape[0]))
    gains = jnp.concatenate(
        [jnp.stack([gain_attn, gain_mlp]), jnp.zeros((14, w_query.shape[0]), BF)]
    )
    norm1, heads, logs, mixed, w_heads, mid, norm2, w_ff, cot_all, gains = front(
        x, cot, gains, w_query, w_key, w_value, w_output, w_gate, w_up, tables
    )
    output, input_grad, grad_output, grad_down, pieces_ff, pieces_heads = rear(
        norm2, cot_all, w_ff, w_down, norm1, mixed, w_output, heads, logs, tables,
        w_heads, mid, cot, x, gains, lax.axis_size("replica"),
    )
    grads, (grad_gain_two, grad_gain_one), moved = finish(
        (pieces_ff, pieces_heads),
        ((w_gate, w_up), (w_query, w_key, w_value)),
        (gain_mlp, gain_attn),
        (output, input_grad, grad_output, grad_down),
        shard,
        replica,
    )
    grad_gate, grad_up, grad_query, grad_key, grad_value = grads
    output, input_grad, grad_output, grad_down = moved
    return (
        output[None],
        input_grad[None],
        grad_gain_one,
        grad_query,
        grad_key,
        grad_value,
        grad_output,
        grad_gain_two,
        grad_gate,
        grad_up,
        grad_down,
    )


def solution(mesh):
    placed = (
        P("replica", "shard", None),
        P("replica", "shard", None),
        P("shard"),
        P("shard", None),
        P("shard", None),
        P("shard", None),
        P("shard", None),
        P("shard"),
        P("shard", None),
        P("shard", None),
        P("shard", None),
    )
    both_axes = ("shard", "replica")
    return jax.shard_map(
        on_device,
        mesh=mesh,
        in_specs=placed,
        out_specs=(
            P("replica", "shard", None),
            P("replica", "shard", None),
            P(both_axes),
            P(both_axes, None),
            P(both_axes, None),
            P(both_axes, None),
            P(both_axes, None),
            P(both_axes),
            P(both_axes, None),
            P(both_axes, None),
            P(both_axes, None),
        ),
        check_vma=False,
    )
```

```python
import functools
import itertools

import jax
import jax.numpy as jnp
import numpy as np
from jax import lax
from jax.experimental import pallas as pl
from jax.experimental.pallas import tpu as pltpu
from jax.sharding import PartitionSpec as P

H = 32
KV = 4
HD = 64
EPS = 1e-05
THETA = 10000.0
S = 4
BF = jnp.bfloat16
F32 = jnp.float32
LANES = 128
QB = 256


def matmul(left, right):
    return jnp.dot(left, right, preferred_element_type=F32)


def matmul_left_t(left, right):
    return lax.dot_general(
        left, right, (((0,), (0,)), ((), ())), preferred_element_type=F32
    )


def matmul_right_t(left, right):
    return lax.dot_general(
        left, right, (((1,), (1,)), ((), ())), preferred_element_type=F32
    )


def rms_scale(values):
    return lax.rsqrt(jnp.mean(values * values, axis=-1, keepdims=True) + EPS)


def finish_kernel(groups, moved, place_ref, *refs):
    refs = list(refs)

    def take(count):
        taken = refs[:count]
        del refs[:count]
        return taken

    many = [len(widths) for widths in groups]
    pieces, gains = take(len(groups)), take(len(groups))
    weights = [take(n) for n in many]
    sources = take(moved)
    outs, gain_outs = [take(n) for n in many], take(len(groups))
    targets = take(moved)
    held, staged = [take(n) for n in many], take(moved)
    sems = refs[0]
    shard, replica = place_ref[0], place_ref[1]
    copies = []

    def start(source, target):
        copies.append(pltpu.make_async_copy(source, target, sems.at[len(copies)]))
        copies[-1].start()

    for mine, kept in zip(weights, held):
        for weight, here in zip(mine, kept):
            rows = here.shape[0]
            start(weight.at[pl.ds(pl.multiple_of(replica * rows, rows), rows)], here)
    loads = list(copies)
    for source, stage in zip(sources, staged):
        start(source, stage)
    stages = copies[len(loads) :]
    for copy in loads:
        copy.wait()
    for copy, stage, target in zip(stages, staged, targets):
        copy.wait()
        start(stage, target)
    for g, widths in enumerate(groups):
        total = jnp.zeros(gain_outs[g].shape, F32)
        for mask in range(S):
            piece = pieces[g].at[mask]
            owner = shard ^ mask
            begin = 0
            for width, weight, out in zip(widths, held[g], outs[g]):
                if width % LANES == 0:
                    cols = pl.ds(pl.multiple_of(owner * width, LANES), width)
                    part = piece[:, begin : begin + width].astype(F32)
                    out[:, cols] = part
                else:
                    base = begin // LANES * LANES
                    part = piece[:, base : base + LANES].astype(F32)
                    lane = lax.broadcasted_iota(jnp.int32, part.shape, 1) // HD
                    side = owner % 2
                    part = jnp.where(
                        side == (begin - base) // HD, part, pltpu.roll(part, HD, 1)
                    )
                    part = jnp.where(lane == side, part, 0.0)
                    cols = pl.ds(pl.multiple_of(owner // 2 * LANES, LANES), LANES)
                    out[:, cols] = jnp.where(lane == side, part, out[:, cols])
                total += jnp.sum(
                    part * weight[:, cols].astype(F32), axis=1, keepdims=True
                )
                begin += width
        gain_outs[g][...] = total / gains[g][...]
    for copy in copies[len(loads) + moved :]:
        copy.wait()


def finish(pieces, weights, gains, moved, shard, replica):
    rows = pieces[0].shape[1]
    groups = [tuple(w.shape[1] // S for w in mine) for mine in weights]
    flat = [w for mine in weights for w in mine]
    own_gains = [
        lax.dynamic_slice_in_dim(gain, replica * rows, rows, 0)
        .astype(F32)
        .reshape(rows, 1)
        for gain in gains
    ]
    shapes = [jax.ShapeDtypeStruct((rows, w.shape[1]), F32) for w in flat]
    shapes += [jax.ShapeDtypeStruct((rows, 1), F32)] * len(groups)
    shapes += [jax.ShapeDtypeStruct(a.shape, a.dtype) for a in moved]
    vmem, hbm = (pl.BlockSpec(memory_space=m) for m in (pltpu.VMEM, pl.ANY))
    held = len(flat) + len(groups)
    result = pl.pallas_call(
        functools.partial(finish_kernel, groups, len(moved)),
        out_shape=shapes,
        in_specs=[pl.BlockSpec(memory_space=pltpu.SMEM)]
        + [vmem] * (2 * len(groups))
        + [hbm] * (len(flat) + len(moved)),
        out_specs=[vmem] * held + [hbm] * len(moved),
        scratch_shapes=[pltpu.VMEM((rows, w.shape[1]), BF) for w in flat]
        + [pltpu.VMEM(a.shape, a.dtype) for a in moved]
        + [pltpu.SemaphoreType.DMA((len(flat) + 2 * len(moved),))],
        compiler_params=pltpu.CompilerParams(vmem_limit_bytes=62 * 2**20),
    )(
        jnp.stack([shard, replica]).astype(jnp.int32),
        *pieces,
        *own_gains,
        *flat,
        *moved,
    )
    return (
        result[: len(flat)],
        [gain.reshape(rows) for gain in result[len(flat) : held]],
        result[held:],
    )


def rope_tables(seq_len):
    half = HD // 2
    freq = THETA ** (-2.0 * np.arange(half, dtype=np.float64) / HD)
    angles = np.arange(seq_len, dtype=np.float64)[:, None] * freq[None, :]
    cos, sin = np.cos(angles), np.sin(angles)
    one, zero = np.ones((seq_len, HD)), np.zeros((seq_len, HD))
    cos_head = np.concatenate([cos, cos], 1)
    sin_head = np.concatenate([-sin, sin], 1)
    tables = [
        np.concatenate([cos_head, cos_head], 1),
        np.concatenate([sin_head, sin_head], 1),
        np.concatenate([cos_head, one], 1),
        np.concatenate([sin_head, zero], 1),
    ]
    return np.stack(tables).astype(np.float32)


def turned(values):
    lane = lax.broadcasted_iota(jnp.int32, values.shape, 1)
    return jnp.where(
        lane % HD < HD // 2,
        pltpu.roll(values, LANES - HD // 2, 1),
        pltpu.roll(values, HD // 2, 1),
    )


def both(first, second):
    lane = lax.broadcasted_iota(jnp.int32, first.shape, 1)
    return jnp.where(lane < HD, first, second)


def two_heads(pair):
    zero = jnp.zeros_like(pair)
    return jnp.concatenate([both(pair, zero), both(zero, pair)], axis=0)


def causal_mask(scores, first_row):
    block = scores.shape[0] // 2
    last = scores[:, first_row:]
    row = lax.broadcasted_iota(jnp.int32, last.shape, 0) % block
    col = lax.broadcasted_iota(jnp.int32, last.shape, 1)
    last = jnp.where(col <= row, last, -1e30)
    if not first_row:
        return last
    return jnp.concatenate([scores[:, :first_row], last], axis=1)


MESH_ID = pl.DeviceIdType.MESH
ANY = pl.BlockSpec(memory_space=pl.ANY)
VMEM = pl.BlockSpec(memory_space=pltpu.VMEM)


class Copy:
    def __init__(self, describe):
        self.describe = describe
        describe().start()

    def wait(self):
        self.describe().wait()

    def wait_recv(self):
        self.describe().wait_recv()

    def wait_send(self):
        self.describe().wait_send()


class Links:
    def __init__(self, shard, replica, send, recv, local):
        self.shard, self.replica = shard, replica
        self.send, self.recv, self.local = send, recv, local
        self.used, self.used_local = 0, 0
        self.open = []

    def to(self, source, target, shard=0, replica=0):
        n, self.used = self.used, self.used + 1
        copy = Copy(
            lambda: pltpu.make_async_remote_copy(
                src_ref=source,
                dst_ref=target,
                send_sem=self.send.at[n],
                recv_sem=self.recv.at[n],
                device_id={
                    "shard": self.shard ^ shard,
                    "replica": self.replica ^ replica,
                },
                device_id_type=MESH_ID,
            )
        )
        self.open.append(copy)
        return copy

    def here(self, source, target):
        n, self.used_local = self.used_local, self.used_local + 1
        return Copy(
            lambda: pltpu.make_async_copy(source, target, self.local.at[n])
        )

    def sent(self, copy):
        copy.wait_send()
        self.open = [other for other in self.open if other is not copy]

    def close(self):
        for copy in self.open:
            copy.wait_send()


def greet(shard, replica, shard_masks, replica_masks):
    barrier = pltpu.get_barrier_semaphore()
    for mask in shard_masks:
        pl.semaphore_signal(
            barrier,
            inc=1,
            device_id={"shard": shard ^ mask, "replica": replica},
            device_id_type=MESH_ID,
        )
    for mask in replica_masks:
        pl.semaphore_signal(
            barrier,
            inc=1,
            device_id={"shard": shard, "replica": replica ^ mask},
            device_id_type=MESH_ID,
        )
    pl.semaphore_wait(barrier, len(shard_masks) + len(replica_masks))


def norm_rows(source, target, gains, which, start, count):
    model = source.shape[1]
    part = model // S

    def step(i, carry):
        rows = pl.ds(pl.multiple_of(start + i * 16, 16), 16)
        values = source[rows, :].astype(F32)
        scale = rms_scale(values)
        for j in range(S):
            gain = gains[j, which : which + 1, :].astype(F32)
            cols = slice(j * part, (j + 1) * part)
            target[rows, cols] = (values[:, cols] * scale * gain).astype(BF)
        return carry

    lax.fori_loop(0, count // 16, step, 0, unroll=2)


def front_kernel(
    x_ref, cot_ref, gain_ref, wq_ref, wk_ref, wv_ref, wo_ref, gate_ref, up_ref, table_ref,
    norm1_ref, heads_ref, log_ref, mixed_ref, w_heads_ref, mid_ref, norm2_ref, w_ff_ref, cot_all_ref, gains_ref,
    x_all, gains, kv_parts, near_q, near_kv, near_gate, near_up, w_heads, norm1, pre, kk_ref, vv_ref,
    far_out, far_in, across_out, across_in, beside_out, beside_in, term, norm2, own_ff, send, recv, local,
):
    shard, replica = lax.axis_index("shard"), lax.axis_index("replica")
    x, core, quarter, eighth = shard // 2, shard % 2, replica % 4, replica % 8
    tokens, model = x_ref.shape
    seq_len = S * tokens
    rows = wq_ref.shape[0]
    q_cols, ff_cols = wq_ref.shape[1] // S, gate_ref.shape[1] // S
    width = q_cols + LANES
    q_rows, f_rows, half = rows // 4, rows // 8, tokens // 2
    links = Links(shard, replica, send, recv, local)

    def lanes(index, size):
        return pl.ds(pl.multiple_of(index * size, LANES), size)

    def block(index, size=tokens, extra=0):
        return pl.ds(pl.multiple_of(index * size + extra, 16), size)

    for j in range(S):
        keys = wk_ref[:, j // 2 * LANES : (j // 2 + 1) * LANES].astype(F32)
        vals = wv_ref[:, j // 2 * LANES : (j // 2 + 1) * LANES].astype(F32)
        if j % 2 == 0:
            pair = both(keys, pltpu.roll(vals, HD, 1))
        else:
            pair = both(pltpu.roll(keys, HD, 1), vals)
        kv_parts[j] = pair.astype(BF)

    greet(shard, replica, (1, 2, 3), (1, 2, 4))

    mine = pl.ds(pl.multiple_of(quarter * q_rows, q_rows), q_rows)
    other_chip = 1 - x
    across_q = links.to(wq_ref.at[mine, lanes(other_chip, 2 * q_cols)], near_q, 2)
    across_kv = links.to(kv_parts.at[pl.ds(2 * other_chip, 2), mine], near_kv, 2)
    gain_copies = [links.to(gain_ref, gains.at[shard], m) for m in (1, 2, 3)]
    own_rows = [
        pl.ds(pl.multiple_of(shard * tokens + i * half, half), half) for i in range(2)
    ]
    x_across = [
        links.to(x_ref.at[pl.ds(i * half, half)], x_all.at[own_rows[i]], 2)
        for i in range(2)
    ]
    eighth_rows = pl.ds(pl.multiple_of(eighth * f_rows, f_rows), f_rows)
    ff_near = (near_gate, near_up)
    ff_across = [
        links.to(ref.at[eighth_rows, lanes(other_chip, 2 * ff_cols)], near, 2)
        for ref, near in zip((gate_ref, up_ref), ff_near)
    ]
    first_rows = pl.ds(0, half)
    cot_across = links.to(cot_ref.at[first_rows], cot_all_ref.at[own_rows[0]], 2)
    x_beside = links.to(x_ref, x_all.at[block(shard)], 1)
    own_w = pl.ds(pl.multiple_of(shard * rows, rows), rows)
    pair_shard = shard ^ 1
    w_beside = [
        links.to(
            wq_ref.at[:, lanes(pair_shard, q_cols)], w_heads.at[own_w, :q_cols], 1
        ),
        links.to(kv_parts.at[pair_shard], w_heads.at[own_w, q_cols:], 1),
    ]
    here = [
        links.here(x_ref, x_all.at[block(shard)]),
        links.here(gain_ref, gains.at[shard]),
        links.here(wq_ref.at[:, lanes(shard, q_cols)], w_heads.at[own_w, :q_cols]),
        links.here(kv_parts.at[shard], w_heads.at[own_w, q_cols:]),
    ]
    own_ff_in = [
        links.here(ref.at[:, lanes(shard, ff_cols)], own_ff.at[i])
        for i, ref in enumerate((gate_ref, up_ref))
    ]
    here_late = [links.here(cot_ref, cot_all_ref.at[block(shard)])]

    def rows_from(mask, of):
        return pl.ds(
            pl.multiple_of((shard ^ mask) * rows + (quarter ^ of) * q_rows, q_rows),
            q_rows,
        )

    across_q.wait_recv()
    across_kv.wait_recv()
    near_rows, far_rows = rows_from(2, 0), rows_from(3, 0)
    pair_lanes = lanes(1 - core, q_cols)
    core_q = links.to(near_q.at[:, pair_lanes], w_heads.at[near_rows, :q_cols], 1)
    core_kv = links.to(near_kv.at[1 - core], w_heads.at[near_rows, q_cols:], 1)
    near_copies = [
        links.here(near_q.at[:, lanes(core, q_cols)], w_heads.at[near_rows, :q_cols]),
        links.here(near_kv.at[core], w_heads.at[near_rows, q_cols:]),
    ]
    for copy in near_copies:
        copy.wait()
    y_near, z_near = (
        links.to(w_heads.at[near_rows], w_heads.at[near_rows], 0, m) for m in (1, 2)
    )
    core_q.wait_recv()
    core_kv.wait_recv()
    y_far, z_far = (
        links.to(w_heads.at[far_rows], w_heads.at[far_rows], 0, m) for m in (1, 2)
    )

    for copy in here:
        copy.wait()
    for copy in gain_copies:
        copy.wait_recv()
    gains_ref[...] = gains[...]
    norm_rows(x_all, norm1, gains, 0, shard * tokens, tokens)
    x_beside.wait_recv()
    norm_rows(x_all, norm1, gains, 0, (shard ^ 1) * tokens, tokens)

    y_near.wait_recv()
    y_far.wait_recv()
    z_forward = [
        links.to(w_heads.at[r], w_heads.at[r], 0, 2)
        for r in (rows_from(2, 1), rows_from(3, 1))
    ]
    x_core = []
    for i in range(2):
        x_across[i].wait_recv()
        got = pl.ds(pl.multiple_of((shard ^ 2) * tokens + i * half, half), half)
        x_core.append(links.to(x_all.at[got], x_all.at[got], 1))
        norm_rows(x_all, norm1, gains, 0, (shard ^ 2) * tokens + i * half, half)
    for copy in w_beside + [z_near, z_far] + z_forward:
        copy.wait_recv()
    w_heads_out = links.here(w_heads, w_heads_ref)

    def project(mask):
        r = block(shard ^ mask)
        pre[r, :] = matmul(norm1[r, :], w_heads[...])

    project(0)
    project(1)
    for i in range(2):
        x_core[i].wait_recv()
        norm_rows(x_all, norm1, gains, 0, (shard ^ 3) * tokens + i * half, half)
    norm1_out = links.here(norm1, norm1_ref)
    for i in range(2):
        own_ff_in[i].wait()
        cols = slice(i * ff_cols, (i + 1) * ff_cols)
        here_late.append(links.here(own_ff.at[i], w_ff_ref.at[own_w, cols]))
    w_beside_ff = [
        links.to(ref.at[:, lanes(pair_shard, ff_cols)], w_ff_ref.at[own_w, cols], 1)
        for ref, cols in (
            (gate_ref, slice(0, ff_cols)),
            (up_ref, slice(ff_cols, 2 * ff_cols)),
        )
    ]
    cot_beside = links.to(cot_ref, cot_all_ref.at[block(shard)], 1)
    project(2)
    project(3)

    ff_cols_of = (slice(0, ff_cols), slice(ff_cols, 2 * ff_cols))
    ff_core, ff_z2, ff_z1, ff_y = ([[], []] for _ in range(4))
    ff_here = []

    def ff_at(k, mask, of):
        start = (shard ^ mask) * rows + (eighth ^ of) * f_rows
        return w_ff_ref.at[pl.ds(pl.multiple_of(start, f_rows), f_rows), ff_cols_of[k]]

    def ff_arrived(k):
        ff_across[k].wait_recv()
        near = ff_near[k].at[:, lanes(core, ff_cols)]
        pair = ff_near[k].at[:, lanes(1 - core, ff_cols)]
        ff_core[k] = links.to(pair, ff_at(k, 2, 0), 1)
        for way, where in ((ff_z2, 4), (ff_z1, 2), (ff_y, 1)):
            way[k].append(links.to(near, ff_at(k, 2, 0), 0, where))
        ff_here.append(links.here(near, ff_at(k, 2, 0)))

    def ff_paired(k):
        ff_core[k].wait_recv()
        for way, where in ((ff_z2, 4), (ff_z1, 2), (ff_y, 1)):
            way[k].append(links.to(ff_at(k, 3, 0), ff_at(k, 3, 0), 0, where))

    def ff_handed(k):
        for copy in ff_z2[k]:
            copy.wait_recv()
        for mask in (2, 3):
            for way, where in ((ff_z1, 2), (ff_y, 1)):
                way[k].append(links.to(ff_at(k, mask, 4), ff_at(k, mask, 4), 0, where))

    def ff_last(k):
        for copy in ff_z1[k]:
            copy.wait_recv()
        for of in (2, 6):
            for mask in (2, 3):
                ff_y[k].append(
                    links.to(ff_at(k, mask, of), ff_at(k, mask, of), 0, 1)
                )

    kv = pre[:, q_cols:]
    kv = (kv * table_ref[2] + turned(kv) * table_ref[3]).astype(BF)
    heads_ref[:, q_cols:] = kv
    kv = kv.astype(F32)
    swapped = pltpu.roll(kv, HD, 1)
    kk_ref[...] = both(kv, swapped).astype(BF)
    vv_ref[...] = both(swapped, jnp.ones_like(kv)).astype(BF)

    ff_arrived(0)

    def attend_rows(i):
        q_rows_i = slice(i * tokens, (i + 1) * tokens)
        seen = (i + 1) * tokens

        def pair_step(j, carry):
            cols = pl.ds(pl.multiple_of(j * LANES, LANES), LANES)
            q = pre[q_rows_i, cols]
            q = q * table_ref[0, q_rows_i] + turned(q) * table_ref[1, q_rows_i]
            q = (q.astype(BF).astype(F32) * HD**-0.5).astype(BF)
            heads_ref[q_rows_i, cols] = q
            scores = matmul_right_t(two_heads(q), kk_ref[:seen])
            scores = causal_mask(scores, i * tokens)
            peak = jnp.max(scores, axis=-1, keepdims=True)
            exps = jnp.exp(scores - peak).astype(BF)
            out = matmul(exps, vv_ref[:seen])
            first, second = out[:tokens], out[tokens:]
            first_r, second_r = pltpu.roll(first, HD, 1), pltpu.roll(second, HD, 1)
            total = both(first_r, second)
            mixed_ref[q_rows_i, cols] = (both(first, second_r) / total).astype(BF)
            peaks = [
                jnp.broadcast_to(p, (tokens, LANES)) for p in (peak[:tokens], peak[tokens:])
            ]
            log_ref[q_rows_i, cols] = both(*peaks) + jnp.log(total)
            return carry

        lax.fori_loop(0, q_cols // LANES, pair_step, 0)

    def out_term(index):
        r = block(index)

        def step(j, carry):
            cols = pl.ds(pl.multiple_of(j * 512, 512), 512)
            term[:, cols] = matmul(mixed_ref[r, :], wo_ref[:, cols])
            return carry

        lax.fori_loop(0, model // 512, step, 0)

    def attend_block(index):
        for i in range(S):
            pl.when(index == i)(functools.partial(attend_rows, i))

    attend_block(shard ^ 3)
    out_term(shard ^ 3)
    far_out[...] = term[...].astype(BF)
    far = links.to(far_out, far_in, 1)
    ff_paired(0)
    ff_arrived(1)
    attend_block(shard ^ 2)
    out_term(shard ^ 2)
    far.wait_recv()
    across = []
    for i in range(2):
        r = slice(i * half, (i + 1) * half)
        across_out[r] = (term[r] + far_in[r].astype(F32)).astype(BF)
        across.append(links.to(across_out.at[r], across_in.at[r], 2))
    ff_paired(1)
    attend_block(shard ^ 1)
    out_term(shard ^ 1)
    beside_out[...] = term[...].astype(BF)
    beside = links.to(beside_out, beside_in, 1)
    attend_block(shard)
    out_term(shard)
    ff_handed(0)
    beside.wait_recv()
    term[...] += x_ref[...].astype(F32) + beside_in[...].astype(F32)
    n2_across, n2_beside, n2_here = [], [], []
    for i in range(2):
        r = slice(i * half, (i + 1) * half)
        across[i].wait_recv()
        mid_ref[r] = term[r] + across_in[r].astype(F32)
        norm_rows(mid_ref, norm2, gains, 1, i * half, half)
        n2_across.append(links.to(norm2.at[r], norm2_ref.at[own_rows[i]], 2))
        n2_beside.append(links.to(norm2.at[r], norm2_ref.at[own_rows[i]], 1))
        n2_here.append(links.here(norm2.at[r], norm2_ref.at[own_rows[i]]))
        if i == 0:
            ff_last(0)
    ff_handed(1)
    cot_across.wait_recv()
    got = pl.ds(pl.multiple_of((shard ^ 2) * tokens, half), half)
    cot_core = links.to(cot_all_ref.at[got], cot_all_ref.at[got], 1)
    n2_core = []
    for i in range(2):
        n2_across[i].wait_recv()
        got = pl.ds(pl.multiple_of((shard ^ 2) * tokens + i * half, half), half)
        n2_core.append(links.to(norm2_ref.at[got], norm2_ref.at[got], 1))
        if i == 0:
            ff_last(1)
    for copy in w_beside_ff + [cot_beside] + n2_beside + n2_core + [cot_core]:
        copy.wait_recv()
    for copy in ff_y[0] + ff_y[1]:
        copy.wait_recv()
    for copy in here_late + ff_here + n2_here + [norm1_out, w_heads_out]:
        copy.wait()
    links.close()


def front(x, cot, gains, wq, wk, wv, wo, gate, up, tables):
    tokens, model = x.shape
    seq_len, rows = S * tokens, wq.shape[0]
    q_cols, ff_cols = wq.shape[1] // S, gate.shape[1] // S
    width, q_rows = q_cols + LANES, rows // 4
    shape = jax.ShapeDtypeStruct
    chip_ff = (rows // 8, 2 * ff_cols)
    row_block = pltpu.VMEM((tokens, model), BF)
    return pl.pallas_call(
        front_kernel,
        out_shape=(
            shape((seq_len, model), BF),
            shape((seq_len, width), BF),
            shape((seq_len, q_cols), F32),
            shape((seq_len, q_cols), BF),
            shape((S * rows, width), BF),
            shape((tokens, model), F32),
            shape((seq_len, model), BF),
            shape((S * rows, 2 * ff_cols), BF),
            shape((seq_len, model), BF),
            shape((S, 16, rows), BF),
        ),
        in_specs=[VMEM, VMEM, VMEM, ANY, VMEM, VMEM, VMEM, ANY, ANY, VMEM],
        out_specs=[ANY, VMEM, VMEM, VMEM, ANY, VMEM, ANY, ANY, ANY, VMEM],
        scratch_shapes=[
            pltpu.VMEM((seq_len, model), BF),
            pltpu.VMEM((S, 16, rows), BF),
            pltpu.VMEM((S, rows, LANES), BF),
            pltpu.VMEM((q_rows, 2 * q_cols), BF),
            pltpu.VMEM((2, q_rows, LANES), BF),
            pltpu.VMEM(chip_ff, BF),
            pltpu.VMEM(chip_ff, BF),
            pltpu.VMEM((S * rows, width), BF),
            pltpu.VMEM((seq_len, model), BF),
            pltpu.VMEM((seq_len, width), F32),
            pltpu.VMEM((seq_len, LANES), BF),
            pltpu.VMEM((seq_len, LANES), BF),
            row_block,
            row_block,
            row_block,
            row_block,
            row_block,
            row_block,
            pltpu.VMEM((tokens, model), F32),
            row_block,
            pltpu.VMEM((2, rows, ff_cols), BF),
            pltpu.SemaphoreType.DMA((96,)),
            pltpu.SemaphoreType.DMA((96,)),
            pltpu.SemaphoreType.DMA((24,)),
        ],
        compiler_params=pltpu.CompilerParams(
            collective_id=0, has_side_effects=True, vmem_limit_bytes=60 * 2**20
        ),
    )(x, cot, gains, wq, wk, wv, wo, gate, up, tables)


def by_rows(count, body, step=16):
    if count % step:
        body(pl.ds(0, count))
        return

    def one(i, carry):
        body(pl.ds(pl.multiple_of(i * step, step), step))
        return carry

    lax.fori_loop(0, count // step, one, 0)


class Scatter:
    def __init__(self, links, term, far_in, across_out, across_in, beside_in):
        self.links, self.term = links, term
        self.far_in, self.across_out = far_in, across_out
        self.across_in, self.beside_in = across_in, beside_in
        self.tokens = far_in.shape[0]
        self.half = self.tokens // 2
        self.starts = [
            [
                pl.multiple_of((links.shard ^ mask) * self.tokens + extra, 16)
                for extra in (0, self.half)
            ]
            for mask in range(S)
        ]

    def rows(self, mask, part=None):
        if part is None:
            return pl.ds(self.starts[mask][0], self.tokens)
        return pl.ds(self.starts[mask][part], self.half)

    def send_far(self):
        self.far = self.links.to(self.term.at[self.rows(3)], self.far_in, 1)

    def send_across(self):
        self.far.wait_recv()
        self.across = []
        base = self.starts[2][0]
        for i in range(2):

            def add(rows):
                start = i * self.half + rows.start
                here = pl.ds(pl.multiple_of(start, 16), rows.size)
                there = pl.ds(pl.multiple_of(base + start, 16), rows.size)
                total = self.term[there, :].astype(F32)
                total += self.far_in[here, :].astype(F32)
                self.across_out[here, :] = total.astype(BF)

            by_rows(self.half, add)
            part = pl.ds(i * self.half, self.half)
            self.across.append(
                self.links.to(self.across_out.at[part], self.across_in.at[part], 2)
            )

    def send_beside(self):
        self.beside = self.links.to(self.term.at[self.rows(1)], self.beside_in, 1)

    def finish(self, i, use):
        if i == 0:
            self.beside.wait_recv()
        self.across[i].wait_recv()
        base = self.starts[0][0]

        def one(rows):
            start = i * self.half + rows.start
            here = pl.ds(pl.multiple_of(start, 16), rows.size)
            there = pl.ds(pl.multiple_of(base + start, 16), rows.size)
            total = self.term[there, :].astype(F32)
            total += self.beside_in[here, :].astype(F32)
            total += self.across_in[here, :].astype(F32)
            use(here, total)

        by_rows(self.half, one)

    def release(self):
        for copy in [self.far, self.beside] + self.across:
            self.links.sent(copy)


STEPS = {
    "tff2": ("down0", "down1"),
    "pout": ("ff3",),
    "mix": ("ff2",),
    "gath1": ("down0",),
    "att0": ("ff1",),
    "att3": ("ff2", "ff3", "down1"),
    "w_rf3": ("down0",),
    "heads": ("ff1", "ff0"),
    "last": (
        ("ff2", "out0", "ff3", "down1", "ff0", "ff1", "heads0", "out0", "heads1")
        + ("heads0", "ff0", "out0", "heads1", "heads0", "heads1")
    ),
}


class Flow:
    def __init__(self, links, order, arrive, sends):
        self.links, self.arrive, self.sends = links, list(arrive), list(sends)
        self.bits = len(self.arrive)
        self.order = [b for b in order if b < self.bits]
        self.order += list(range(len(order), self.bits))
        self.left = list(range(self.bits - 1, -1, -1))
        self.sides = [(links.replica >> b) % 2 for b in range(self.bits)]
        self.others = [1 - side for side in self.sides]
        self.at = 0
        self.done = False

    def begin(self, term):
        self.parts = [term]
        self.step()

    def pick(self, bit, side):
        where = (slice(None),) * self.left.index(bit) + (side,)
        return [part.at[where] for part in self.parts]

    def step(self):
        bit = self.order[self.at]
        mine = self.sides[bit]
        if self.at:
            self.copy.wait_recv()
        other = self.pick(bit, self.others[bit])
        source = other[0]
        if self.at:
            source = self.sends[self.at - 1]
            self.add(other, source, len(self.left) - 1)
        self.copy = self.links.to(source, self.arrive[self.at], 0, 1 << bit)
        self.parts = self.pick(bit, mine) + [self.arrive[self.at]]
        self.left.remove(bit)
        self.at += 1

    def advance(self):
        if self.at < self.bits:
            self.step()
        elif not self.done:
            self.done = True
            self.conclude(self)

    def end(self, target):
        self.copy.wait_recv()
        self.add(self.parts, target, 0)

    def add(self, parts, target, free):
        ways = list(itertools.product(range(2), repeat=free))
        rest = parts[0].shape[free:]
        jobs = [(way, part) for way in ways for part in parts]

        def inner(fetch, sems):
            copies = []
            for n, (way, part) in enumerate(jobs):
                source = part.at[way] if way else part
                copy = pltpu.make_async_copy(source, fetch.at[n], sems.at[n])
                copy.start()
                copies.append(copy)
            for w, way in enumerate(ways):
                first = w * len(parts)
                for k in range(len(parts)):
                    copies[first + k].wait()
                leads = [()] if len(rest) == 2 else [(g,) for g in range(rest[0])]
                for lead in leads:

                    def one(rows):
                        total = fetch[(first,) + lead + (rows,)].astype(F32)
                        for k in range(1, len(parts)):
                            more = fetch[(first + k,) + lead + (rows,)]
                            total += more.astype(F32)
                        target[way + lead + (rows,)] = total.astype(target.dtype)

                    by_rows(rest[-2], one)

        pl.run_scoped(
            inner,
            pltpu.VMEM((len(jobs),) + tuple(rest), BF),
            pltpu.SemaphoreType.DMA((len(jobs),)),
        )


def bits_of(index, count):
    return tuple((index >> b) & 1 for b in reversed(range(count.bit_length() - 1)))


def turn(source, cols, target):
    rows = source.shape[0]
    for i in range(0, rows, 256):
        part = source[i : i + 256, cols]
        target[:, i : i + 256] = part.astype(F32).T.astype(BF)


def produce(left_t, right, first, size, stage, replicas, lead=(), tile=256):
    share = left_t.shape[0] // replicas

    def one(t, carry):
        start = pl.multiple_of(t * tile, LANES)
        cols = pl.ds(pl.multiple_of(first + start, LANES), tile)
        result = matmul(left_t[...], right[:, cols])
        for r in range(replicas):
            where = bits_of(r, replicas) + lead + (slice(None), pl.ds(start, tile))
            stage[where] = result[r * share : (r + 1) * share].astype(BF)
        return carry

    lax.fori_loop(0, size // tile, one, 0)


def stream(count, copies_of, use):
    for copy in copies_of(0, 0):
        copy.start()

    def one(t, carry):
        slot = t % 2

        @pl.when(t + 1 < count)
        def _():
            for copy in copies_of(t + 1, 1 - slot):
                copy.start()

        for copy in copies_of(t, slot):
            copy.wait()
        use(t, slot)
        return carry

    lax.fori_loop(0, count, one, 0)


def norm_back_rows(grad, values, gain_row):
    scale = rms_scale(values)
    weighted = grad * gain_row
    mean = jnp.mean(weighted * values, axis=-1, keepdims=True)
    return scale * weighted - values * (scale * scale * scale * mean)


def rear_kernel(
    norm2_hbm, cot_hbm, w_ff_hbm, w_down_hbm, norm1_hbm, mixed_hbm, w_out_hbm, heads_hbm, logs_hbm,
    table_hbm, w_heads_hbm, mid_ref, cot_ref, x_ref, gain_ref,
    output_ref, input_grad_ref, grad_out_ref, grad_down_ref, pieces_ff, pieces_heads, *others,
):
    shard, replica = lax.axis_index("shard"), lax.axis_index("replica")
    tokens, model = mid_ref.shape
    seq_len = S * tokens
    ff_cols, rows = w_down_hbm.shape[0], model // S
    width = heads_hbm.shape[1]
    q_cols = width - LANES
    replicas = model // (S * pieces_ff.shape[1])
    bits = replicas.bit_length() - 1
    share, share_down = pieces_ff.shape[1], grad_down_ref.shape[0]
    half, half_model = tokens // 2, model // 2
    others = list(others)

    def take(count):
        taken = others[:count]
        del others[:count]
        return taken

    hbm = {name: take(1 + bits) for name in ("ff", "down", "out", "heads")}
    cot_all, term, far_in, across_out, across_in, beside_in, grad_mid, grad_mid_b = take(8)
    sends = {name: take(bits) for name in ("ff", "down", "out", "heads")}
    send, recv, local, slots = take(4)
    links = Links(shard, replica, send, recv, local)
    other_chip = 1 - shard // 2

    def flow(name, order, index=None):
        pick = (lambda ref: ref) if index is None else (lambda ref: ref.at[index])
        made = Flow(
            links,
            order,
            [pick(ref) for ref in hbm[name][1:]],
            [pick(ref) for ref in sends[name][:-1]],
        )
        made.term, made.last = pick(hbm[name][0]), pick(sends[name][-1])
        return made

    ff_order = ((0, 1, 2), (0, 1, 2), (1, 0, 2), (0, 1, 2))
    flows_ff = [flow("ff", ff_order[m], m) for m in range(S)]
    flows_down = [flow("down", order, i) for i, order in enumerate(((0, 1, 2), (1, 2, 0)))]
    flow_out = flow("out", (0, 1, 2))
    flows_heads = [flow("heads", (0, 1, 2), i) for i in range(2)]
    flows = {"out0": flow_out}
    for name, many in (("ff", flows_ff), ("down", flows_down), ("heads", flows_heads)):
        flows.update({f"{name}{i}": made for i, made in enumerate(many)})
    finals, finals_here = [], []

    def deliver(piece, pieces, mask):
        if mask:
            finals.append(links.to(piece, pieces.at[mask], mask))
        else:
            finals_here.append(links.here(piece, pieces.at[mask]))

    def end_ff(mask, made):
        made.end(made.last)
        deliver(made.last, pieces_ff, mask)

    def end_down(i, made):
        made.end(made.last)
        cols = pl.ds(i * half_model, half_model)
        finals_here.append(links.here(made.last, grad_down_ref.at[:, cols]))

    def end_out(made):
        made.end(made.last)
        finals_here.append(links.here(made.last, grad_out_ref))

    def end_heads(i, made):
        made.end(made.last)
        for n, mask in enumerate(((3, 2), (1, 0))[i]):
            deliver(made.last.at[n], pieces_heads, mask)

    for i in range(S):
        flows_ff[i].conclude = functools.partial(end_ff, i)
    for i in range(2):
        flows_down[i].conclude = functools.partial(end_down, i)
        flows_heads[i].conclude = functools.partial(end_heads, i)
    flow_out.conclude = end_out

    def pump(point):
        for name in STEPS.get(point, ()):
            flows[name].advance()

    greet(shard, replica, (1, 2, 3), [1 << b for b in range(bits)])
    gain_one, gain_two = (
        jnp.concatenate(
            [gain_ref[j, i : i + 1, :].astype(F32) for j in range(S)], axis=1
        )
        for i in range(2)
    )
    sums = Scatter(links, term, far_in, across_out, across_in, beside_in)
    last_rows = pl.ds(half, half)
    cot_across = links.to(cot_ref.at[last_rows], cot_all.at[sums.rows(0, 1)], 2)
    chip_rows = pl.ds(pl.multiple_of(shard // 2 * 2 * tokens, 2 * tokens), 2 * tokens)

    def first_half(norm2, hidden, grad_ff):
        norm2_in = links.here(norm2_hbm, norm2)
        cot_in = [
            links.here(cot_hbm.at[r], cot_all.at[r])
            for r in (chip_rows, sums.rows(2, 0), sums.rows(3, 0))
        ]

        tile = 256
        tiles = [(i, min(tile, ff_cols - i)) for i in range(0, ff_cols, tile)]

        def over_tiles(copies_of, use):
            for copy in copies_of(0):
                copy.start()
            for t, (start, size) in enumerate(tiles):
                if t + 1 < len(tiles):
                    for copy in copies_of(t + 1):
                        copy.start()
                for copy in copies_of(t):
                    copy.wait()

                def block(b, carry):
                    use(pl.ds(pl.multiple_of(b * 512, 512), 512), start, size, t % 2)
                    return carry

                lax.fori_loop(0, seq_len // 512, block, 0)

        def gate_up(gates, ups):
            def copies_of(t):
                start, size = tiles[t]
                slot = t % 2
                cols = slice(start, start + size)
                up_cols = slice(ff_cols + start, ff_cols + start + size)
                return [
                    pltpu.make_async_copy(*pair, slots.at[slot, n])
                    for n, pair in enumerate(
                        (
                            (w_ff_hbm.at[:, cols], gates.at[slot, :, :size]),
                            (w_ff_hbm.at[:, up_cols], ups.at[slot, :, :size]),
                        )
                    )
                ]

            def use(r, start, size, slot):
                gate = matmul(norm2[r, :], gates[slot, :, :size])
                up = matmul(norm2[r, :], ups[slot, :, :size])
                silu = gate * (1.0 / (1.0 + jnp.exp(-gate)))
                hidden[r, start : start + size] = (silu * up).astype(BF)
                grad_ff[r, start : start + size] = gate.astype(BF)
                grad_ff[r, ff_cols + start : ff_cols + start + size] = up.astype(BF)

            norm2_in.wait()
            over_tiles(copies_of, use)

        weight_tile = pltpu.VMEM((2, model, tile), BF)
        pl.run_scoped(gate_up, weight_tile, weight_tile)
        cot_across.wait_recv()
        there = cot_all.at[sums.rows(2, 1)]
        cot_core = links.to(there, there, 1)
        for copy in cot_in:
            copy.wait()
        cot_core.wait_recv()
        links.sent(cot_core)

        def down_terms(left_t, stage):
            turn(hidden, slice(None), left_t)
            for i in range(2):
                produce(left_t, cot_all, i * half_model, half_model, stage, replicas)
                links.here(stage, flows_down[i].term).wait()
                flows_down[i].begin(flows_down[i].term)

        pl.run_scoped(
            down_terms,
            pltpu.VMEM((ff_cols, seq_len), BF),
            pltpu.VMEM((2,) * bits + (share_down, half_model), BF),
        )

        def hidden_grads(downs):
            def copies_of(t):
                start, size = tiles[t]
                slot = t % 2
                return [
                    pltpu.make_async_copy(
                        w_down_hbm.at[slice(start, start + size)],
                        downs.at[slot, :size],
                        slots.at[slot, 0],
                    )
                ]

            def use(r, start, size, slot):
                grad = matmul_right_t(cot_all[r, :], downs[slot, :size])
                cols = slice(start, start + size)
                up_cols = slice(ff_cols + start, ff_cols + start + size)
                gate, up = grad_ff[r, cols].astype(F32), grad_ff[r, up_cols].astype(F32)
                sigmoid = 1.0 / (1.0 + jnp.exp(-gate))
                slope = sigmoid * (1.0 + gate * (1.0 - sigmoid))
                grad_ff[r, cols] = (grad * up * slope).astype(BF)
                grad_ff[r, up_cols] = (grad * gate * sigmoid).astype(BF)

            over_tiles(copies_of, use)

        pl.run_scoped(hidden_grads, pltpu.VMEM((2, tile, model), BF))
        pump("hid")

        def norm_terms(chip):
            def inner(tiles):
                r = pl.ds(pl.multiple_of(chip * 2 * tokens, 2 * tokens), 2 * tokens)

                def copies_of(t, slot):
                    part = pl.ds(pl.multiple_of(t * 256, 256), 256)
                    return [
                        pltpu.make_async_copy(
                            w_ff_hbm.at[part], tiles.at[slot], slots.at[slot, 0]
                        )
                    ]

                def use(t, slot):
                    cols = pl.ds(pl.multiple_of(t * 256, 256), 256)
                    product = matmul_right_t(grad_ff[r, :], tiles[slot])
                    term[r, cols] = product.astype(BF)

                stream(model // 256, copies_of, use)

            pl.run_scoped(inner, pltpu.VMEM((2, 256, 2 * ff_cols), BF))

        norm_terms(other_chip)
        sums.send_far()
        pump("far")

        def ff_terms(left_t, stages):
            copies = {}

            def launch(n):
                copies[n][0].wait()
                if copies[n][1] is not flows_ff[0]:
                    copies[n][1].begin(copies[n][1].term)

            for n, mask in enumerate((3, 2, 1, 0)):
                cols = pl.ds(pl.multiple_of((shard ^ mask) * rows, rows), rows)
                turn(norm2, cols, left_t)
                if n:
                    launch(n - 1)
                produce(left_t, grad_ff, 0, 2 * ff_cols, stages.at[n % 2], replicas)
                copies[n] = (
                    links.here(stages.at[n % 2], flows_ff[mask].term),
                    flows_ff[mask],
                )
                if n == 0:
                    pump("w_rf")
                    sums.send_across()
                pump(f"tff{n}")
            launch(3)

        pl.run_scoped(
            ff_terms,
            pltpu.VMEM((rows, seq_len), BF),
            pltpu.VMEM((2,) + (2,) * bits + (share, 2 * ff_cols), BF),
        )
        norm_terms(1 - other_chip)
        sums.send_beside()
        pump("near")

        def to_mid(r, grad):
            values = mid_ref[r, :]
            total = cot_ref[r, :].astype(F32)
            total += norm_back_rows(grad, values, gain_two)
            grad_mid[r, :] = total
            grad_mid_b[r, :] = total.astype(BF)

        gathered = []
        for i in range(2):
            sums.finish(i, to_mid)
            part = slice(i * half, (i + 1) * half)
            there = sums.rows(0, i)
            gathered.append(
                [
                    links.to(grad_mid_b.at[part], cot_all.at[there], 2),
                    links.to(grad_mid_b.at[part], cot_all.at[there], 1),
                    links.here(grad_mid_b.at[part], cot_all.at[there]),
                ]
            )
        sums.release()
        pump("mid")

        def out_terms(tiles):
            def copies_of(t, slot):
                part = pl.ds(pl.multiple_of(t * 256, 256), 256)
                return [
                    pltpu.make_async_copy(
                        w_down_hbm.at[:, part], tiles.at[slot], slots.at[slot, 0]
                    )
                ]

            def use(t, slot):
                cols = pl.ds(pl.multiple_of(t * 256, 256), 256)
                term[:, cols] = matmul(hidden[...], tiles[slot]).astype(BF)

            stream(model // 256, copies_of, use)

        pl.run_scoped(out_terms, pltpu.VMEM((2, ff_cols, 256), BF))
        pump("pout")
        return gathered

    gathered = []
    pl.run_scoped(
        lambda *refs: gathered.extend(first_half(*refs)),
        pltpu.VMEM((seq_len, model), BF),
        pltpu.VMEM((seq_len, ff_cols), BF),
        pltpu.VMEM((seq_len, 2 * ff_cols), BF),
    )

    def second_half(mixed, w_out, heads, logs, table, w_heads, grad_mixed, grad_heads,
                    kk_ref, vv_ref, dk_ref, dv_ref):
        loads = [
            links.here(*pair)
            for pair in (
                (w_out_hbm, w_out),
                (heads_hbm, heads),
                (logs_hbm, logs),
                (table_hbm, table),
                (mixed_hbm, mixed),
                (w_heads_hbm, w_heads),
            )
        ]
        for i in range(2):
            gathered[i][1].wait_recv()
            gathered[i][2].wait()
        sums.send_far()
        sums.send_beside()
        for copy in loads:
            copy.wait()

        def mix(mask, part=None):
            r = sums.rows(mask, part)
            grad_mixed[r, :] = matmul_right_t(cot_all[r, :], w_out[...]).astype(BF)

        mix(0)
        mix(1)
        kv = heads[:, q_cols:].astype(F32)
        swapped = pltpu.roll(kv, HD, 1)
        kk_ref[...] = both(kv, swapped).astype(BF)
        vv_ref[...] = both(swapped, kv).astype(BF)
        dk_ref[...] = jnp.zeros_like(dk_ref)
        dv_ref[...] = jnp.zeros_like(dv_ref)
        pump("mix")
        forward = []
        for i in range(2):
            gathered[i][0].wait_recv()
            r = sums.rows(2, i)
            forward.append(links.to(cot_all.at[r], cot_all.at[r], 1))
            mix(2, i)
            pump(f"gath{i}")
        sums.send_across()
        flows_ff[0].begin(flows_ff[0].term)
        pump("across2")
        for i in range(2):
            forward[i].wait_recv()
            mix(3, i)

        def out_grad(left_t, stage):
            turn(mixed, slice(None), left_t)
            produce(left_t, cot_all, 0, model, stage, replicas)
            links.here(stage, flow_out.term).wait()
            flow_out.begin(flow_out.term)

        pl.run_scoped(
            out_grad,
            pltpu.VMEM((rows, seq_len), BF),
            pltpu.VMEM((2,) * bits + (share, model), BF),
        )

        def attend_rows(i):
            r = slice(i * tokens, (i + 1) * tokens)
            seen = (i + 1) * tokens

            def pair_step(j, carry):
                cols = pl.ds(pl.multiple_of(j * LANES, LANES), LANES)
                q = two_heads(heads[r, cols])
                grad = two_heads(grad_mixed[r, cols])
                log_pair = logs[r, cols]
                log_col = jnp.concatenate(
                    [log_pair[:, :1], log_pair[:, HD : HD + 1]], axis=0
                )
                mixed_pair = mixed[r, cols].astype(F32)
                product = grad.astype(F32) * jnp.concatenate([mixed_pair] * 2, axis=0)
                inner = jnp.sum(product, axis=-1, keepdims=True)
                scores = matmul_right_t(q, kk_ref[:seen])
                soft = jnp.exp(causal_mask(scores, i * tokens) - log_col)
                grad_soft = matmul_right_t(grad, vv_ref[:seen])
                grad_scores = (soft * (grad_soft - inner)).astype(BF)
                dq = matmul(grad_scores, kk_ref[:seen])
                dq = both(dq[:tokens], dq[tokens:]) * HD**-0.5
                dq = dq * table[0, r] - turned(dq) * table[1, r]
                grad_heads[r, cols] = dq.astype(BF)
                dk_ref[:seen] += matmul_left_t(grad_scores, q)
                dv_ref[:seen] += matmul_left_t(soft.astype(BF), grad)
                return carry

            lax.fori_loop(0, q_cols // LANES, pair_step, 0)

        pump("out")
        for i in range(S):
            attend_rows(i)
            pump(f"att{i}")
        dk, dv = dk_ref[...], dv_ref[...]
        dk, dv = dk + pltpu.roll(dk, HD, 1), dv + pltpu.roll(dv, HD, 1)
        dkv = both(dk, dv)
        dkv = dkv * table[2] - turned(dkv) * table[3]
        grad_heads[:, q_cols:] = dkv.astype(BF)

        def to_output(r, total):
            output_ref[r, :] = (mid_ref[r, :] + total).astype(BF)

        for i in range(2):
            sums.finish(i, to_output)
        sums.release()
        for mask in (1, 2):
            pl.semaphore_signal(
                credit.at[mask - 1],
                inc=1,
                device_id={"shard": shard ^ mask, "replica": replica},
                device_id_type=MESH_ID,
            )

        def head_terms(chip):
            r = pl.ds(pl.multiple_of(chip * 2 * tokens, 2 * tokens), 2 * tokens)

            def one(t, carry):
                cols = pl.ds(pl.multiple_of(t * 256, 256), 256)
                product = matmul_right_t(grad_heads[r, :], w_heads[cols, :])
                term[r, cols] = product.astype(BF)
                return carry

            lax.fori_loop(0, model // 256, one, 0)

        def head_grads(norm1, left_t, stages):
            norm1_in = links.here(norm1_hbm, norm1)
            head_terms(other_chip)
            pl.semaphore_wait(credit.at[0], 1)
            sums.send_far()
            norm1_in.wait()
            stage_out = []
            for i, masks in enumerate(((3, 2), (1, 0))):
                for n, mask in enumerate(masks):
                    cols = pl.ds(pl.multiple_of((shard ^ mask) * rows, rows), rows)
                    turn(norm1, cols, left_t)
                    produce(
                        left_t, grad_heads, 0, width, stages.at[i], replicas, (n,), LANES
                    )
                stage_out.append(links.here(stages.at[i], flows_heads[i].term))
                if i == 0:
                    pump("w_rf3")
                    pl.semaphore_wait(credit.at[1], 1)
                    sums.send_across()
                    stage_out[0].wait()
                    flows_heads[0].begin(flows_heads[0].term)
            stage_out[1].wait()
            flows_heads[1].begin(flows_heads[1].term)
            head_terms(1 - other_chip)
            sums.send_beside()

        pl.run_scoped(
            head_grads,
            pltpu.VMEM((seq_len, model), BF),
            pltpu.VMEM((rows, seq_len), BF),
            pltpu.VMEM((2,) + (2,) * bits + (2, share, width), BF),
        )
        pump("heads")

    credit = take(1)[0]
    pl.run_scoped(
        second_half,
        pltpu.VMEM((seq_len, q_cols), BF),
        pltpu.VMEM((q_cols, model), BF),
        pltpu.VMEM((seq_len, width), BF),
        pltpu.VMEM((seq_len, q_cols), F32),
        pltpu.VMEM((4, seq_len, LANES), F32),
        pltpu.VMEM((model, width), BF),
        pltpu.VMEM((seq_len, q_cols), BF),
        pltpu.VMEM((seq_len, width), BF),
        pltpu.VMEM((seq_len, LANES), BF),
        pltpu.VMEM((seq_len, LANES), BF),
        pltpu.VMEM((seq_len, LANES), F32),
        pltpu.VMEM((seq_len, LANES), F32),
    )

    def to_input_grad(r, grad):
        total = grad_mid[r, :]
        total += norm_back_rows(grad, x_ref[r, :].astype(F32), gain_one)
        input_grad_ref[r, :] = total.astype(BF)

    for i in range(2):
        sums.finish(i, to_input_grad)
    pump("last")
    waiting = list(flows.values())
    while waiting:
        for made in waiting:
            made.advance()
        waiting = [made for made in waiting if not made.done]
    for copy in finals:
        copy.wait_recv()
    for copy in finals_here:
        copy.wait()
    links.close()


def rear(norm2, cot_all, w_ff, w_down, norm1, mixed, w_out, heads, logs, tables, w_heads, mid, cot, x, gains, replicas):
    tokens, model = mid.shape
    seq_len, rows, ff_cols = S * tokens, model // S, w_down.shape[0]
    width = heads.shape[1]
    bits = replicas.bit_length() - 1
    share, share_down = rows // replicas, ff_cols // replicas
    shape = jax.ShapeDtypeStruct
    rests = {
        "ff": ((S,), (share, 2 * ff_cols), BF),
        "down": ((2,), (share_down, model // 2), F32),
        "out": ((), (share, model), F32),
        "heads": ((2,), (2, share, width), BF),
    }
    work, sends = [], []
    for many, rest, last in rests.values():
        work += [shape(many + (2,) * bits + rest, BF)]
        work += [shape(many + (2,) * n + rest, BF) for n in reversed(range(bits))]
        sends += [
            pltpu.VMEM(many + (2,) * n + rest, BF) for n in reversed(range(bits - 1))
        ]
        sends += [pltpu.VMEM(many + rest, last)]
    outs = (
        shape((tokens, model), BF),
        shape((tokens, model), BF),
        shape((share, model), F32),
        shape((share_down, model), F32),
        shape((S, share, 2 * ff_cols), BF),
        shape((S, share, width), BF),
    )
    row_block = pltpu.VMEM((tokens, model), BF)
    result = pl.pallas_call(
        rear_kernel,
        out_shape=outs + tuple(work),
        in_specs=[ANY] * 11 + [VMEM] * 4,
        out_specs=[VMEM] * 2 + [ANY] * (4 + len(work)),
        scratch_shapes=[
            pltpu.VMEM((seq_len, model), BF),
            pltpu.VMEM((seq_len, model), BF),
            row_block,
            row_block,
            row_block,
            row_block,
            pltpu.VMEM((tokens, model), F32),
            row_block,
        ]
        + sends
        + [
            pltpu.SemaphoreType.DMA((96,)),
            pltpu.SemaphoreType.DMA((96,)),
            pltpu.SemaphoreType.DMA((48,)),
            pltpu.SemaphoreType.DMA((2, 3)),
            pltpu.SemaphoreType.REGULAR((2,)),
        ],
        compiler_params=pltpu.CompilerParams(
            collective_id=1, has_side_effects=True, vmem_limit_bytes=62 * 2**20
        ),
    )(norm2, cot_all, w_ff, w_down, norm1, mixed, w_out, heads, logs, tables, w_heads, mid, cot, x, gains)
    return result[: len(outs)]


def on_device(
    inputs, cotangent, gain_attn, w_query, w_key, w_value, w_output, gain_mlp, w_gate, w_up, w_down
):
    shard, replica = lax.axis_index("shard"), lax.axis_index("replica")
    x, cot = inputs[0], cotangent[0]
    tables = jnp.asarray(rope_tables(S * x.shape[0]))
    gains = jnp.concatenate(
        [jnp.stack([gain_attn, gain_mlp]), jnp.zeros((14, w_query.shape[0]), BF)]
    )
    norm1, heads, logs, mixed, w_heads, mid, norm2, w_ff, cot_all, gains = front(
        x, cot, gains, w_query, w_key, w_value, w_output, w_gate, w_up, tables
    )
    output, input_grad, grad_output, grad_down, pieces_ff, pieces_heads = rear(
        norm2, cot_all, w_ff, w_down, norm1, mixed, w_output, heads, logs, tables,
        w_heads, mid, cot, x, gains, lax.axis_size("replica"),
    )
    grads, (grad_gain_two, grad_gain_one), moved = finish(
        (pieces_ff, pieces_heads),
        ((w_gate, w_up), (w_query, w_key, w_value)),
        (gain_mlp, gain_attn),
        (output, input_grad, grad_output, grad_down),
        shard,
        replica,
    )
    grad_gate, grad_up, grad_query, grad_key, grad_value = grads
    output, input_grad, grad_output, grad_down = moved
    return (
        output[None],
        input_grad[None],
        grad_gain_one,
        grad_query,
        grad_key,
        grad_value,
        grad_output,
        grad_gain_two,
        grad_gate,
        grad_up,
        grad_down,
    )


def solution(mesh):
    placed = (
        P("replica", "shard", None),
        P("replica", "shard", None),
        P("shard"),
        P("shard", None),
        P("shard", None),
        P("shard", None),
        P("shard", None),
        P("shard"),
        P("shard", None),
        P("shard", None),
        P("shard", None),
    )
    both_axes = ("shard", "replica")
    return jax.shard_map(
        on_device,
        mesh=mesh,
        in_specs=placed,
        out_specs=(
            P("replica", "shard", None),
            P("replica", "shard", None),
            P(both_axes),
            P(both_axes, None),
            P(both_axes, None),
            P(both_axes, None),
            P(both_axes, None),
            P(both_axes),
            P(both_axes, None),
            P(both_axes, None),
            P(both_axes, None),
        ),
        check_vma=False,
    )
```

```python
import functools
import itertools

import jax
import jax.numpy as jnp
import numpy as np
from jax import lax
from jax.experimental import pallas as pl
from jax.experimental.pallas import tpu as pltpu
from jax.sharding import PartitionSpec as P

H = 32
KV = 4
HD = 64
EPS = 1e-05
THETA = 10000.0
S = 4
BF = jnp.bfloat16
F32 = jnp.float32
LANES = 128
QB = 256


def matmul(left, right):
    return jnp.dot(left, right, preferred_element_type=F32)


def matmul_left_t(left, right):
    return lax.dot_general(
        left, right, (((0,), (0,)), ((), ())), preferred_element_type=F32
    )


def matmul_right_t(left, right):
    return lax.dot_general(
        left, right, (((1,), (1,)), ((), ())), preferred_element_type=F32
    )


def rms_scale(values):
    return lax.rsqrt(jnp.mean(values * values, axis=-1, keepdims=True) + EPS)


def finish_kernel(groups, moved, place_ref, *refs):
    refs = list(refs)

    def take(count):
        taken = refs[:count]
        del refs[:count]
        return taken

    many = [len(widths) for widths in groups]
    pieces, gains = take(len(groups)), take(len(groups))
    weights = [take(n) for n in many]
    sources = take(moved)
    outs, gain_outs = [take(n) for n in many], take(len(groups))
    targets = take(moved)
    held, staged = [take(n) for n in many], take(moved)
    sems = refs[0]
    shard, replica = place_ref[0], place_ref[1]
    copies = []

    def start(source, target):
        copies.append(pltpu.make_async_copy(source, target, sems.at[len(copies)]))
        copies[-1].start()

    for mine, kept in zip(weights, held):
        for weight, here in zip(mine, kept):
            rows = here.shape[0]
            start(weight.at[pl.ds(pl.multiple_of(replica * rows, rows), rows)], here)
    loads = list(copies)
    for source, stage in zip(sources, staged):
        start(source, stage)
    stages = copies[len(loads) :]
    for copy in loads:
        copy.wait()
    for copy, stage, target in zip(stages, staged, targets):
        copy.wait()
        start(stage, target)
    for g, widths in enumerate(groups):
        total = jnp.zeros((pieces[g].shape[1], 1), F32)
        for mask in range(S):
            piece = pieces[g].at[mask]
            owner = shard ^ mask
            begin = 0
            for width, weight, out in zip(widths, held[g], outs[g]):
                if width % LANES == 0:
                    cols = pl.ds(pl.multiple_of(owner * width, LANES), width)
                    part = piece[:, begin : begin + width].astype(F32)
                    out[:, cols] = part
                else:
                    base = begin // LANES * LANES
                    part = piece[:, base : base + LANES].astype(F32)
                    lane = lax.broadcasted_iota(jnp.int32, part.shape, 1) // HD
                    side = owner % 2
                    part = jnp.where(
                        side == (begin - base) // HD, part, pltpu.roll(part, HD, 1)
                    )
                    part = jnp.where(lane == side, part, 0.0)
                    cols = pl.ds(pl.multiple_of(owner // 2 * LANES, LANES), LANES)
                    out[:, cols] = jnp.where(lane == side, part, out[:, cols])
                total += jnp.sum(
                    part * weight[:, cols].astype(F32), axis=1, keepdims=True
                )
                begin += width
        rows = total.shape[0]
        turned_total = jnp.broadcast_to(total, (rows, LANES)).T
        gain_outs[g][...] = turned_total[:1, :rows] / gains[g][...]
    for copy in copies[len(loads) + moved :]:
        copy.wait()


def finish(pieces, weights, gains, moved, shard, replica):
    rows = pieces[0].shape[1]
    groups = [tuple(w.shape[1] // S for w in mine) for mine in weights]
    flat = [w for mine in weights for w in mine]
    own_gains = [
        lax.dynamic_slice_in_dim(gain, replica * rows, rows, 0)
        .astype(F32)
        .reshape(1, rows)
        for gain in gains
    ]
    shapes = [jax.ShapeDtypeStruct((rows, w.shape[1]), F32) for w in flat]
    shapes += [jax.ShapeDtypeStruct((1, rows), F32)] * len(groups)
    shapes += [jax.ShapeDtypeStruct(a.shape, a.dtype) for a in moved]
    vmem, hbm = (pl.BlockSpec(memory_space=m) for m in (pltpu.VMEM, pl.ANY))
    held = len(flat) + len(groups)
    result = pl.pallas_call(
        functools.partial(finish_kernel, groups, len(moved)),
        out_shape=shapes,
        in_specs=[pl.BlockSpec(memory_space=pltpu.SMEM)]
        + [vmem] * (2 * len(groups))
        + [hbm] * (len(flat) + len(moved)),
        out_specs=[vmem] * held + [hbm] * len(moved),
        scratch_shapes=[pltpu.VMEM((rows, w.shape[1]), BF) for w in flat]
        + [pltpu.VMEM(a.shape, a.dtype) for a in moved]
        + [pltpu.SemaphoreType.DMA((len(flat) + 2 * len(moved),))],
        compiler_params=pltpu.CompilerParams(vmem_limit_bytes=62 * 2**20),
    )(
        jnp.stack([shard, replica]).astype(jnp.int32),
        *pieces,
        *own_gains,
        *flat,
        *moved,
    )
    return (
        result[: len(flat)],
        [gain.reshape(rows) for gain in result[len(flat) : held]],
        result[held:],
    )


def rope_tables(seq_len):
    half = HD // 2
    freq = THETA ** (-2.0 * np.arange(half, dtype=np.float64) / HD)
    angles = np.arange(seq_len, dtype=np.float64)[:, None] * freq[None, :]
    cos, sin = np.cos(angles), np.sin(angles)
    one, zero = np.ones((seq_len, HD)), np.zeros((seq_len, HD))
    cos_head = np.concatenate([cos, cos], 1)
    sin_head = np.concatenate([-sin, sin], 1)
    tables = [
        np.concatenate([cos_head, cos_head], 1),
        np.concatenate([sin_head, sin_head], 1),
        np.concatenate([cos_head, one], 1),
        np.concatenate([sin_head, zero], 1),
    ]
    return np.stack(tables).astype(np.float32)


def turned(values):
    lane = lax.broadcasted_iota(jnp.int32, values.shape, 1)
    return jnp.where(
        lane % HD < HD // 2,
        pltpu.roll(values, LANES - HD // 2, 1),
        pltpu.roll(values, HD // 2, 1),
    )


def both(first, second):
    lane = lax.broadcasted_iota(jnp.int32, first.shape, 1)
    return jnp.where(lane < HD, first, second)


def two_heads(pair):
    zero = jnp.zeros_like(pair)
    return jnp.concatenate([both(pair, zero), both(zero, pair)], axis=0)


def causal_mask(scores, first_row):
    block = scores.shape[0] // 2
    last = scores[:, first_row:]
    row = lax.broadcasted_iota(jnp.int32, last.shape, 0) % block
    col = lax.broadcasted_iota(jnp.int32, last.shape, 1)
    last = jnp.where(col <= row, last, -1e30)
    if not first_row:
        return last
    return jnp.concatenate([scores[:, :first_row], last], axis=1)


MESH_ID = pl.DeviceIdType.MESH
ANY = pl.BlockSpec(memory_space=pl.ANY)
VMEM = pl.BlockSpec(memory_space=pltpu.VMEM)


class Copy:
    def __init__(self, describe, only=None):
        self.describe, self.only = describe, only
        self.where(lambda: describe().start())

    def where(self, act):
        act() if self.only is None else pl.when(self.only)(act)

    def wait(self):
        self.describe().wait()

    def wait_recv(self):
        self.describe().wait_recv()

    def wait_send(self):
        self.where(lambda: self.describe().wait_send())


class Links:
    def __init__(self, shard, replica, send, recv, local):
        self.shard, self.replica = shard, replica
        self.send, self.recv, self.local = send, recv, local
        self.used, self.used_local = 0, 0
        self.open = []

    def to(self, source, target, shard=0, replica=0, only=None):
        n, self.used = self.used, self.used + 1
        copy = Copy(
            lambda: pltpu.make_async_remote_copy(
                src_ref=source,
                dst_ref=target,
                send_sem=self.send.at[n],
                recv_sem=self.recv.at[n],
                device_id={
                    "shard": self.shard ^ shard,
                    "replica": self.replica ^ replica,
                },
                device_id_type=MESH_ID,
            ),
            only,
        )
        self.open.append(copy)
        return copy

    def here(self, source, target):
        n, self.used_local = self.used_local, self.used_local + 1
        return Copy(
            lambda: pltpu.make_async_copy(source, target, self.local.at[n])
        )

    def sent(self, copy):
        copy.wait_send()
        self.open = [other for other in self.open if other is not copy]

    def close(self):
        for copy in self.open:
            copy.wait_send()


def greet(shard, replica, shard_masks, replica_masks):
    barrier = pltpu.get_barrier_semaphore()
    for mask in shard_masks:
        pl.semaphore_signal(
            barrier,
            inc=1,
            device_id={"shard": shard ^ mask, "replica": replica},
            device_id_type=MESH_ID,
        )
    for mask in replica_masks:
        pl.semaphore_signal(
            barrier,
            inc=1,
            device_id={"shard": shard, "replica": replica ^ mask},
            device_id_type=MESH_ID,
        )
    pl.semaphore_wait(barrier, len(shard_masks) + len(replica_masks))


def norm_rows(source, target, gains, which, start, count):
    model = source.shape[1]
    part = model // S

    def step(i, carry):
        rows = pl.ds(pl.multiple_of(start + i * 16, 16), 16)
        values = source[rows, :].astype(F32)
        scale = rms_scale(values)
        for j in range(S):
            gain = gains[j, which : which + 1, :].astype(F32)
            cols = slice(j * part, (j + 1) * part)
            target[rows, cols] = (values[:, cols] * scale * gain).astype(BF)
        return carry

    lax.fori_loop(0, count // 16, step, 0, unroll=2)


def front_kernel(
    x_ref, cot_ref, gain_ref, wq_ref, wk_ref, wv_ref, wo_ref, gate_ref, up_ref, table_ref,
    norm1_ref, heads_ref, log_ref, mixed_ref, w_heads_ref, mid_ref, norm2_ref, w_ff_ref, cot_all_ref, gains_ref,
    x_all, gains, kv_parts, near_q, near_kv, near_gate, near_up, w_heads, norm1, pre, kk_ref, vv_ref,
    far_out, far_in, across_out, across_in, beside_out, beside_in, term, norm2, own_ff, send, recv, local,
):
    shard, replica = lax.axis_index("shard"), lax.axis_index("replica")
    x, core, quarter, eighth = shard // 2, shard % 2, replica % 4, replica % 8
    tokens, model = x_ref.shape
    seq_len = S * tokens
    rows = wq_ref.shape[0]
    q_cols, ff_cols = wq_ref.shape[1] // S, gate_ref.shape[1] // S
    width = q_cols + LANES
    q_rows, f_rows, half = rows // 4, rows // 8, tokens // 2
    links = Links(shard, replica, send, recv, local)

    def lanes(index, size):
        return pl.ds(pl.multiple_of(index * size, LANES), size)

    def block(index, size=tokens, extra=0):
        return pl.ds(pl.multiple_of(index * size + extra, 16), size)

    for j in range(S):
        keys = wk_ref[:, j // 2 * LANES : (j // 2 + 1) * LANES].astype(F32)
        vals = wv_ref[:, j // 2 * LANES : (j // 2 + 1) * LANES].astype(F32)
        if j % 2 == 0:
            pair = both(keys, pltpu.roll(vals, HD, 1))
        else:
            pair = both(pltpu.roll(keys, HD, 1), vals)
        kv_parts[j] = pair.astype(BF)

    greet(shard, replica, (1, 2, 3), (1, 2, 4))

    mine = pl.ds(pl.multiple_of(quarter * q_rows, q_rows), q_rows)
    other_chip = 1 - x
    across_q = links.to(wq_ref.at[mine, lanes(other_chip, 2 * q_cols)], near_q, 2)
    across_kv = links.to(kv_parts.at[pl.ds(2 * other_chip, 2), mine], near_kv, 2)
    gain_copies = [links.to(gain_ref, gains.at[shard], m) for m in (1, 2, 3)]
    own_rows = [
        pl.ds(pl.multiple_of(shard * tokens + i * half, half), half) for i in range(2)
    ]
    x_across = [
        links.to(x_ref.at[pl.ds(i * half, half)], x_all.at[own_rows[i]], 2)
        for i in range(2)
    ]
    ff_near, ff_split = (near_gate, near_up), ((eighth, f_rows), (quarter, q_rows))
    ff_across = [
        links.to(
            ref.at[
                pl.ds(pl.multiple_of(index * size, size), size),
                lanes(other_chip, 2 * ff_cols),
            ],
            near,
            2,
        )
        for ref, near, (index, size) in zip((gate_ref, up_ref), ff_near, ff_split)
    ]
    first_rows = pl.ds(0, half)
    cot_across = links.to(cot_ref.at[first_rows], cot_all_ref.at[own_rows[0]], 2)
    x_beside = links.to(x_ref, x_all.at[block(shard)], 1)
    own_w = pl.ds(pl.multiple_of(shard * rows, rows), rows)
    pair_shard = shard ^ 1
    w_beside = [
        links.to(
            wq_ref.at[:, lanes(pair_shard, q_cols)], w_heads.at[own_w, :q_cols], 1
        ),
        links.to(kv_parts.at[pair_shard], w_heads.at[own_w, q_cols:], 1),
    ]
    here = [
        links.here(x_ref, x_all.at[block(shard)]),
        links.here(gain_ref, gains.at[shard]),
        links.here(wq_ref.at[:, lanes(shard, q_cols)], w_heads.at[own_w, :q_cols]),
        links.here(kv_parts.at[shard], w_heads.at[own_w, q_cols:]),
    ]
    own_ff_in = [
        links.here(ref.at[:, lanes(shard, ff_cols)], own_ff.at[i])
        for i, ref in enumerate((gate_ref, up_ref))
    ]
    here_late = [links.here(cot_ref, cot_all_ref.at[block(shard)])]

    def rows_from(mask, of):
        return pl.ds(
            pl.multiple_of((shard ^ mask) * rows + (quarter ^ of) * q_rows, q_rows),
            q_rows,
        )

    across_q.wait_recv()
    across_kv.wait_recv()
    near_rows, far_rows = rows_from(2, 0), rows_from(3, 0)
    pair_lanes = lanes(1 - core, q_cols)
    core_q = links.to(near_q.at[:, pair_lanes], w_heads.at[near_rows, :q_cols], 1)
    core_kv = links.to(near_kv.at[1 - core], w_heads.at[near_rows, q_cols:], 1)
    near_copies = [
        links.here(near_q.at[:, lanes(core, q_cols)], w_heads.at[near_rows, :q_cols]),
        links.here(near_kv.at[core], w_heads.at[near_rows, q_cols:]),
    ]
    for copy in near_copies:
        copy.wait()
    y_near, z_near = (
        links.to(w_heads.at[near_rows], w_heads.at[near_rows], 0, m) for m in (1, 2)
    )
    core_q.wait_recv()
    core_kv.wait_recv()
    y_far, z_far = (
        links.to(w_heads.at[far_rows], w_heads.at[far_rows], 0, m) for m in (1, 2)
    )

    for copy in here:
        copy.wait()
    for copy in gain_copies:
        copy.wait_recv()
    gains_ref[...] = gains[...]
    norm_rows(x_all, norm1, gains, 0, shard * tokens, tokens)
    x_beside.wait_recv()
    norm_rows(x_all, norm1, gains, 0, (shard ^ 1) * tokens, tokens)

    y_near.wait_recv()
    y_far.wait_recv()
    z_forward = [
        links.to(w_heads.at[r], w_heads.at[r], 0, 2)
        for r in (rows_from(2, 1), rows_from(3, 1))
    ]
    x_core = []
    for i in range(2):
        x_across[i].wait_recv()
        got = pl.ds(pl.multiple_of((shard ^ 2) * tokens + i * half, half), half)
        x_core.append(links.to(x_all.at[got], x_all.at[got], 1))
        norm_rows(x_all, norm1, gains, 0, (shard ^ 2) * tokens + i * half, half)
    for copy in w_beside + [z_near, z_far] + z_forward:
        copy.wait_recv()
    w_heads_out = links.here(w_heads, w_heads_ref)

    def project(mask):
        r = block(shard ^ mask)
        pre[r, :] = matmul(norm1[r, :], w_heads[...])

    project(0)
    project(1)
    for i in range(2):
        x_core[i].wait_recv()
        norm_rows(x_all, norm1, gains, 0, (shard ^ 3) * tokens + i * half, half)
    norm1_out = links.here(norm1, norm1_ref)
    for i in range(2):
        own_ff_in[i].wait()
        cols = slice(i * ff_cols, (i + 1) * ff_cols)
        here_late.append(links.here(own_ff.at[i], w_ff_ref.at[own_w, cols]))
    w_beside_ff = [
        links.to(ref.at[:, lanes(pair_shard, ff_cols)], w_ff_ref.at[own_w, cols], 1)
        for ref, cols in (
            (gate_ref, slice(0, ff_cols)),
            (up_ref, slice(ff_cols, 2 * ff_cols)),
        )
    ]
    cot_beside = links.to(cot_ref, cot_all_ref.at[block(shard)], 1)
    project(2)
    project(3)

    ff_cols_of = (slice(0, ff_cols), slice(ff_cols, 2 * ff_cols))
    ff_core, ff_z2, ff_z1, ff_y = ([[], []] for _ in range(4))
    ff_here = []

    def ff_at(k, mask, of):
        index, size = ff_split[k]
        start = (shard ^ mask) * rows + (index ^ of) * size
        return w_ff_ref.at[pl.ds(pl.multiple_of(start, size), size), ff_cols_of[k]]

    ff_ways = (((ff_z2, 4), (ff_z1, 2), (ff_y, 1)), ((ff_z1, 2), (ff_y, 1)))

    def ff_arrived(k):
        ff_across[k].wait_recv()
        near = ff_near[k].at[:, lanes(core, ff_cols)]
        pair = ff_near[k].at[:, lanes(1 - core, ff_cols)]
        ff_core[k] = links.to(pair, ff_at(k, 2, 0), 1)
        for way, where in ff_ways[k]:
            way[k].append(links.to(near, ff_at(k, 2, 0), 0, where))
        ff_here.append(links.here(near, ff_at(k, 2, 0)))

    def ff_paired(k):
        ff_core[k].wait_recv()
        for way, where in ff_ways[k]:
            way[k].append(links.to(ff_at(k, 3, 0), ff_at(k, 3, 0), 0, where))

    def ff_handed(k):
        for copy in ff_z2[k]:
            copy.wait_recv()
        for mask in (2, 3):
            for way, where in ((ff_z1, 2), (ff_y, 1)):
                way[k].append(links.to(ff_at(k, mask, 4), ff_at(k, mask, 4), 0, where))

    def ff_last(k):
        for copy in ff_z1[k]:
            copy.wait_recv()
        for of in ((2, 6), (2,))[k]:
            for mask in (2, 3):
                ff_y[k].append(
                    links.to(ff_at(k, mask, of), ff_at(k, mask, of), 0, 1)
                )

    kv = pre[:, q_cols:]
    kv = (kv * table_ref[2] + turned(kv) * table_ref[3]).astype(BF)
    heads_ref[:, q_cols:] = kv
    kv = kv.astype(F32)
    swapped = pltpu.roll(kv, HD, 1)
    kk_ref[...] = both(kv, swapped).astype(BF)
    vv_ref[...] = both(swapped, jnp.ones_like(kv)).astype(BF)

    ff_arrived(0)

    def attend_rows(i):
        q_rows_i = slice(i * tokens, (i + 1) * tokens)
        seen = (i + 1) * tokens

        def pair_step(j, carry):
            cols = pl.ds(pl.multiple_of(j * LANES, LANES), LANES)
            q = pre[q_rows_i, cols]
            q = q * table_ref[0, q_rows_i] + turned(q) * table_ref[1, q_rows_i]
            q = (q.astype(BF).astype(F32) * HD**-0.5).astype(BF)
            heads_ref[q_rows_i, cols] = q
            scores = matmul_right_t(two_heads(q), kk_ref[:seen])
            scores = causal_mask(scores, i * tokens)
            peak = jnp.max(scores, axis=-1, keepdims=True)
            exps = jnp.exp(scores - peak).astype(BF)
            out = matmul(exps, vv_ref[:seen])
            first, second = out[:tokens], out[tokens:]
            first_r, second_r = pltpu.roll(first, HD, 1), pltpu.roll(second, HD, 1)
            total = both(first_r, second)
            mixed_ref[q_rows_i, cols] = (both(first, second_r) / total).astype(BF)
            peaks = [
                jnp.broadcast_to(p, (tokens, LANES)) for p in (peak[:tokens], peak[tokens:])
            ]
            log_ref[q_rows_i, cols] = both(*peaks) + jnp.log(total)
            return carry

        lax.fori_loop(0, q_cols // LANES, pair_step, 0)

    def out_term(index):
        r = block(index)

        def step(j, carry):
            cols = pl.ds(pl.multiple_of(j * 512, 512), 512)
            term[:, cols] = matmul(mixed_ref[r, :], wo_ref[:, cols])
            return carry

        lax.fori_loop(0, model // 512, step, 0)

    def attend_block(index):
        for i in range(S):
            pl.when(index == i)(functools.partial(attend_rows, i))

    attend_block(shard ^ 3)
    out_term(shard ^ 3)
    far_out[...] = term[...].astype(BF)
    far = links.to(far_out, far_in, 1)
    ff_paired(0)
    ff_arrived(1)
    attend_block(shard ^ 2)
    out_term(shard ^ 2)
    far.wait_recv()
    across = []
    for i in range(2):
        r = slice(i * half, (i + 1) * half)
        across_out[r] = (term[r] + far_in[r].astype(F32)).astype(BF)
        across.append(links.to(across_out.at[r], across_in.at[r], 2))
    ff_paired(1)
    attend_block(shard ^ 1)
    out_term(shard ^ 1)
    beside_out[...] = term[...].astype(BF)
    beside = links.to(beside_out, beside_in, 1)
    attend_block(shard)
    out_term(shard)
    ff_handed(0)
    beside.wait_recv()
    term[...] += x_ref[...].astype(F32) + beside_in[...].astype(F32)
    n2_across, n2_beside, n2_here = [], [], []
    for i in range(2):
        r = slice(i * half, (i + 1) * half)
        across[i].wait_recv()
        mid_ref[r] = term[r] + across_in[r].astype(F32)
        norm_rows(mid_ref, norm2, gains, 1, i * half, half)
        n2_across.append(links.to(norm2.at[r], norm2_ref.at[own_rows[i]], 2))
        n2_beside.append(links.to(norm2.at[r], norm2_ref.at[own_rows[i]], 1))
        n2_here.append(links.here(norm2.at[r], norm2_ref.at[own_rows[i]]))
        if i == 0:
            ff_last(1)
    ff_last(0)
    cot_across.wait_recv()
    got = pl.ds(pl.multiple_of((shard ^ 2) * tokens, half), half)
    cot_core = links.to(cot_all_ref.at[got], cot_all_ref.at[got], 1)
    n2_core = []
    for i in range(2):
        n2_across[i].wait_recv()
        got = pl.ds(pl.multiple_of((shard ^ 2) * tokens + i * half, half), half)
        n2_core.append(links.to(norm2_ref.at[got], norm2_ref.at[got], 1))
    for copy in w_beside_ff + [cot_beside] + n2_beside + n2_core + [cot_core]:
        copy.wait_recv()
    for copy in ff_y[0] + ff_y[1]:
        copy.wait_recv()
    for copy in here_late + ff_here + n2_here + [norm1_out, w_heads_out]:
        copy.wait()
    links.close()


def front(x, cot, gains, wq, wk, wv, wo, gate, up, tables):
    tokens, model = x.shape
    seq_len, rows = S * tokens, wq.shape[0]
    q_cols, ff_cols = wq.shape[1] // S, gate.shape[1] // S
    width, q_rows = q_cols + LANES, rows // 4
    shape = jax.ShapeDtypeStruct
    chip_gate, chip_up = (rows // 8, 2 * ff_cols), (rows // 4, 2 * ff_cols)
    row_block = pltpu.VMEM((tokens, model), BF)
    return pl.pallas_call(
        front_kernel,
        out_shape=(
            shape((seq_len, model), BF),
            shape((seq_len, width), BF),
            shape((seq_len, q_cols), F32),
            shape((seq_len, q_cols), BF),
            shape((S * rows, width), BF),
            shape((tokens, model), F32),
            shape((seq_len, model), BF),
            shape((S * rows, 2 * ff_cols), BF),
            shape((seq_len, model), BF),
            shape((S, 16, rows), BF),
        ),
        in_specs=[VMEM, VMEM, VMEM, ANY, VMEM, VMEM, VMEM, ANY, ANY, VMEM],
        out_specs=[ANY, VMEM, VMEM, VMEM, ANY, VMEM, ANY, ANY, ANY, VMEM],
        scratch_shapes=[
            pltpu.VMEM((seq_len, model), BF),
            pltpu.VMEM((S, 16, rows), BF),
            pltpu.VMEM((S, rows, LANES), BF),
            pltpu.VMEM((q_rows, 2 * q_cols), BF),
            pltpu.VMEM((2, q_rows, LANES), BF),
            pltpu.VMEM(chip_gate, BF),
            pltpu.VMEM(chip_up, BF),
            pltpu.VMEM((S * rows, width), BF),
            pltpu.VMEM((seq_len, model), BF),
            pltpu.VMEM((seq_len, width), F32),
            pltpu.VMEM((seq_len, LANES), BF),
            pltpu.VMEM((seq_len, LANES), BF),
            row_block,
            row_block,
            row_block,
            row_block,
            row_block,
            row_block,
            pltpu.VMEM((tokens, model), F32),
            row_block,
            pltpu.VMEM((2, rows, ff_cols), BF),
            pltpu.SemaphoreType.DMA((96,)),
            pltpu.SemaphoreType.DMA((96,)),
            pltpu.SemaphoreType.DMA((24,)),
        ],
        compiler_params=pltpu.CompilerParams(
            collective_id=0, has_side_effects=True, vmem_limit_bytes=60 * 2**20
        ),
    )(x, cot, gains, wq, wk, wv, wo, gate, up, tables)


def by_rows(count, body, step=16):
    if count % step:
        body(pl.ds(0, count))
        return

    def one(i, carry):
        body(pl.ds(pl.multiple_of(i * step, step), step))
        return carry

    lax.fori_loop(0, count // step, one, 0)


class Scatter:
    def __init__(self, links, term, far_in, across_out, across_in, beside_in):
        self.links, self.term = links, term
        self.far_in, self.across_out = far_in, across_out
        self.across_in, self.beside_in = across_in, beside_in
        self.tokens = far_in.shape[0]
        self.half = self.tokens // 2
        self.starts = [
            [
                pl.multiple_of((links.shard ^ mask) * self.tokens + extra, 16)
                for extra in (0, self.half)
            ]
            for mask in range(S)
        ]

    def rows(self, mask, part=None):
        if part is None:
            return pl.ds(self.starts[mask][0], self.tokens)
        return pl.ds(self.starts[mask][part], self.half)

    def send_far(self):
        self.far = self.links.to(self.term.at[self.rows(3)], self.far_in, 1)

    def send_across(self):
        self.far.wait_recv()
        self.across = []
        base = self.starts[2][0]
        for i in range(2):

            def add(rows):
                start = i * self.half + rows.start
                here = pl.ds(pl.multiple_of(start, 16), rows.size)
                there = pl.ds(pl.multiple_of(base + start, 16), rows.size)
                total = self.term[there, :].astype(F32)
                total += self.far_in[here, :].astype(F32)
                self.across_out[here, :] = total.astype(BF)

            by_rows(self.half, add)
            part = pl.ds(i * self.half, self.half)
            self.across.append(
                self.links.to(self.across_out.at[part], self.across_in.at[part], 2)
            )

    def send_beside(self):
        self.beside = self.links.to(self.term.at[self.rows(1)], self.beside_in, 1)

    def finish(self, i, use):
        if i == 0:
            self.beside.wait_recv()
        self.across[i].wait_recv()
        base = self.starts[0][0]

        def one(rows):
            start = i * self.half + rows.start
            here = pl.ds(pl.multiple_of(start, 16), rows.size)
            there = pl.ds(pl.multiple_of(base + start, 16), rows.size)
            total = self.term[there, :].astype(F32)
            total += self.beside_in[here, :].astype(F32)
            total += self.across_in[here, :].astype(F32)
            use(here, total)

        by_rows(self.half, one)

    def release(self):
        for copy in [self.far, self.beside] + self.across:
            self.links.sent(copy)


ORDERS = {
    "ff": ((0, 1, 2), (0, 1, 2), (0, 1, 2), (1, 0, 2)),
    "down": ((1, 0, 2), (0, 1, 2)),
    "out": (1, 0, 2),
    "heads": (0, 1, 2),
}
HELD = {1: 'att1'}
STEPS = {
    "tff2": ('down0', 'down1'),
    "pout": ('ff3',),
    "mix": ('ff2',),
    "gath1": ('down1', 'down0'),
    "out": ('ff2',),
    "att1": ('down1',),
    "att2": ('down0',),
    "att3": ('ff0', 'down1'),
    "w_rf3": ('ff3', 'down0', 'out0', 'ff2'),
    "w_ra31": ('ff0', 'ff2', 'ff1', 'ff3'),
    "last": ('out0', 'ff0', 'ff3', 'heads0', 'ff1', 'ff0', 'out0', 'heads1', 'heads0', 'ff1', 'out0', 'heads1', 'heads0', 'ff1', 'heads1', 'heads0', 'heads1'),
}


class Flow:
    def __init__(self, links, order, arrive, relays, sends):
        self.links, self.arrive, self.sends = links, list(arrive), list(sends)
        self.relays, self.relayed = relays, None
        along = (links.replica >> 1) % 4
        self.outer = (along == 0) | (along == 3)
        self.inner = (along == 1) | (along == 2)
        self.bits = len(self.arrive)
        self.order = [b for b in order if b < self.bits]
        self.order += list(range(len(order), self.bits))
        self.left = list(range(self.bits - 1, -1, -1))
        self.sides = [(links.replica >> b) % 2 for b in range(self.bits)]
        self.others = [1 - side for side in self.sides]
        self.at = 0
        self.done = False

    def relay(self, source):
        self.relayed = [
            self.links.to(source, self.relays[0], 0, 2, self.outer),
            self.links.to(source, self.relays[1], 0, 6, self.inner),
        ]

    def hand_on(self):
        arrive = self.arrive[self.at - 1]
        first, second = self.relayed
        pl.when(self.inner)(first.wait_recv)
        to_inner = self.links.to(self.relays[0], arrive, 0, 6, self.inner)
        pl.when(self.inner)(second.wait_recv)
        to_outer = self.links.to(self.relays[1], arrive, 0, 2, self.inner)
        self.relayed, self.copy = None, (to_inner, to_outer)

    def arrived(self):
        if isinstance(self.copy, tuple):
            pl.when(self.inner)(self.copy[0].wait_recv)
            pl.when(self.outer)(self.copy[1].wait_recv)
        else:
            self.copy.wait_recv()

    def begin(self, term):
        self.parts = [term]
        self.step()

    def pick(self, bit, side):
        where = (slice(None),) * self.left.index(bit) + (side,)
        return [part.at[where] for part in self.parts]

    def step(self):
        bit = self.order[self.at]
        mine = self.sides[bit]
        if self.at:
            self.arrived()
        other = self.pick(bit, self.others[bit])
        source = other[0]
        if self.at:
            source = self.sends[self.at - 1]
            self.add(other, source, len(self.left) - 1)
        if bit == 2:
            self.relay(source)
        else:
            self.copy = self.links.to(source, self.arrive[self.at], 0, 1 << bit)
        self.parts = self.pick(bit, mine) + [self.arrive[self.at]]
        self.left.remove(bit)
        self.at += 1

    def advance(self):
        if self.relayed:
            self.hand_on()
        elif self.at < self.bits:
            self.step()
        elif not self.done:
            self.done = True
            self.conclude(self)

    def end(self, target):
        self.arrived()
        self.add(self.parts, target, 0)

    def add(self, parts, target, free):
        ways = list(itertools.product(range(2), repeat=free))
        rest = parts[0].shape[free:]
        jobs = [(way, part) for way in ways for part in parts]

        def inner(fetch, sems):
            copies = []
            for n, (way, part) in enumerate(jobs):
                source = part.at[way] if way else part
                copy = pltpu.make_async_copy(source, fetch.at[n], sems.at[n])
                copy.start()
                copies.append(copy)
            for w, way in enumerate(ways):
                first = w * len(parts)
                for k in range(len(parts)):
                    copies[first + k].wait()
                leads = [()] if len(rest) == 2 else [(g,) for g in range(rest[0])]
                for lead in leads:

                    def one(rows):
                        total = fetch[(first,) + lead + (rows,)].astype(F32)
                        for k in range(1, len(parts)):
                            more = fetch[(first + k,) + lead + (rows,)]
                            total += more.astype(F32)
                        target[way + lead + (rows,)] = total.astype(target.dtype)

                    by_rows(rest[-2], one)

        pl.run_scoped(
            inner,
            pltpu.VMEM((len(jobs),) + tuple(rest), BF),
            pltpu.SemaphoreType.DMA((len(jobs),)),
        )


def bits_of(index, count):
    return tuple((index >> b) & 1 for b in reversed(range(count.bit_length() - 1)))


def turn(source, cols, target):
    rows = source.shape[0]
    for i in range(0, rows, 256):
        part = source[i : i + 256, cols]
        target[:, i : i + 256] = part.astype(F32).T.astype(BF)


def produce(left_t, right, first, size, stage, replicas, lead=(), tile=256):
    share = left_t.shape[0] // replicas

    def one(t, carry):
        start = pl.multiple_of(t * tile, LANES)
        cols = pl.ds(pl.multiple_of(first + start, LANES), tile)
        result = matmul(left_t[...], right[:, cols])
        for r in range(replicas):
            where = bits_of(r, replicas) + lead + (slice(None), pl.ds(start, tile))
            stage[where] = result[r * share : (r + 1) * share].astype(BF)
        return carry

    lax.fori_loop(0, size // tile, one, 0)


def stream(count, copies_of, use):
    for copy in copies_of(0, 0):
        copy.start()

    def one(t, carry):
        slot = t % 2

        @pl.when(t + 1 < count)
        def _():
            for copy in copies_of(t + 1, 1 - slot):
                copy.start()

        for copy in copies_of(t, slot):
            copy.wait()
        use(t, slot)
        return carry

    lax.fori_loop(0, count, one, 0)


def norm_back_rows(grad, values, gain_row):
    scale = rms_scale(values)
    weighted = grad * gain_row
    mean = jnp.mean(weighted * values, axis=-1, keepdims=True)
    return scale * weighted - values * (scale * scale * scale * mean)


def rear_kernel(
    norm2_hbm, cot_hbm, w_ff_hbm, w_down_hbm, norm1_hbm, mixed_hbm, w_out_hbm, heads_hbm, logs_hbm,
    table_hbm, w_heads_hbm, mid_ref, cot_ref, x_ref, gain_ref,
    output_ref, input_grad_ref, grad_out_ref, grad_down_ref, pieces_ff, pieces_heads, *others,
):
    shard, replica = lax.axis_index("shard"), lax.axis_index("replica")
    tokens, model = mid_ref.shape
    seq_len = S * tokens
    ff_cols, rows = w_down_hbm.shape[0], model // S
    width = heads_hbm.shape[1]
    q_cols = width - LANES
    replicas = model // (S * pieces_ff.shape[1])
    bits = replicas.bit_length() - 1
    share, share_down = pieces_ff.shape[1], grad_down_ref.shape[0]
    half, half_model = tokens // 2, model // 2
    others = list(others)

    def take(count):
        taken = others[:count]
        del others[:count]
        return taken

    hbm = {name: take(3 + bits) for name in ("ff", "down", "out", "heads")}
    cot_all, term, far_in, across_out, across_in, beside_in, grad_mid, grad_mid_b = take(8)
    sends = {name: take(bits) for name in ("ff", "down", "out", "heads")}
    send, recv, local, slots = take(4)
    links = Links(shard, replica, send, recv, local)
    other_chip = 1 - shard // 2

    def flow(name, order, index=None):
        pick = (lambda ref: ref) if index is None else (lambda ref: ref.at[index])
        made = Flow(
            links,
            order,
            [pick(ref) for ref in hbm[name][1:-2]],
            [pick(ref) for ref in hbm[name][-2:]],
            [pick(ref) for ref in sends[name][:-1]],
        )
        made.term, made.last = pick(hbm[name][0]), pick(sends[name][-1])
        return made

    flows_ff = [flow("ff", ORDERS["ff"][m], m) for m in range(S)]
    flows_down = [flow("down", ORDERS["down"][i], i) for i in range(2)]
    flow_out = flow("out", ORDERS["out"])
    flows_heads = [flow("heads", ORDERS["heads"], i) for i in range(2)]
    flows = {"out0": flow_out}
    for name, many in (("ff", flows_ff), ("down", flows_down), ("heads", flows_heads)):
        flows.update({f"{name}{i}": made for i, made in enumerate(many)})
    finals, finals_here = [], []

    def deliver(piece, pieces, mask):
        if mask:
            finals.append(links.to(piece, pieces.at[mask], mask))
        else:
            finals_here.append(links.here(piece, pieces.at[mask]))

    def end_ff(mask, made):
        made.end(made.last)
        deliver(made.last, pieces_ff, mask)

    def end_down(i, made):
        made.end(made.last)
        cols = pl.ds(i * half_model, half_model)
        finals_here.append(links.here(made.last, grad_down_ref.at[:, cols]))

    def end_out(made):
        made.end(made.last)
        finals_here.append(links.here(made.last, grad_out_ref))

    def end_heads(i, made):
        made.end(made.last)
        for n, mask in enumerate(((3, 2), (1, 0))[i]):
            deliver(made.last.at[n], pieces_heads, mask)

    for i in range(S):
        flows_ff[i].conclude = functools.partial(end_ff, i)
    for i in range(2):
        flows_down[i].conclude = functools.partial(end_down, i)
        flows_heads[i].conclude = functools.partial(end_heads, i)
    flow_out.conclude = end_out

    def pump(point):
        for m, when in HELD.items():
            if when == point:
                flows_ff[m].begin(flows_ff[m].term)
        for name in STEPS.get(point, ()):
            flows[name].advance()

    greet(shard, replica, (1, 2, 3), [1, 2, 6] + [1 << b for b in range(3, bits)])
    gain_one, gain_two = (
        jnp.concatenate(
            [gain_ref[j, i : i + 1, :].astype(F32) for j in range(S)], axis=1
        )
        for i in range(2)
    )
    sums = Scatter(links, term, far_in, across_out, across_in, beside_in)
    last_rows = pl.ds(half, half)
    cot_across = links.to(cot_ref.at[last_rows], cot_all.at[sums.rows(0, 1)], 2)
    chip_rows = pl.ds(pl.multiple_of(shard // 2 * 2 * tokens, 2 * tokens), 2 * tokens)

    def first_half(norm2, hidden, grad_ff):
        norm2_in = links.here(norm2_hbm, norm2)
        cot_in = [
            links.here(cot_hbm.at[r], cot_all.at[r])
            for r in (chip_rows, sums.rows(2, 0), sums.rows(3, 0))
        ]

        tile = 256
        tiles = [(i, min(tile, ff_cols - i)) for i in range(0, ff_cols, tile)]

        def over_tiles(copies_of, use):
            for copy in copies_of(0):
                copy.start()
            for t, (start, size) in enumerate(tiles):
                if t + 1 < len(tiles):
                    for copy in copies_of(t + 1):
                        copy.start()
                for copy in copies_of(t):
                    copy.wait()

                def block(b, carry):
                    use(pl.ds(pl.multiple_of(b * 512, 512), 512), start, size, t % 2)
                    return carry

                lax.fori_loop(0, seq_len // 512, block, 0)

        def gate_up(gates, ups):
            def copies_of(t):
                start, size = tiles[t]
                slot = t % 2
                cols = slice(start, start + size)
                up_cols = slice(ff_cols + start, ff_cols + start + size)
                return [
                    pltpu.make_async_copy(*pair, slots.at[slot, n])
                    for n, pair in enumerate(
                        (
                            (w_ff_hbm.at[:, cols], gates.at[slot, :, :size]),
                            (w_ff_hbm.at[:, up_cols], ups.at[slot, :, :size]),
                        )
                    )
                ]

            def use(r, start, size, slot):
                gate = matmul(norm2[r, :], gates[slot, :, :size])
                up = matmul(norm2[r, :], ups[slot, :, :size])
                silu = gate * (1.0 / (1.0 + jnp.exp(-gate)))
                hidden[r, start : start + size] = (silu * up).astype(BF)
                grad_ff[r, start : start + size] = gate.astype(BF)
                grad_ff[r, ff_cols + start : ff_cols + start + size] = up.astype(BF)

            norm2_in.wait()
            over_tiles(copies_of, use)

        weight_tile = pltpu.VMEM((2, model, tile), BF)
        pl.run_scoped(gate_up, weight_tile, weight_tile)
        cot_across.wait_recv()
        there = cot_all.at[sums.rows(2, 1)]
        cot_core = links.to(there, there, 1)
        for copy in cot_in:
            copy.wait()
        cot_core.wait_recv()
        links.sent(cot_core)

        def down_terms(left_t, stage):
            turn(hidden, slice(None), left_t)
            for i in range(2):
                produce(left_t, cot_all, i * half_model, half_model, stage, replicas)
                links.here(stage, flows_down[i].term).wait()
                flows_down[i].begin(flows_down[i].term)

        pl.run_scoped(
            down_terms,
            pltpu.VMEM((ff_cols, seq_len), BF),
            pltpu.VMEM((2,) * bits + (share_down, half_model), BF),
        )

        def hidden_grads(downs):
            def copies_of(t):
                start, size = tiles[t]
                slot = t % 2
                return [
                    pltpu.make_async_copy(
                        w_down_hbm.at[slice(start, start + size)],
                        downs.at[slot, :size],
                        slots.at[slot, 0],
                    )
                ]

            def use(r, start, size, slot):
                grad = matmul_right_t(cot_all[r, :], downs[slot, :size])
                cols = slice(start, start + size)
                up_cols = slice(ff_cols + start, ff_cols + start + size)
                gate, up = grad_ff[r, cols].astype(F32), grad_ff[r, up_cols].astype(F32)
                sigmoid = 1.0 / (1.0 + jnp.exp(-gate))
                slope = sigmoid * (1.0 + gate * (1.0 - sigmoid))
                grad_ff[r, cols] = (grad * up * slope).astype(BF)
                grad_ff[r, up_cols] = (grad * gate * sigmoid).astype(BF)

            over_tiles(copies_of, use)

        pl.run_scoped(hidden_grads, pltpu.VMEM((2, tile, model), BF))
        pump("hid")

        def norm_terms(chip):
            def inner(tiles):
                r = pl.ds(pl.multiple_of(chip * 2 * tokens, 2 * tokens), 2 * tokens)

                def copies_of(t, slot):
                    part = pl.ds(pl.multiple_of(t * 256, 256), 256)
                    return [
                        pltpu.make_async_copy(
                            w_ff_hbm.at[part], tiles.at[slot], slots.at[slot, 0]
                        )
                    ]

                def use(t, slot):
                    cols = pl.ds(pl.multiple_of(t * 256, 256), 256)
                    product = matmul_right_t(grad_ff[r, :], tiles[slot])
                    term[r, cols] = product.astype(BF)

                stream(model // 256, copies_of, use)

            pl.run_scoped(inner, pltpu.VMEM((2, 256, 2 * ff_cols), BF))

        norm_terms(other_chip)
        sums.send_far()
        pump("far")

        def ff_terms(left_t, stages):
            copies = {}

            def launch(n):
                copies[n][0].wait()
                if copies[n][2] not in HELD:
                    copies[n][1].begin(copies[n][1].term)

            for n, mask in enumerate((3, 2, 1, 0)):
                cols = pl.ds(pl.multiple_of((shard ^ mask) * rows, rows), rows)
                turn(norm2, cols, left_t)
                if n:
                    launch(n - 1)
                produce(left_t, grad_ff, 0, 2 * ff_cols, stages.at[n % 2], replicas)
                copies[n] = (
                    links.here(stages.at[n % 2], flows_ff[mask].term),
                    flows_ff[mask],
                    mask,
                )
                if n == 0:
                    pump("w_rf")
                    sums.send_across()
                pump(f"tff{n}")
            launch(3)

        pl.run_scoped(
            ff_terms,
            pltpu.VMEM((rows, seq_len), BF),
            pltpu.VMEM((2,) + (2,) * bits + (share, 2 * ff_cols), BF),
        )
        norm_terms(1 - other_chip)
        sums.send_beside()
        pump("near")

        def to_mid(r, grad):
            values = mid_ref[r, :]
            total = cot_ref[r, :].astype(F32)
            total += norm_back_rows(grad, values, gain_two)
            grad_mid[r, :] = total
            grad_mid_b[r, :] = total.astype(BF)

        gathered = []
        for i in range(2):
            pump(f"w_ra{i}")
            sums.finish(i, to_mid)
            part = slice(i * half, (i + 1) * half)
            there = sums.rows(0, i)
            gathered.append(
                [
                    links.to(grad_mid_b.at[part], cot_all.at[there], 2),
                    links.to(grad_mid_b.at[part], cot_all.at[there], 1),
                    links.here(grad_mid_b.at[part], cot_all.at[there]),
                ]
            )
        sums.release()
        pump("mid")

        def out_terms(tiles):
            def copies_of(t, slot):
                part = pl.ds(pl.multiple_of(t * 256, 256), 256)
                return [
                    pltpu.make_async_copy(
                        w_down_hbm.at[:, part], tiles.at[slot], slots.at[slot, 0]
                    )
                ]

            def use(t, slot):
                cols = pl.ds(pl.multiple_of(t * 256, 256), 256)
                term[:, cols] = matmul(hidden[...], tiles[slot]).astype(BF)

            stream(model // 256, copies_of, use)

        pl.run_scoped(out_terms, pltpu.VMEM((2, ff_cols, 256), BF))
        pump("pout")
        return gathered

    gathered = []
    pl.run_scoped(
        lambda *refs: gathered.extend(first_half(*refs)),
        pltpu.VMEM((seq_len, model), BF),
        pltpu.VMEM((seq_len, ff_cols), BF),
        pltpu.VMEM((seq_len, 2 * ff_cols), BF),
    )

    def second_half(mixed, w_out, heads, logs, table, w_heads, grad_mixed, grad_heads,
                    kk_ref, vv_ref, dk_ref, dv_ref):
        loads = [
            links.here(*pair)
            for pair in (
                (w_out_hbm, w_out),
                (heads_hbm, heads),
                (logs_hbm, logs),
                (table_hbm, table),
                (mixed_hbm, mixed),
                (w_heads_hbm, w_heads),
            )
        ]
        for i in range(2):
            gathered[i][1].wait_recv()
            gathered[i][2].wait()
        sums.send_far()
        sums.send_beside()
        for copy in loads:
            copy.wait()

        def mix(mask, part=None):
            r = sums.rows(mask, part)
            grad_mixed[r, :] = matmul_right_t(cot_all[r, :], w_out[...]).astype(BF)

        mix(0)
        mix(1)
        kv = heads[:, q_cols:].astype(F32)
        swapped = pltpu.roll(kv, HD, 1)
        kk_ref[...] = both(kv, swapped).astype(BF)
        vv_ref[...] = both(swapped, kv).astype(BF)
        dk_ref[...] = jnp.zeros_like(dk_ref)
        dv_ref[...] = jnp.zeros_like(dv_ref)
        pump("mix")
        forward = []
        for i in range(2):
            pump(f"w_g{i}")
            gathered[i][0].wait_recv()
            r = sums.rows(2, i)
            forward.append(links.to(cot_all.at[r], cot_all.at[r], 1))
            mix(2, i)
            pump(f"gath{i}")
        pump("w_rf2")
        sums.send_across()
        pump("across2")
        for i in range(2):
            forward[i].wait_recv()
            mix(3, i)

        def out_grad(left_t, stage):
            turn(mixed, slice(None), left_t)
            produce(left_t, cot_all, 0, model, stage, replicas)
            links.here(stage, flow_out.term).wait()
            flow_out.begin(flow_out.term)

        pl.run_scoped(
            out_grad,
            pltpu.VMEM((rows, seq_len), BF),
            pltpu.VMEM((2,) * bits + (share, model), BF),
        )

        def attend_rows(i):
            r = slice(i * tokens, (i + 1) * tokens)
            seen = (i + 1) * tokens

            def pair_step(j, carry):
                cols = pl.ds(pl.multiple_of(j * LANES, LANES), LANES)
                q = two_heads(heads[r, cols])
                grad = two_heads(grad_mixed[r, cols])
                log_pair = logs[r, cols]
                log_col = jnp.concatenate(
                    [log_pair[:, :1], log_pair[:, HD : HD + 1]], axis=0
                )
                mixed_pair = mixed[r, cols].astype(F32)
                product = grad.astype(F32) * jnp.concatenate([mixed_pair] * 2, axis=0)
                inner = jnp.sum(product, axis=-1, keepdims=True)
                scores = matmul_right_t(q, kk_ref[:seen])
                soft = jnp.exp(causal_mask(scores, i * tokens) - log_col)
                grad_soft = matmul_right_t(grad, vv_ref[:seen])
                grad_scores = (soft * (grad_soft - inner)).astype(BF)
                dq = matmul(grad_scores, kk_ref[:seen])
                dq = both(dq[:tokens], dq[tokens:]) * HD**-0.5
                dq = dq * table[0, r] - turned(dq) * table[1, r]
                grad_heads[r, cols] = dq.astype(BF)
                dk_ref[:seen] += matmul_left_t(grad_scores, q)
                dv_ref[:seen] += matmul_left_t(soft.astype(BF), grad)
                return carry

            lax.fori_loop(0, q_cols // LANES, pair_step, 0)

        pump("out")
        for i in range(S):
            attend_rows(i)
            pump(f"att{i}")
        dk, dv = dk_ref[...], dv_ref[...]
        dk, dv = dk + pltpu.roll(dk, HD, 1), dv + pltpu.roll(dv, HD, 1)
        dkv = both(dk, dv)
        dkv = dkv * table[2] - turned(dkv) * table[3]
        grad_heads[:, q_cols:] = dkv.astype(BF)

        def to_output(r, total):
            output_ref[r, :] = (mid_ref[r, :] + total).astype(BF)

        for i in range(2):
            pump(f"w_ra2{i}")
            sums.finish(i, to_output)
        sums.release()
        for mask in (1, 2):
            pl.semaphore_signal(
                credit.at[mask - 1],
                inc=1,
                device_id={"shard": shard ^ mask, "replica": replica},
                device_id_type=MESH_ID,
            )

        def head_terms(chip):
            r = pl.ds(pl.multiple_of(chip * 2 * tokens, 2 * tokens), 2 * tokens)

            def one(t, carry):
                cols = pl.ds(pl.multiple_of(t * 256, 256), 256)
                product = matmul_right_t(grad_heads[r, :], w_heads[cols, :])
                term[r, cols] = product.astype(BF)
                return carry

            lax.fori_loop(0, model // 256, one, 0)

        def head_grads(norm1, left_t, stages):
            norm1_in = links.here(norm1_hbm, norm1)
            head_terms(other_chip)
            pl.semaphore_wait(credit.at[0], 1)
            sums.send_far()
            norm1_in.wait()
            stage_out = []
            for i, masks in enumerate(((3, 2), (1, 0))):
                for n, mask in enumerate(masks):
                    cols = pl.ds(pl.multiple_of((shard ^ mask) * rows, rows), rows)
                    turn(norm1, cols, left_t)
                    produce(
                        left_t, grad_heads, 0, width, stages.at[i], replicas, (n,), LANES
                    )
                stage_out.append(links.here(stages.at[i], flows_heads[i].term))
                if i == 0:
                    pump("w_rf3")
                    pl.semaphore_wait(credit.at[1], 1)
                    sums.send_across()
                    stage_out[0].wait()
                    flows_heads[0].begin(flows_heads[0].term)
            stage_out[1].wait()
            flows_heads[1].begin(flows_heads[1].term)
            head_terms(1 - other_chip)
            sums.send_beside()

        pl.run_scoped(
            head_grads,
            pltpu.VMEM((seq_len, model), BF),
            pltpu.VMEM((rows, seq_len), BF),
            pltpu.VMEM((2,) + (2,) * bits + (2, share, width), BF),
        )
        pump("heads")

    credit = take(1)[0]
    pl.run_scoped(
        second_half,
        pltpu.VMEM((seq_len, q_cols), BF),
        pltpu.VMEM((q_cols, model), BF),
        pltpu.VMEM((seq_len, width), BF),
        pltpu.VMEM((seq_len, q_cols), F32),
        pltpu.VMEM((4, seq_len, LANES), F32),
        pltpu.VMEM((model, width), BF),
        pltpu.VMEM((seq_len, q_cols), BF),
        pltpu.VMEM((seq_len, width), BF),
        pltpu.VMEM((seq_len, LANES), BF),
        pltpu.VMEM((seq_len, LANES), BF),
        pltpu.VMEM((seq_len, LANES), F32),
        pltpu.VMEM((seq_len, LANES), F32),
    )

    def to_input_grad(r, grad):
        total = grad_mid[r, :]
        total += norm_back_rows(grad, x_ref[r, :].astype(F32), gain_one)
        input_grad_ref[r, :] = total.astype(BF)

    for i in range(2):
        pump(f"w_ra3{i}")
        sums.finish(i, to_input_grad)
    pump("last")
    waiting = list(flows.values())
    while waiting:
        for made in waiting:
            made.advance()
        waiting = [made for made in waiting if not made.done]
    for copy in finals:
        copy.wait_recv()
    for copy in finals_here:
        copy.wait()
    links.close()


def rear(norm2, cot_all, w_ff, w_down, norm1, mixed, w_out, heads, logs, tables, w_heads, mid, cot, x, gains, replicas):
    tokens, model = mid.shape
    seq_len, rows, ff_cols = S * tokens, model // S, w_down.shape[0]
    width = heads.shape[1]
    bits = replicas.bit_length() - 1
    share, share_down = rows // replicas, ff_cols // replicas
    shape = jax.ShapeDtypeStruct
    rests = {
        "ff": ((S,), (share, 2 * ff_cols), BF),
        "down": ((2,), (share_down, model // 2), F32),
        "out": ((), (share, model), F32),
        "heads": ((2,), (2, share, width), BF),
    }
    work, sends = [], []
    for many, rest, last in rests.values():
        work += [shape(many + (2,) * bits + rest, BF)]
        work += [shape(many + (2,) * n + rest, BF) for n in reversed(range(bits))]
        work += [shape(many + (2,) * (bits - 3) + rest, BF)] * 2
        sends += [
            pltpu.VMEM(many + (2,) * n + rest, BF) for n in reversed(range(bits - 1))
        ]
        sends += [pltpu.VMEM(many + rest, last)]
    outs = (
        shape((tokens, model), BF),
        shape((tokens, model), BF),
        shape((share, model), F32),
        shape((share_down, model), F32),
        shape((S, share, 2 * ff_cols), BF),
        shape((S, share, width), BF),
    )
    row_block = pltpu.VMEM((tokens, model), BF)
    result = pl.pallas_call(
        rear_kernel,
        out_shape=outs + tuple(work),
        in_specs=[ANY] * 11 + [VMEM] * 4,
        out_specs=[VMEM] * 2 + [ANY] * (4 + len(work)),
        scratch_shapes=[
            pltpu.VMEM((seq_len, model), BF),
            pltpu.VMEM((seq_len, model), BF),
            row_block,
            row_block,
            row_block,
            row_block,
            pltpu.VMEM((tokens, model), F32),
            row_block,
        ]
        + sends
        + [
            pltpu.SemaphoreType.DMA((128,)),
            pltpu.SemaphoreType.DMA((128,)),
            pltpu.SemaphoreType.DMA((48,)),
            pltpu.SemaphoreType.DMA((2, 3)),
            pltpu.SemaphoreType.REGULAR((2,)),
        ],
        compiler_params=pltpu.CompilerParams(
            collective_id=1, has_side_effects=True, vmem_limit_bytes=62 * 2**20
        ),
    )(norm2, cot_all, w_ff, w_down, norm1, mixed, w_out, heads, logs, tables, w_heads, mid, cot, x, gains)
    return result[: len(outs)]


def on_device(
    inputs, cotangent, gain_attn, w_query, w_key, w_value, w_output, gain_mlp, w_gate, w_up, w_down
):
    shard, replica = lax.axis_index("shard"), lax.axis_index("replica")
    x, cot = inputs[0], cotangent[0]
    tables = jnp.asarray(rope_tables(S * x.shape[0]))
    gains = jnp.concatenate(
        [jnp.stack([gain_attn, gain_mlp]), jnp.zeros((14, w_query.shape[0]), BF)]
    )
    norm1, heads, logs, mixed, w_heads, mid, norm2, w_ff, cot_all, gains = front(
        x, cot, gains, w_query, w_key, w_value, w_output, w_gate, w_up, tables
    )
    output, input_grad, grad_output, grad_down, pieces_ff, pieces_heads = rear(
        norm2, cot_all, w_ff, w_down, norm1, mixed, w_output, heads, logs, tables,
        w_heads, mid, cot, x, gains, lax.axis_size("replica"),
    )
    grads, (grad_gain_two, grad_gain_one), moved = finish(
        (pieces_ff, pieces_heads),
        ((w_gate, w_up), (w_query, w_key, w_value)),
        (gain_mlp, gain_attn),
        (output, input_grad, grad_output, grad_down),
        shard,
        replica,
    )
    grad_gate, grad_up, grad_query, grad_key, grad_value = grads
    output, input_grad, grad_output, grad_down = moved
    return (
        output[None],
        input_grad[None],
        grad_gain_one,
        grad_query,
        grad_key,
        grad_value,
        grad_output,
        grad_gain_two,
        grad_gate,
        grad_up,
        grad_down,
    )


def solution(mesh):
    placed = (
        P("replica", "shard", None),
        P("replica", "shard", None),
        P("shard"),
        P("shard", None),
        P("shard", None),
        P("shard", None),
        P("shard", None),
        P("shard"),
        P("shard", None),
        P("shard", None),
        P("shard", None),
    )
    both_axes = ("shard", "replica")
    return jax.shard_map(
        on_device,
        mesh=mesh,
        in_specs=placed,
        out_specs=(
            P("replica", "shard", None),
            P("replica", "shard", None),
            P(both_axes),
            P(both_axes, None),
            P(both_axes, None),
            P(both_axes, None),
            P(both_axes, None),
            P(both_axes),
            P(both_axes, None),
            P(both_axes, None),
            P(both_axes, None),
        ),
        check_vma=False,
    )
```
